32 devices in a mesh: dp: 8 (over y, x, core), bucket: 4 (over z).
Axes of the slice: x: 2, y: 2, z: 4, core: 2. Of those that a mesh axis runs over, the one named last changes fastest.
Arguments:
- feats: float32 [65536, 400], P(('dp', 'bucket'))
- labels: int32 [65536], P(('dp', 'bucket')), may hold values from 0 to 46
- valid: int32 [65536], P(('dp', 'bucket')), may hold values from 0 to 1, as said below
- branch_w: float32 [4, 100, 512], replicated, may hold values from -0.625 to 0.625
- branch_gain: float32 [4, 512], replicated, may hold values from 0.5 to 1.5
- branch_shift: float32 [4, 512], replicated, may hold values from -3 to 3
- branch_slope: float32 [4, 512], replicated, may hold values from 0.05 to 0.5
- mix_slope: float32 [2048], replicated, may hold values from 0.05 to 0.5
- mix_w: float32 [2048, 512], replicated, may hold values from -0.125 to 0.125
- mix_gain: float32 [512], replicated, may hold values from 0.5 to 1.5
- mix_shift: float32 [512], replicated, may hold values from -3 to 3
- out_slope: float32 [512], replicated, may hold values from 0.05 to 0.5
- head_w: float32 [512, 47], replicated, may hold values from -0.25 to 0.25
- head_bias: float32 [47], replicated, may hold values from -3 to 3
Outputs:
- loss: float32 [], replicated
- feats_grad: float32 [65536, 400], P(('dp', 'bucket'))
- branch_w_grad: float32 [4, 100, 512], replicated
- branch_gain_grad: float32 [4, 512], replicated
- branch_shift_grad: float32 [4, 512], replicated
- branch_slope_grad: float32 [4, 512], replicated
- mix_slope_grad: float32 [2048], replicated
- mix_w_grad: float32 [2048, 512], replicated
- mix_gain_grad: float32 [512], replicated
- mix_shift_grad: float32 [512], replicated
- out_slope_grad: float32 [512], replicated
- head_w_grad: float32 [512, 47], replicated
- head_bias_grad: float32 [47], replicated
The draws below stay inside these ranges and needn't reach their ends.
Inputs may be any that keep to these rules, and one draw needn't show every extreme that they name: `valid`: within each device's 2048 node slots the training nodes form one leading block; its length varies between devices (two may be equal), and some device's block fills all 2048 slots.
All inputs are finite; a program needn't handle non-finite values.
Results may differ from the reference program's by a relative error of at most 0.0003.
Values sent between devices are 32-bit elements; how exact they have to be, the bound alone decides.
No kernel may reach another device: no remote copies, remote signals or barrier semaphores. Data moves between devices by JAX's collectives and lax.ppermute only.
A program may use at most 192 MiB of HBM per device.

```python
import jax
import jax.numpy as jnp
from jax import lax

HOPS = 4
IN_W = 100
HID = 512
CLASSES = 47
MIX = 2048
ROWS_DEV = 2048
NODES = 65536


def draw_feats(key, part):
    key = jax.random.fold_in(key, 11)
    first, second, third = jax.random.split(key, 3)
    width = HOPS * IN_W
    rise = 1.0 + 2.0 * jnp.arange(NODES, dtype=jnp.float32) / NODES
    row_scale = jnp.exp(jax.random.uniform(second, (NODES, 1), minval=0.0, maxval=2.3)) * rise[:, None]
    col_scale = jnp.exp(jax.random.uniform(third, (1, width), minval=0.0, maxval=1.4))
    base = jax.random.normal(first, (NODES, width))
    return (base * row_scale * col_scale * 0.3).astype(jnp.float32)


def draw_valid(key, part):
    key = jax.random.fold_in(key, 23)
    first, second, third = jax.random.split(key, 3)
    devices = NODES // ROWS_DEV
    halvings = jax.random.randint(first, (devices,), 0, 4)
    full_one = jax.random.randint(second, (), 0, devices)
    halvings = jnp.where(jnp.arange(devices, dtype=jnp.int32) == full_one, 0, halvings)
    base = jnp.right_shift(jnp.full((devices,), ROWS_DEV, jnp.int32), halvings)
    jitter = jax.random.randint(third, (devices,), 0, max(ROWS_DEV // 16, 1))
    length = jnp.clip(base - jitter * (halvings > 0).astype(jnp.int32), 1, ROWS_DEV)
    local = jnp.arange(ROWS_DEV, dtype=jnp.int32)
    return (local[None, :] < length[:, None]).astype(jnp.int32).reshape(NODES)


def with_ends(array, own_key, low, largest):
    shape = array.shape
    place = [jax.random.randint(jax.random.fold_in(own_key, axis), (), 0, shape[axis]) for axis in range(len(shape))]
    array = array.at[tuple(place)].set(low)
    longest = shape.index(max(shape))
    place[longest] = (place[longest] + 1) % shape[longest]
    return array.at[tuple(place)].set(largest)


def normal_values(stream_key, dims, spread, most, held_as=jnp.bfloat16):
    entries = jax.random.normal(stream_key, dims, jnp.float32) * spread
    return jnp.minimum(jnp.maximum(entries, -most), most).astype(held_as)


def setup_inputs(seed: int = 0) -> dict:
    splits = jax.random.split(jax.random.key(seed), 15)
    feats = draw_feats(jax.random.fold_in(splits[14], 71), 0)
    labels = with_ends(jax.random.randint(splits[1], (NODES,), 0, CLASSES), jax.random.fold_in(splits[1], 1), 0, CLASSES - 1).astype(jnp.int32)
    valid = draw_valid(jax.random.fold_in(splits[14], 71), 0)
    branch_w = normal_values(splits[3], (HOPS, IN_W, HID), IN_W ** -0.5, 0.625, jnp.float32)
    branch_gain = jnp.clip(1.0 + 0.1 * jax.random.normal(splits[4], (HOPS, HID), jnp.float32), 0.5, 1.5)
    branch_shift = normal_values(splits[5], (HOPS, HID), 0.5, 3.0, jnp.float32)
    branch_slope = jnp.clip(jax.random.uniform(splits[6], (HOPS, HID), jnp.float32, 0.05, 0.5), 0.05, 0.5)
    mix_slope = jnp.clip(jax.random.uniform(splits[7], (MIX,), jnp.float32, 0.05, 0.5), 0.05, 0.5)
    mix_w = normal_values(splits[8], (MIX, HID), MIX ** -0.5, 0.125, jnp.float32)
    mix_gain = jnp.clip(1.0 + 0.1 * jax.random.normal(splits[9], (HID,), jnp.float32), 0.5, 1.5)
    mix_shift = normal_values(splits[10], (HID,), 0.5, 3.0, jnp.float32)
    out_slope = jnp.clip(jax.random.uniform(splits[11], (HID,), jnp.float32, 0.05, 0.5), 0.05, 0.5)
    head_w = normal_values(splits[12], (HID, CLASSES), HID ** -0.5, 0.25, jnp.float32)
    head_bias = normal_values(splits[13], (CLASSES,), 0.5, 3.0, jnp.float32)
    return {"feats": feats, "labels": labels, "valid": valid, "branch_w": branch_w, "branch_gain": branch_gain, "branch_shift": branch_shift, "branch_slope": branch_slope, "mix_slope": mix_slope, "mix_w": mix_w, "mix_gain": mix_gain, "mix_shift": mix_shift, "out_slope": out_slope, "head_w": head_w, "head_bias": head_bias}


HIGH = lax.Precision.HIGHEST
EPS = 1e-05

def matmul(a, b):
    return jnp.dot(a, b, precision=HIGH, preferred_element_type=jnp.float32)

def smooth_act(y, slope):
    return slope * y + (1.0 - slope) * jax.nn.softplus(y)

def batch_norm(z, mask, count, gain, shift):
    mean = lax.optimization_barrier(jnp.sum(mask * z, axis=0)) / count
    var = lax.optimization_barrier(jnp.sum(mask * z * z, axis=0)) / count - mean * mean
    return gain * (z - mean) * lax.rsqrt(var + EPS) + shift

def reference(feats, labels, valid, branch_w, branch_gain, branch_shift, branch_slope, mix_slope, mix_w, mix_gain, mix_shift, out_slope, head_w, head_bias):
    mask = valid.astype(jnp.float32)[:, None]
    count = jnp.sum(mask)
    classes = head_w.shape[1]
    hit = (labels[:, None] == jnp.arange(classes, dtype=jnp.int32)[None, :]).astype(jnp.float32)

    def forward(feats, branch_w, branch_gain, branch_shift, branch_slope, mix_slope, mix_w, mix_gain, mix_shift, out_slope, head_w, head_bias):
        in_w = branch_w.shape[1]
        pieces = []
        for hop in range(branch_w.shape[0]):
            z = matmul(feats[:, hop * in_w:(hop + 1) * in_w], branch_w[hop])
            y = batch_norm(z, mask, count, branch_gain[hop], branch_shift[hop])
            pieces.append(smooth_act(y, branch_slope[hop]))
        joined = jnp.concatenate(pieces, axis=1)
        mixed_in = smooth_act(joined, mix_slope)
        mixed = matmul(mixed_in, mix_w)
        y2 = batch_norm(mixed, mask, count, mix_gain, mix_shift)
        final = smooth_act(y2, out_slope)
        logits = matmul(final, head_w) + head_bias
        total = jax.nn.logsumexp(logits, axis=1)
        picked = lax.optimization_barrier(jnp.sum(logits * hit, axis=1))
        return jnp.sum(mask[:, 0] * (total - picked)) / count
    loss, pullback = jax.vjp(forward, feats, branch_w, branch_gain, branch_shift, branch_slope, mix_slope, mix_w, mix_gain, mix_shift, out_slope, head_w, head_bias)
    grads = pullback(jnp.ones((), jnp.float32))
    return (loss, grads[0], grads[1], grads[2], grads[3], grads[4], grads[5], grads[6], grads[7], grads[8], grads[9], grads[10], grads[11])
```

```python
import functools

import jax
import jax.numpy as jnp
from jax import lax
from jax.experimental import pallas as pl
from jax.experimental.pallas import tpu as pltpu
from jax.sharding import PartitionSpec as P

EPS = 1e-05
F32 = jnp.float32
BF16 = jnp.bfloat16
LANES = 128
VMEM = 56 * 1024 * 1024
TILE = 256
NN = (((1,), (0,)), ((), ()))
NT = (((1,), (1,)), ((), ()))
TN = (((0,), (0,)), ((), ()))


def split(x):
    hi = x.astype(BF16)
    return hi, (x - hi.astype(F32)).astype(BF16)


def dot3(a, b, dims=NN):
    ah, al = a
    bh, bl = b
    dot = functools.partial(lax.dot_general, dimension_numbers=dims, preferred_element_type=F32)
    return dot(ah, bh) + (dot(ah, bl) + dot(al, bh))


def soft(y):
    return jnp.maximum(y, 0.0) + jnp.log(1.0 + jnp.exp(-jnp.abs(y)))


def windows(hops, in_w, width):
    out = []
    for h in range(hops):
        lo = h * in_w // LANES * LANES
        hi = min(-(-(h + 1) * in_w // LANES) * LANES, width)
        out.append((lo, hi))
    return out


def params(**kw):
    return pltpu.CompilerParams(vmem_limit_bytes=VMEM, **kw)


def whole(x):
    return pl.BlockSpec(x.shape, lambda *_: (0,) * len(x.shape))


def row_mask(valid_ref, step, tile):
    n = jnp.sum(valid_ref[...])
    row = step * tile + lax.broadcasted_iota(jnp.int32, (tile, 1), 0)
    return row < n


def branch_kernel(wins, valid_ref, x_ref, wh_ref, wl_ref, z_ref, st_ref):
    step = pl.program_id(0)
    tile = x_ref.shape[0]
    hid = wh_ref.shape[2]
    mask = row_mask(valid_ref, step, tile)

    @pl.when(step == 0)
    def _():
        st_ref[...] = jnp.zeros_like(st_ref)
        n = jnp.sum(valid_ref[...]).astype(F32)
        st_ref[2:3, :] = jnp.broadcast_to(n, (1, st_ref.shape[1]))

    for h, (lo, hi) in enumerate(wins):
        xs = split(x_ref[:, lo:hi])
        z = dot3(xs, (wh_ref[h, : hi - lo, :], wl_ref[h, : hi - lo, :]))
        cols = slice(h * hid, (h + 1) * hid)
        z_ref[:, cols] = z
        zm = jnp.where(mask, z, 0.0)
        st_ref[0:1, cols] += jnp.sum(zm, axis=0, keepdims=True)
        st_ref[1:2, cols] += jnp.sum(zm * zm, axis=0, keepdims=True)


def branch(valid, x, wh, wl, wins):
    rows, width = x.shape
    hops, _, hid = wh.shape
    mix = hops * hid
    return pl.pallas_call(
        functools.partial(branch_kernel, wins),
        grid=(rows // TILE,),
        in_specs=[
            whole(valid),
            pl.BlockSpec((TILE, width), lambda i: (i, 0)),
            whole(wh),
            whole(wl),
        ],
        out_specs=[
            pl.BlockSpec((TILE, mix), lambda i: (i, 0)),
            pl.BlockSpec((3, mix), lambda i: (0, 0)),
        ],
        out_shape=[
            jax.ShapeDtypeStruct((rows, mix), F32),
            jax.ShapeDtypeStruct((3, mix), F32),
        ],
        compiler_params=params(),
        name="branch",
    )(valid, x, wh, wl)


def gram_kernel(wins, valid_ref, x_ref, g_ref, xm_ref):
    step = pl.program_id(0)
    mask = row_mask(valid_ref, step, x_ref.shape[0])

    @pl.when(step == 0)
    def _():
        g_ref[...] = jnp.zeros_like(g_ref)
        xm_ref[...] = jnp.zeros_like(xm_ref)

    x = jnp.where(mask, x_ref[...], 0.0)
    xm_ref[...] += jnp.sum(x, axis=0, keepdims=True)
    xh, xl = split(x)
    for h, (lo, hi) in enumerate(wins):
        xs = xh[:, lo:hi], xl[:, lo:hi]
        g_ref[h, : hi - lo, : hi - lo] += dot3(xs, xs, TN)


def gram(valid, x, wins):
    rows, width = x.shape
    kw = max(hi - lo for lo, hi in wins)
    return pl.pallas_call(
        functools.partial(gram_kernel, wins),
        grid=(rows // TILE,),
        in_specs=[whole(valid), pl.BlockSpec((TILE, width), lambda i: (i, 0))],
        out_specs=[
            pl.BlockSpec((len(wins), kw, kw), lambda i: (0, 0, 0)),
            pl.BlockSpec((1, width), lambda i: (0, 0)),
        ],
        out_shape=[
            jax.ShapeDtypeStruct((len(wins), kw, kw), F32),
            jax.ShapeDtypeStruct((1, width), F32),
        ],
        compiler_params=params(),
        name="gram",
    )(valid, x)


def norm_of(st_ref, cols):
    count = st_ref[2:3, cols]
    mean = st_ref[0:1, cols] / count
    var = st_ref[1:2, cols] / count - mean * mean
    return mean, lax.rsqrt(var + EPS)


def forward_kernel(
    valid_ref, z_ref, st_ref, gain_ref, shift_ref, slope_ref, mslope_ref, w_ref,
    j_ref, uh_ref, ul_ref, v_ref, st2_ref, wh_ref, wl_ref,
):
    step = pl.program_id(0)
    tile = z_ref.shape[0]
    hops, hid = gain_ref.shape
    mask = row_mask(valid_ref, step, tile)

    @pl.when(step == 0)
    def _():
        st2_ref[...] = jnp.zeros_like(st2_ref)
        for h in range(hops):
            rows = slice(h * hid, (h + 1) * hid)
            wh_ref[rows, :], wl_ref[rows, :] = split(w_ref[rows, :])

    v = None
    for h in range(hops):
        cols = slice(h * hid, (h + 1) * hid)
        mean, rstd = norm_of(st_ref, cols)
        a = gain_ref[h : h + 1, :] * rstd
        b = shift_ref[h : h + 1, :] - mean * a
        s1 = slope_ref[h : h + 1, :]
        s2 = mslope_ref[h : h + 1, :]
        y = z_ref[:, cols] * a + b
        j = s1 * y + (1.0 - s1) * soft(y)
        u = s2 * j + (1.0 - s2) * soft(j)
        j_ref[:, cols] = j
        us = split(u)
        uh_ref[:, cols], ul_ref[:, cols] = us
        part = dot3(us, (wh_ref[cols, :], wl_ref[cols, :]))
        v = part if v is None else v + part
    v_ref[...] = v
    vm = jnp.where(mask, v, 0.0)
    st2_ref[0:1, :] += jnp.sum(vm, axis=0, keepdims=True)
    st2_ref[1:2, :] += jnp.sum(vm * vm, axis=0, keepdims=True)


def forward(valid, z, st, gain, shift, slope, mslope, w):
    rows, mix = z.shape
    hid = w.shape[1]
    tile = lambda n: pl.BlockSpec((TILE, n), lambda i: (i, 0))
    return pl.pallas_call(
        forward_kernel,
        grid=(rows // TILE,),
        in_specs=[whole(valid), tile(mix)] + [whole(t) for t in (st, gain, shift, slope, mslope, w)],
        out_specs=[tile(mix), tile(mix), tile(mix), tile(hid)]
        + [pl.BlockSpec(s, lambda i: (0, 0)) for s in ((2, hid), (mix, hid), (mix, hid))],
        out_shape=[
            jax.ShapeDtypeStruct((rows, mix), F32),
            jax.ShapeDtypeStruct((rows, mix), BF16),
            jax.ShapeDtypeStruct((rows, mix), BF16),
            jax.ShapeDtypeStruct((rows, hid), F32),
            jax.ShapeDtypeStruct((2, hid), F32),
            jax.ShapeDtypeStruct((mix, hid), BF16),
            jax.ShapeDtypeStruct((mix, hid), BF16),
        ],
        compiler_params=params(),
        name="forward",
    )(valid, z, st, gain, shift, slope, mslope, w)


def head_kernel(
    valid_ref, labels_ref, v_ref, st_ref, cnt_ref, gain_ref, shift_ref, slope_ref, hw_ref, hb_ref,
    dy_ref, st3_ref, misc_ref,
):
    step = pl.program_id(0)
    tile, hid = v_ref.shape
    classes = hw_ref.shape[1]
    mask = row_mask(valid_ref, step, tile)
    count = cnt_ref[2:3, 0:1]

    @pl.when(step == 0)
    def _():
        st3_ref[...] = jnp.zeros_like(st3_ref)
        misc_ref[...] = jnp.zeros_like(misc_ref)

    mean = st_ref[0:1, :] / count
    rstd = lax.rsqrt(st_ref[1:2, :] / count - mean * mean + EPS)
    s = slope_ref[...]
    zn = (v_ref[...] - mean) * rstd
    y = gain_ref[...] * zn + shift_ref[...]
    sp = soft(y)
    w = s * y + (1.0 - s) * sp
    ws = split(w)
    hw = split(hw_ref[...])
    logits = dot3(ws, hw) + hb_ref[...]
    peak = jnp.max(logits, axis=1, keepdims=True)
    ex = jnp.exp(logits - peak)
    tot = jnp.sum(ex, axis=1, keepdims=True)
    lab = labels_ref[pl.ds(step * (tile // LANES), tile // LANES), :]
    lab = jnp.concatenate(
        [jnp.broadcast_to(lab[k : k + 1, :], (LANES, LANES)).T for k in range(tile // LANES)], axis=0
    )
    hit = lab[:, :classes] == lax.broadcasted_iota(jnp.int32, (tile, classes), 1)
    picked = jnp.sum(jnp.where(hit, logits, 0.0), axis=1, keepdims=True)
    loss = jnp.sum(jnp.where(mask, peak + jnp.log(tot) - picked, 0.0))
    dl = jnp.where(mask, (ex / tot - hit.astype(F32)) / count, 0.0)
    dls = split(dl)
    misc_ref[0:classes, :] += dot3(dls, ws, TN)
    misc_ref[classes : classes + 1, 0:classes] += jnp.sum(dl, axis=0, keepdims=True)
    misc_ref[classes : classes + 1, LANES : 2 * LANES] += jnp.broadcast_to(loss, (1, LANES))
    dw = dot3(dls, hw, NT)
    dy = dw * (1.0 - (1.0 - s) * jnp.exp(-sp))
    dy_ref[...] = dy
    misc_ref[classes + 1 : classes + 2, :] += jnp.sum(dw * (y - sp), axis=0, keepdims=True)
    st3_ref[0:1, :] += jnp.sum(dy, axis=0, keepdims=True)
    st3_ref[1:2, :] += jnp.sum(dy * zn, axis=0, keepdims=True)


def head(valid, labels, v, st2, st, gain, shift, slope, hw, hb):
    rows, hid = v.shape
    tile = lambda n: pl.BlockSpec((TILE, n), lambda i: (i, 0))
    misc = -(-(hw.shape[1] + 2) // 8) * 8
    return pl.pallas_call(
        head_kernel,
        grid=(rows // TILE,),
        in_specs=[whole(valid), whole(labels), tile(hid)]
        + [whole(t) for t in (st2, st, gain, shift, slope, hw, hb)],
        out_specs=[
            tile(hid),
            pl.BlockSpec((2, hid), lambda i: (0, 0)),
            pl.BlockSpec((misc, hid), lambda i: (0, 0)),
        ],
        out_shape=[
            jax.ShapeDtypeStruct((rows, hid), F32),
            jax.ShapeDtypeStruct((2, hid), F32),
            jax.ShapeDtypeStruct((misc, hid), F32),
        ],
        compiler_params=params(),
        name="head",
    )(valid, labels, v, st2, st, gain, shift, slope, hw, hb)


def mix_kernel(
    valid_ref, dy_ref, v_ref, st2_ref, cnt_ref, st3_ref, gain_ref, uh_ref, ul_ref,
    m_ref, dvh_ref, dvl_ref,
):
    step = pl.program_id(0)
    tile = dy_ref.shape[0]
    mask = row_mask(valid_ref, step, tile)
    count = cnt_ref[2:3, 0:1]
    mean = st2_ref[0:1, :] / count
    rstd = lax.rsqrt(st2_ref[1:2, :] / count - mean * mean + EPS)
    a = gain_ref[...] * rstd
    c1 = a * st3_ref[0:1, :] / count
    c2 = a * st3_ref[1:2, :] / count
    zn = (v_ref[...] - mean) * rstd
    dv = jnp.where(mask, a * dy_ref[...] - (c1 + zn * c2), 0.0)
    dvs = split(dv)
    dvh_ref[...], dvl_ref[...] = dvs

    @pl.when(step == 0)
    def _():
        m_ref[...] = jnp.zeros_like(m_ref)

    hid = dy_ref.shape[1]
    for h in range(uh_ref.shape[1] // hid):
        cols = slice(h * hid, (h + 1) * hid)
        m_ref[cols, :] += dot3((uh_ref[:, cols], ul_ref[:, cols]), dvs, TN)


def mix_back(valid, dy, v, st2, st, st3, gain, uh, ul):
    rows, hid = dy.shape
    mix = uh.shape[1]
    tile = lambda n: pl.BlockSpec((TILE, n), lambda i: (i, 0))
    return pl.pallas_call(
        mix_kernel,
        grid=(rows // TILE,),
        in_specs=[whole(valid), tile(hid), tile(hid)]
        + [whole(t) for t in (st2, st, st3, gain)]
        + [tile(mix), tile(mix)],
        out_specs=[pl.BlockSpec((mix, hid), lambda i: (0, 0)), tile(hid), tile(hid)],
        out_shape=[
            jax.ShapeDtypeStruct((mix, hid), F32),
            jax.ShapeDtypeStruct((rows, hid), BF16),
            jax.ShapeDtypeStruct((rows, hid), BF16),
        ],
        compiler_params=params(),
        name="mix_back",
    )(valid, dy, v, st2, st, st3, gain, uh, ul)


def hop_kernel(
    h, lo, hi, st_ref, gain_ref, shift_ref, slope_ref, mslope_ref, dvh_ref, dvl_ref, mwh_ref, mwl_ref,
    z_ref, j_ref, uh_ref, ul_ref, x_ref, bwh_ref, bwl_ref,
    dx_ref, bw_ref, sums_ref,
):
    step = pl.program_id(0)

    @pl.when(step == 0)
    def _():
        bw_ref[...] = jnp.zeros_like(bw_ref)
        sums_ref[...] = jnp.zeros_like(sums_ref)

    mean, rstd = norm_of(st_ref, slice(None))
    gain = gain_ref[h : h + 1, :]
    a = gain * rstd
    b = shift_ref[h : h + 1, :] - mean * a
    s1 = slope_ref[h : h + 1, :]
    s2 = mslope_ref[h : h + 1, :]
    y = z_ref[...] * a + b
    j = j_ref[...]
    u = uh_ref[...].astype(F32) + ul_ref[...].astype(F32)
    du = dot3((dvh_ref[...], dvl_ref[...]), (mwh_ref[...], mwl_ref[...]), NT)
    r2 = 1.0 / (1.0 - s2)
    r1 = 1.0 / (1.0 - s1)
    dj = du * (1.0 - (1.0 - s2) * jnp.exp((s2 * r2) * j - r2 * u))
    dy = dj * (1.0 - (1.0 - s1) * jnp.exp((s1 * r1) * y - r1 * j))
    row = lambda t: jnp.sum(t, axis=0, keepdims=True)
    sums_ref[0:1, :] += row(dy)
    sums_ref[1:2, :] += row(dy * y)
    sums_ref[2:3, :] += row(dj * (y - j)) * r1
    sums_ref[3:4, :] += row(du * (j - u)) * r2
    dys = split(dy * a)
    wb = bwh_ref[0, : hi - lo, :], bwl_ref[0, : hi - lo, :]
    dx_ref[...] = dot3(dys, wb, NT)
    bw_ref[...] += dot3(split(x_ref[:, lo:hi]), dys, TN)


def hop_back(h, lo, hi, st, gain, shift, slope, mslope, dvh, dvl, mwh, mwl, z, j, uh, ul, x, bwh, bwl):
    rows, width = x.shape
    hid = dvh.shape[1]
    kw = bwh.shape[1]
    tile = lambda n, k=0: pl.BlockSpec((TILE, n), lambda i: (i, k))
    block = lambda r: pl.BlockSpec((r, hid), lambda i: (h, 0))
    return pl.pallas_call(
        functools.partial(hop_kernel, h, lo, hi),
        grid=(rows // TILE,),
        in_specs=[pl.BlockSpec((3, hid), lambda i: (0, h))]
        + [whole(t) for t in (gain, shift, slope, mslope)]
        + [tile(hid), tile(hid), block(hid), block(hid)]
        + [tile(hid, h)] * 4
        + [tile(width)]
        + [pl.BlockSpec((1, kw, hid), lambda i: (h, 0, 0))] * 2,
        out_specs=[
            tile(hi - lo),
            pl.BlockSpec((hi - lo, hid), lambda i: (0, 0)),
            pl.BlockSpec((4, hid), lambda i: (0, 0)),
        ],
        out_shape=[
            jax.ShapeDtypeStruct((rows, hi - lo), F32),
            jax.ShapeDtypeStruct((hi - lo, hid), F32),
            jax.ShapeDtypeStruct((4, hid), F32),
        ],
        compiler_params=params(),
        name=f"hop_back_{h}",
    )(st, gain, shift, slope, mslope, dvh, dvl, mwh, mwl, z, j, uh, ul, x, bwh, bwl)


def branch_fix_kernel(
    wins, in_w, st_ref, tot_ref, own_ref, gain_ref, shift_ref, g_ref, xm_ref, wh_ref, wl_ref,
    *refs,
):
    hops = len(wins)
    bws, (misc_ref, out_ref, q_ref, r_ref, gs_ref) = refs[:hops], refs[hops:]
    hid = gain_ref.shape[1]
    pad = -(-in_w // 8) * 8
    out_ref[...] = jnp.zeros_like(out_ref)
    for h, (lo, hi) in enumerate(wins):
        cols = slice(h * hid, (h + 1) * hid)
        n = hi - lo
        off = h * in_w - lo
        mean, rstd = norm_of(st_ref, cols)
        count = st_ref[2:3, cols]
        gain = gain_ref[h : h + 1, :]
        total = tot_ref[4 * h : 4 * h + 1, :]
        gsum = (tot_ref[4 * h + 1 : 4 * h + 2, :] - shift_ref[h : h + 1, :] * total) / gain
        gs_ref[h : h + 1, :] = gsum
        a = gain * rstd
        c1 = a * total / count
        c2 = a * gsum * rstd / count
        wh, wl = wh_ref[h, :n, :], wl_ref[h, :n, :]
        w = wh.astype(F32) + wl.astype(F32)
        wc = split(w * c2)
        k0 = c1 - mean * c2
        q_ref[h, :n, :n] = dot3((wh, wl), wc, NT)
        r_ref[h : h + 1, :n] = dot3(split(jnp.broadcast_to(k0, (8, hid))), (wh, wl), NT)[0:1, :]
        xm = jnp.broadcast_to(xm_ref[0:1, lo:hi], (LANES, n)).T[:, 0:1]
        bw = bws[h][...] - dot3(split(g_ref[h, :n, :n]), wc) - xm * k0
        out_ref[h * pad : h * pad + in_w, :] = bw[off : off + in_w, :]
    base = hops * pad
    k = misc_ref.shape[0]
    out_ref[base : base + k, :] = misc_ref[...]
    out_ref[base + k : base + k + 4 * hops, :] = own_ref[...]


def branch_fix(st, tot, own, gain, shift, g, xm, wh, wl, bws, misc, wins, in_w):
    hops, hid = gain.shape
    kw = g.shape[1]
    rows = hops * (-(-in_w // 8) * 8) + misc.shape[0] + 4 * hops
    rows = -(-rows // 512) * 512
    args = (st, tot, own, gain, shift, g, xm, wh, wl, *bws, misc)
    shapes = ((rows, hid), (hops, kw, kw), (hops, kw), (hops, hid))
    return pl.pallas_call(
        functools.partial(branch_fix_kernel, wins, in_w),
        out_shape=[jax.ShapeDtypeStruct(s, F32) for s in shapes],
        compiler_params=params(),
        name="branch_fix",
    )(*args)


def feats_kernel(wins, valid_ref, x_ref, q_ref, r_ref, *refs):
    dxs, out_ref = refs[:-1], refs[-1]
    tile = x_ref.shape[0]
    mask = row_mask(valid_ref, pl.program_id(0), tile)
    xh, xl = split(x_ref[...])
    pieces = {}
    for h, (lo, hi) in enumerate(wins):
        n = hi - lo
        fix = dot3((xh[:, lo:hi], xl[:, lo:hi]), split(q_ref[h, :n, :n]), NT) + r_ref[h : h + 1, :n]
        d = dxs[h][...] - jnp.where(mask, fix, 0.0)
        for c in range(lo, hi, LANES):
            e = min(c + LANES, hi)
            part = d[:, c - lo : e - lo]
            pieces[c, e] = pieces[c, e] + part if (c, e) in pieces else part
    for (c, e), part in pieces.items():
        out_ref[:, c:e] = part


def feats_fix(valid, x, q, r, dxs, wins):
    rows, width = x.shape
    tile = lambda n: pl.BlockSpec((TILE, n), lambda i: (i, 0))
    return pl.pallas_call(
        functools.partial(feats_kernel, wins),
        grid=(rows // TILE,),
        in_specs=[whole(valid), tile(width), whole(q), whole(r)] + [tile(d.shape[1]) for d in dxs],
        out_specs=tile(width),
        out_shape=jax.ShapeDtypeStruct((rows, width), F32),
        compiler_params=params(),
        name="feats_fix",
    )(valid, x, q, r, *dxs)


def flip(v, axis, size, k):
    return lax.ppermute(v, axis, [(i, i ^ k) for i in range(size)])


def sum_small(v, sizes):
    steps = []
    for axis, size in sizes.items():
        k = 1
        if axis == "dp" and size >= 2:
            steps.append((axis, size, 1, 2))
            k = 2
        while k < size:
            wide = 4 if 4 * k <= size else 2
            steps.append((axis, size, k, wide))
            k *= wide
    for axis, size, k, wide in steps:
        if wide == 2:
            v = v + flip(v, axis, size, k)
        else:
            p1, p2, p3 = (flip(v, axis, size, k * m) for m in (1, 2, 3))
            v = (v + p1) + (p2 + p3)
    return v


def halve(v, axis, size, k):
    bit = lax.axis_index(axis) // k % 2
    n = v.shape[0] // 2
    got = flip(lax.dynamic_slice_in_dim(v, (1 - bit) * n, n, 0), axis, size, k)
    return lax.dynamic_slice_in_dim(v, bit * n, n, 0) + got


def double(v, axis, size, k):
    bit = lax.axis_index(axis) // k % 2
    got = flip(v, axis, size, k)
    return jnp.where(bit == 0, jnp.concatenate([v, got], 0), jnp.concatenate([got, v], 0))


def sum_along(v, order):
    for s in order:
        v = halve(v, *s)
    for s in reversed(order):
        v = double(v, *s)
    return v


def sum_large(v, sizes):
    dp, bucket = sizes["dp"], sizes["bucket"]
    bits = lambda n: [1 << i for i in range(n.bit_length() - 1)]
    core = [("dp", dp, 1)] if dp > 1 else []
    square = [("dp", dp, k) for k in bits(dp) if k > 1]
    depth = [("bucket", bucket, k) for k in bits(bucket)]
    for s in core:
        v = halve(v, *s)
    n = v.shape[0] // 2
    v = jnp.concatenate(
        [sum_along(v[:n], square + depth), sum_along(v[n:], square[::-1] + depth)], 0
    )
    for s in core:
        v = double(v, *s)
    return v


def per_device(sizes, feats, labels, valid, branch_w, branch_gain, branch_shift, branch_slope, mix_slope,
               mix_w, mix_gain, mix_shift, out_slope, head_w, head_bias):
    rows, width = feats.shape
    hops, in_w, hid = branch_w.shape
    classes = head_w.shape[1]
    mix = hops * hid
    wins = windows(hops, in_w, width)
    kw = max(hi - lo for lo, hi in wins)
    valid = valid.reshape(rows // LANES, LANES)
    labels = labels.reshape(rows // LANES, LANES)
    mslope = mix_slope.reshape(hops, hid)
    row = lambda t: t.reshape(1, -1)
    wide = jnp.stack(
        [
            jnp.pad(branch_w[h], ((h * in_w - lo, kw - (h * in_w - lo) - in_w), (0, 0)))
            for h, (lo, hi) in enumerate(wins)
        ]
    )
    hi_part = lax.reduce_precision(wide, 8, 7)
    bwh = hi_part.astype(BF16)
    bwl = (wide - hi_part).astype(BF16)

    z, st = branch(valid, feats, bwh, bwl, wins)
    st = sum_small(st, sizes)
    g, xm = gram(valid, feats, wins)
    j, uh, ul, v, st2, mwh, mwl = forward(
        valid, z, st, branch_gain, branch_shift, branch_slope, mslope, mix_w
    )
    st2 = sum_small(st2, sizes)
    dy2, st3, misc = head(
        valid, labels, v, st2, st, row(mix_gain), row(mix_shift), row(out_slope), head_w, row(head_bias)
    )
    st3 = sum_small(st3, sizes)
    m, dvh, dvl = mix_back(valid, dy2, v, st2, st, st3, row(mix_gain), uh, ul)
    dxs, bws, sums = [], [], []
    for h, (lo, hi) in enumerate(wins):
        dx, bw, s = hop_back(
            h, lo, hi, st, branch_gain, branch_shift, branch_slope, mslope, dvh, dvl, mwh, mwl,
            z, j, uh, ul, feats, bwh, bwl,
        )
        dxs.append(dx)
        bws.append(bw)
        sums.append(s)
    m = sum_large(m, sizes)
    own = jnp.concatenate(sums, 0)
    tot = sum_small(own, sizes)
    packed, q, r, branch_gain_grad = branch_fix(
        st, tot, own, branch_gain, branch_shift, g, xm, bwh, bwl, bws, misc, wins, in_w
    )
    packed = sum_large(packed, sizes)
    d_x = feats_fix(valid, feats, q, r, dxs, wins)

    count = st[2, 0]
    pad = -(-in_w // 8) * 8
    base = hops * pad
    k = misc.shape[0]
    tail = packed[base : base + k + 4 * hops]
    per_hop = tail[k:].reshape(hops, 4, hid)
    return (
        tail[classes, LANES] / count,
        d_x,
        packed[:base].reshape(hops, pad, hid)[:, :in_w, :],
        branch_gain_grad,
        per_hop[:, 0, :],
        per_hop[:, 2, :],
        per_hop[:, 3, :].reshape(mix),
        m,
        st3[1],
        st3[0],
        tail[classes + 1],
        tail[:classes].T,
        tail[classes, :classes],
    )


def solution(mesh):
    sizes = {axis: mesh.shape[axis] for axis in ("dp", "bucket")}
    split_rows = P(("dp", "bucket"), None)
    in_specs = (split_rows, P(("dp", "bucket")), P(("dp", "bucket"))) + (P(),) * 11
    out_specs = (P(), split_rows) + (P(),) * 11
    return jax.shard_map(
        functools.partial(per_device, sizes),
        mesh=mesh,
        in_specs=in_specs,
        out_specs=out_specs,
        check_vma=False,
    )
```

```python
import functools

import jax
import jax.numpy as jnp
from jax import lax
from jax.experimental import pallas as pl
from jax.experimental.pallas import tpu as pltpu
from jax.sharding import PartitionSpec as P

EPS = 1e-05
F32 = jnp.float32
BF16 = jnp.bfloat16
LANES = 128
VMEM = 56 * 1024 * 1024
LOG2E = 1.4426950408889634
LN2 = 0.6931471805599453
TILES = {"gram": 1024, "forward": 512, "head": 512, "mix": 512, "hop": 512, "fix": 512}
HOP_STAGES = 3
PACK_STAGES = 2
SUB = 256
CHUNK = 512
NN = (((1,), (0,)), ((), ()))
NT = (((1,), (1,)), ((), ()))
TN = (((0,), (0,)), ((), ()))


def split(x):
    hi = x.astype(BF16)
    return hi, (x - hi.astype(F32)).astype(BF16)


def dot3(a, b, dims=NN):
    ah, al = a
    bh, bl = b
    dot = functools.partial(lax.dot_general, dimension_numbers=dims, preferred_element_type=F32)
    return dot(ah, bh) + (dot(ah, bl) + dot(al, bh))


def act2(y, slope, rest):
    return jnp.maximum(slope * y + rest * jnp.log(1.0 + jnp.exp2(jnp.minimum(y, 30.0))), y)


def cost(us):
    return pl.CostEstimate(flops=0, bytes_accessed=int(us * 3.69e6), transcendentals=0)


def params(**kw):
    return pltpu.CompilerParams(vmem_limit_bytes=VMEM, **kw)


def whole(x):
    return pl.BlockSpec(x.shape, lambda *_: (0,) * len(x.shape))


def row_mask(valid_ref, step, tile, axis=0):
    n = jnp.sum(valid_ref[...])
    shape = (tile, 1) if axis == 0 else (1, tile)
    return step * tile + lax.broadcasted_iota(jnp.int32, shape, axis) < n


def hop_rows(x_ref, h, in_w, extra=None):
    x = x_ref[h * in_w : (h + 1) * in_w, :]
    pad = -(-(in_w + 1) // 16) * 16 - in_w
    tail = jnp.zeros((pad, x.shape[1]), F32)
    if extra is not None:
        first = lax.broadcasted_iota(jnp.int32, tail.shape, 0) == 0
        tail = jnp.where(first, extra, 0.0)
    return jnp.concatenate([x, tail], axis=0)


def stack3(a):
    hi, lo = split(a)
    return jnp.concatenate([hi, lo, hi], axis=0)


def gram_kernel(in_w, valid_ref, x_ref, w_ref, g_ref, st_ref, wp_ref):
    step = pl.program_id(0)
    tile = x_ref.shape[1]
    hops, hid = w_ref.shape[1:]
    mask = row_mask(valid_ref, step, tile, 1)

    @pl.when(step == 0)
    def _():
        g_ref[...] = jnp.zeros_like(g_ref)

    for h in range(hops):
        x = jnp.where(mask, hop_rows(x_ref, h, in_w, 1.0), 0.0)
        hi, lo = split(x)
        n = x.shape[0]
        dot = functools.partial(lax.dot_general, dimension_numbers=NT, preferred_element_type=F32)
        cross = dot(hi, lo)
        g_ref[h, :, :n] += dot(hi, hi) + (cross + cross.T)

    @pl.when(step == pl.num_programs(0) - 1)
    def _():
        for h in range(hops):
            n = g_ref.shape[1]
            w = w_ref[:, h, :]
            w = jnp.concatenate([w, jnp.zeros((n - in_w, hid), F32)], axis=0)
            ws = split(w)
            g = g_ref[h, :, :n]
            gw = dot3(split(g), ws)
            cols = slice(h * hid, (h + 1) * hid)
            st_ref[0:1, cols] = gw[in_w : in_w + 1, :]
            st_ref[1:2, cols] = jnp.sum(w * gw, axis=0, keepdims=True)
            wp_ref[h] = jnp.concatenate([ws[0], ws[0], ws[1]], axis=0)
        st_ref[:, hops * hid :] = jnp.broadcast_to(g_ref[0, in_w : in_w + 1, in_w : in_w + 1], (2, LANES))


def gram(valid, x, w, tile):
    width, rows = x.shape
    in_w, hops, hid = w.shape
    n = -(-(in_w + 1) // 16) * 16
    shapes = ((hops, n, LANES), F32), ((2, hops * hid + LANES), F32), ((hops, 3 * n, hid), BF16)
    return pl.pallas_call(
        functools.partial(gram_kernel, in_w),
        grid=(rows // tile,),
        in_specs=[whole(valid), pl.BlockSpec((width, tile), lambda i: (0, i)), whole(w)],
        out_specs=[pl.BlockSpec(s, lambda i, s=s: (0,) * len(s)) for s, _ in shapes],
        out_shape=[jax.ShapeDtypeStruct(*s) for s in shapes],
        compiler_params=params(),
        name="gram",
        cost_estimate=cost(5),
    )(valid, x, w)


def count_of(st_ref):
    return st_ref[0:1, st_ref.shape[1] - 1 :]


def norm_of(st_ref, cols):
    count = count_of(st_ref)
    mean = st_ref[0:1, cols] / count
    var = st_ref[1:2, cols] / count - mean * mean
    return mean, lax.rsqrt(var + EPS)


def scale_of(st_ref, cols, gain_ref, shift_ref, h):
    mean, rstd = norm_of(st_ref, cols)
    a = gain_ref[h : h + 1, :] * rstd
    return LOG2E * a, LOG2E * (shift_ref[h : h + 1, :] - mean * a)


def forward_kernel(
    in_w, valid_ref, x_ref, wp_ref, st_ref, gain_ref, shift_ref, slope_ref, mslope_ref, w_ref,
    j_ref, uh_ref, ul_ref, v_ref, st2_ref, wh_ref, wl_ref,
):
    step = pl.program_id(0)
    tile = x_ref.shape[1]
    hops, hid = gain_ref.shape
    mask = row_mask(valid_ref, step, tile)

    @pl.when(step == 0)
    def _():
        st2_ref[...] = jnp.zeros_like(st2_ref)
        for h in range(hops):
            rows = slice(h * hid, (h + 1) * hid)
            wh_ref[rows, :], wl_ref[rows, :] = split(w_ref[rows, :])

    dot = functools.partial(lax.dot_general, preferred_element_type=F32)
    chunks = [(h, slice(r, r + CHUNK)) for h in range(hops) for r in range(0, tile, CHUNK)]
    scales, xs = {}, {}

    def project(i):
        h, rows = chunks[i]
        if h not in xs:
            xs[h] = stack3(hop_rows(x_ref, h, in_w))
        return dot(xs[h][:, rows], wp_ref[h], TN)

    def activate(i, z):
        h, rows = chunks[i]
        cols = slice(h * hid, (h + 1) * hid)
        if h not in scales:
            scales[h] = scale_of(st_ref, cols, gain_ref, shift_ref, h)
        a, b = scales[h]
        s1 = slope_ref[h : h + 1, :]
        s2 = mslope_ref[h : h + 1, :]
        j = act2(z * a + b, s1, LOG2E * (1.0 - s1))
        u = act2(j, s2, LOG2E * (1.0 - s2))
        j_ref[rows, cols] = j
        us = split(u)
        uh_ref[rows, cols], ul_ref[rows, cols] = us
        return us

    def mix(i, us):
        h, rows = chunks[i]
        cols = slice(h * hid, (h + 1) * hid)
        both = dot(jnp.concatenate(us, axis=0), wh_ref[cols, :], NN)
        part = both[:CHUNK] + both[CHUNK:] + dot(us[0], wl_ref[cols, :], NN)
        v_ref[rows, :] = part if h == 0 else v_ref[rows, :] + part

    z = project(0)
    before = None
    for i in range(len(chunks)):
        ahead = project(i + 1) if i + 1 < len(chunks) else None
        if before is not None:
            mix(i - 1, before)
        before = activate(i, z)
        z = ahead
    mix(len(chunks) - 1, before)
    v = v_ref[...]
    v = LN2 * v
    v_ref[...] = v
    vm = jnp.where(mask, v, 0.0)
    st2_ref[0:1, :] += jnp.sum(vm, axis=0, keepdims=True)
    st2_ref[1:2, :] += jnp.sum(vm * vm, axis=0, keepdims=True)


def forward(valid, x, wp, st, gain, shift, slope, mslope, w, in_w, tile):
    width, rows = x.shape
    mix, hid = w.shape
    by = lambda n: pl.BlockSpec((tile, n), lambda i: (i, 0))
    return pl.pallas_call(
        functools.partial(forward_kernel, in_w),
        grid=(rows // tile,),
        in_specs=[whole(valid), pl.BlockSpec((width, tile), lambda i: (0, i))]
        + [whole(t) for t in (wp, st, gain, shift, slope, mslope, w)],
        out_specs=[by(mix), by(mix), by(mix), by(hid)]
        + [pl.BlockSpec(s, lambda i: (0, 0)) for s in ((2, hid), (mix, hid), (mix, hid))],
        out_shape=[
            jax.ShapeDtypeStruct((rows, mix), F32),
            jax.ShapeDtypeStruct((rows, mix), BF16),
            jax.ShapeDtypeStruct((rows, mix), BF16),
            jax.ShapeDtypeStruct((rows, hid), F32),
            jax.ShapeDtypeStruct((2, hid), F32),
            jax.ShapeDtypeStruct((mix, hid), BF16),
            jax.ShapeDtypeStruct((mix, hid), BF16),
        ],
        compiler_params=params(),
        name="forward",
        cost_estimate=cost(30),
    )(valid, x, wp, st, gain, shift, slope, mslope, w)


def as_column(row):
    n = row.shape[1]
    same = lax.broadcasted_iota(jnp.int32, (n, n), 0) == lax.broadcasted_iota(jnp.int32, (n, n), 1)
    return jnp.sum(jnp.where(same, jnp.broadcast_to(row, (n, n)), 0.0), axis=1, keepdims=True)


def as_row(col):
    n = col.shape[0]
    same = lax.broadcasted_iota(jnp.int32, (n, n), 0) == lax.broadcasted_iota(jnp.int32, (n, n), 1)
    return jnp.sum(jnp.where(same, jnp.broadcast_to(col, (n, n)), 0.0), axis=0, keepdims=True)


def head_kernel(
    valid_ref, labels_ref, v_ref, st_ref, cnt_ref, gain_ref, shift_ref, slope_ref, hw_ref, hb_ref,
    dy_ref, st3_ref, misc_ref,
):
    step = pl.program_id(0)
    tile, hid = v_ref.shape
    classes = hw_ref.shape[0]
    padded = -(-classes // 16) * 16
    mask = row_mask(valid_ref, step, tile, 1)
    count = count_of(cnt_ref)

    @pl.when(step == 0)
    def _():
        st3_ref[...] = jnp.zeros_like(st3_ref)
        misc_ref[...] = jnp.zeros_like(misc_ref)

    mean = st_ref[0:1, :] / count
    rstd = lax.rsqrt(st_ref[1:2, :] / count - mean * mean + EPS)
    s = slope_ref[...]
    zn = (v_ref[...] - mean) * rstd
    y = gain_ref[...] * zn + shift_ref[...]
    e1 = 1.0 + jnp.exp(jnp.minimum(y, 20.0))
    sp = jnp.maximum(jnp.log(e1), y)
    w = s * y + (1.0 - s) * sp
    ws = split(w)
    hw = hw_ref[...]
    if padded > classes:
        hw = jnp.concatenate([hw, jnp.zeros((padded - classes, hid), F32)], axis=0)
    hh, hl = split(hw)
    dot = functools.partial(lax.dot_general, dimension_numbers=NT, preferred_element_type=F32)
    both = dot(jnp.concatenate([hh, hl], axis=0), ws[0])
    logits = both[:padded] + both[padded:] + dot(hh, ws[1])
    logits = logits[:classes] + as_column(hb_ref[...])
    peak = jnp.max(logits, axis=0, keepdims=True)
    ex = jnp.exp(logits - peak)
    tot = jnp.sum(ex, axis=0, keepdims=True)
    per = tile // LANES
    lab = jnp.concatenate([labels_ref[pl.ds(step * per + k, 1), :] for k in range(per)], axis=1)
    hit = lab == lax.broadcasted_iota(jnp.int32, (classes, tile), 0)
    picked = jnp.sum(jnp.where(hit, logits, 0.0), axis=0, keepdims=True)
    loss = jnp.sum(jnp.where(mask, peak + jnp.log(tot) - picked, 0.0))
    dl = jnp.where(mask, (ex / tot - hit.astype(F32)) / count, 0.0)
    bias = as_row(jnp.sum(dl, axis=1, keepdims=True))
    if padded > classes:
        dl = jnp.concatenate([dl, jnp.zeros((padded - classes, tile), F32)], axis=0)
    dh, dlo = split(dl)
    dot = functools.partial(lax.dot_general, dimension_numbers=NN, preferred_element_type=F32)
    both = dot(jnp.concatenate([dh, dlo], axis=0), ws[0])
    hwg = both[:padded] + both[padded:] + dot(dh, ws[1])
    misc_ref[0:classes, :] += hwg[:classes]
    misc_ref[classes : classes + 1, 0:classes] += bias
    misc_ref[classes : classes + 1, LANES : 2 * LANES] += jnp.broadcast_to(loss, (1, LANES))
    dw = lax.dot_general(
        jnp.concatenate([dh, dlo, dh], axis=0),
        jnp.concatenate([hh, hh, hl], axis=0),
        TN,
        preferred_element_type=F32,
    )
    dy = dw * (1.0 - (1.0 - s) / e1)
    dy_ref[...] = dy
    row = lambda t: jnp.sum(t, axis=0, keepdims=True)
    misc_ref[classes + 1 : classes + 2, :] += row(dw * (y - sp))
    st3_ref[0:1, :] += row(dy)
    st3_ref[1:2, :] += row(dy * zn)


def head(valid, labels, v, st2, st, gain, shift, slope, hw, hb, tile):
    rows, hid = v.shape
    by = lambda n: pl.BlockSpec((tile, n), lambda i: (i, 0))
    misc = -(-(hw.shape[0] + 2) // 8) * 8
    return pl.pallas_call(
        head_kernel,
        grid=(rows // tile,),
        in_specs=[whole(valid), whole(labels), by(hid)]
        + [whole(t) for t in (st2, st, gain, shift, slope, hw, hb)],
        out_specs=[
            by(hid),
            pl.BlockSpec((2, hid), lambda i: (0, 0)),
            pl.BlockSpec((misc, hid), lambda i: (0, 0)),
        ],
        out_shape=[
            jax.ShapeDtypeStruct((rows, hid), F32),
            jax.ShapeDtypeStruct((2, hid), F32),
            jax.ShapeDtypeStruct((misc, hid), F32),
        ],
        compiler_params=params(),
        name="head",
        cost_estimate=cost(9),
    )(valid, labels, v, st2, st, gain, shift, slope, hw, hb)


def mix_dv(valid_ref, dy_ref, v_ref, st2_ref, cnt_ref, st3_ref, gain_ref):
    mask = row_mask(valid_ref, pl.program_id(0), dy_ref.shape[0])
    count = count_of(cnt_ref)
    mean = st2_ref[0:1, :] / count
    rstd = lax.rsqrt(st2_ref[1:2, :] / count - mean * mean + EPS)
    a = LN2 * gain_ref[...] * rstd
    c1 = a * st3_ref[0:1, :] / count
    c2 = a * st3_ref[1:2, :] / count
    zn = (v_ref[...] - mean) * rstd
    return split(jnp.where(mask, a * dy_ref[...] - (c1 + zn * c2), 0.0))


def mix_product(dvs, uh_ref, ul_ref, m_ref):
    @pl.when(pl.program_id(0) == 0)
    def _():
        m_ref[...] = jnp.zeros_like(m_ref)

    hid = dvs[0].shape[1]
    for h in range(uh_ref.shape[1] // hid):
        cols = slice(h * hid, (h + 1) * hid)
        m_ref[cols, :] += dot3((uh_ref[:, cols], ul_ref[:, cols]), dvs, TN)


def mix_first_kernel(half_ref, *refs):
    ins, (uh_ref, ul_ref, m_ref, dvh_ref, dvl_ref) = refs[:7], refs[7:]
    dvs = mix_dv(*ins)
    dvh_ref[...], dvl_ref[...] = dvs
    mix_product(dvs, uh_ref, ul_ref, m_ref)


def mix_second_kernel(half_ref, dvh_ref, dvl_ref, uh_ref, ul_ref, m_ref):
    mix_product((dvh_ref[...], dvl_ref[...]), uh_ref, ul_ref, m_ref)


def mix_back(half, valid, dy, v, st2, st, st3, gain, uh, ul, tile):
    rows, hid = dy.shape
    part = uh.shape[1] // 2
    by = lambda n: pl.BlockSpec((tile, n), lambda i, half: (i, 0))
    return pl.pallas_call(
        mix_first_kernel,
        grid_spec=pltpu.PrefetchScalarGridSpec(
            num_scalar_prefetch=1,
            grid=(rows // tile,),
            in_specs=[whole(valid), by(hid), by(hid)]
            + [whole(t) for t in (st2, st, st3, gain)]
            + [pl.BlockSpec((tile, part), lambda i, half: (i, half[0]))] * 2,
            out_specs=[pl.BlockSpec((part, hid), lambda i, half: (0, 0)), by(hid), by(hid)],
        ),
        out_shape=[
            jax.ShapeDtypeStruct((part, hid), F32),
            jax.ShapeDtypeStruct((rows, hid), BF16),
            jax.ShapeDtypeStruct((rows, hid), BF16),
        ],
        compiler_params=params(),
        name="mix_back",
        cost_estimate=cost(14),
    )(half, valid, dy, v, st2, st, st3, gain, uh, ul)


def mix_back_rest(half, dvh, dvl, uh, ul, tile):
    rows, hid = dvh.shape
    part = uh.shape[1] // 2
    by = lambda n: pl.BlockSpec((tile, n), lambda i, half: (i, 0))
    return pl.pallas_call(
        mix_second_kernel,
        grid_spec=pltpu.PrefetchScalarGridSpec(
            num_scalar_prefetch=1,
            grid=(rows // tile,),
            in_specs=[by(hid), by(hid)]
            + [pl.BlockSpec((tile, part), lambda i, half: (i, half[0]))] * 2,
            out_specs=pl.BlockSpec((part, hid), lambda i, half: (0, 0)),
        ),
        out_shape=jax.ShapeDtypeStruct((part, hid), F32),
        compiler_params=params(),
        name="mix_back_rest",
        cost_estimate=cost(12),
    )(half, dvh, dvl, uh, ul)


def hop_kernel(
    h, in_w, x_ref, wp_ref, st_ref, gain_ref, shift_ref, slope_ref, mslope_ref, dvh_ref, dvl_ref, mwh_ref, mwl_ref,
    j_ref, uh_ref, ul_ref,
    dx_ref, bw_ref, sums_ref,
):
    step = pl.program_id(0)
    n = wp_ref.shape[1] // 3
    hid = gain_ref.shape[1]

    @pl.when(step == 0)
    def _():
        bw_ref[...] = jnp.zeros_like(bw_ref)
        sums_ref[...] = jnp.zeros_like(sums_ref)

    a, b = scale_of(st_ref, slice(h * hid, (h + 1) * hid), gain_ref, shift_ref, h)
    s1 = slope_ref[h : h + 1, :]
    s2 = mslope_ref[h : h + 1, :]
    xall = stack3(hop_rows(x_ref, h, in_w))
    wp = wp_ref[0]
    r2 = 1.0 / (1.0 - s2)
    r1 = 1.0 / (1.0 - s1)
    wh, wl = split((wp[:n].astype(F32) + wp[2 * n :].astype(F32)) * a)
    whl = jnp.concatenate([wh, wl], axis=0)
    dot = functools.partial(lax.dot_general, preferred_element_type=F32)
    row = lambda t: jnp.sum(t, axis=0, keepdims=True)
    sums = [0.0] * 4
    tile = x_ref.shape[1]
    parts = [slice(k, k + SUB) for k in range(0, tile, SUB)]

    def products(rs):
        y = dot(xall[:, rs], wp, TN)
        return y, dot3((dvh_ref[rs, :], dvl_ref[rs, :]), (mwh_ref[...], mwl_ref[...]), NT)

    def middle(rs, z, du):
        y = z * a + b
        j = j_ref[rs, :]
        u = uh_ref[rs, :].astype(F32) + ul_ref[rs, :].astype(F32)
        dj = du * (1.0 - (1.0 - s2) * jnp.exp2((s2 * r2) * j - r2 * u))
        dy = dj * (1.0 - (1.0 - s1) * jnp.exp2((s1 * r1) * y - r1 * j))
        for q, t in enumerate((dy, dy * y, dj * (y - j), du * (j - u))):
            sums[q] = sums[q] + row(t)
        return split(dy)

    def results(rs, dys):
        dh, dl = dys
        xs = xall[: 2 * n, rs]
        both = dot(xs, dh, NN)
        bw_ref[...] += both[:n] + both[n:] + dot(xs[:n], dl, NN)
        both = dot(whl, dh, NT)
        dx_ref[:, rs] = both[:n] + both[n:] + dot(wh, dl, NT)

    now = products(parts[0])
    before = None
    for k, rs in enumerate(parts):
        ahead = products(parts[k + 1]) if k + 1 < len(parts) else None
        if before is not None:
            results(parts[k - 1], before)
        before = middle(rs, *now)
        now = ahead
    results(parts[-1], before)
    for q, f in enumerate((1.0, 1.0, r1, r2)):
        sums_ref[q : q + 1, :] += sums[q] * f

    @pl.when(step == pl.num_programs(0) - 1)
    def _():
        bw_ref[...] = bw_ref[...] * a


def hop_back(h, in_w, x, wp, st, gain, shift, slope, mslope, dvh, dvl, mwh, mwl, j, uh, ul, tile):
    width, rows = x.shape
    hid = dvh.shape[1]
    n = wp.shape[1] // 3
    by = lambda w, k=0: pl.BlockSpec((tile, w), lambda i: (i, k))
    block = lambda r: pl.BlockSpec((r, hid), lambda i: (h, 0))
    return pl.pallas_call(
        functools.partial(hop_kernel, h, in_w),
        grid=(rows // tile,),
        in_specs=[
            pl.BlockSpec((width, tile), lambda i: (0, i)),
            pl.BlockSpec((1, 3 * n, hid), lambda i: (h, 0, 0)),
            whole(st),
        ]
        + [whole(t) for t in (gain, shift, slope, mslope)]
        + [by(hid), by(hid), block(hid), block(hid)]
        + [by(hid, h)] * 3,
        out_specs=[
            pl.BlockSpec((n, tile), lambda i: (0, i)),
            pl.BlockSpec((n, hid), lambda i: (0, 0)),
            pl.BlockSpec((4, hid), lambda i: (0, 0)),
        ],
        out_shape=[
            jax.ShapeDtypeStruct((n, rows), F32),
            jax.ShapeDtypeStruct((n, hid), F32),
            jax.ShapeDtypeStruct((4, hid), F32),
        ],
        compiler_params=params(),
        name=f"hop_back_{h}",
        cost_estimate=cost(14),
    )(x, wp, st, gain, shift, slope, mslope, dvh, dvl, mwh, mwl, j, uh, ul)


def pack_rows(n, hops, misc, unit=1):
    base = hops * n
    gram_at = base + misc + 4 * hops
    used = gram_at + hops * n // 4
    return base, gram_at, -(-used // unit) * unit


def pack_kernel(g_ref, misc_ref, *refs):
    hops = g_ref.shape[0]
    n = g_ref.shape[1]
    out_ref = refs[-1]
    base, gram_at, _ = pack_rows(n, hops, misc_ref.shape[0])
    total = out_ref.shape[0]
    for h in range(hops):
        out_ref[h * n : (h + 1) * n, :] = refs[h][...]
        k = base + misc_ref.shape[0] + 4 * h
        out_ref[k : k + 4, :] = refs[hops + h][...]
        for q in range(4):
            k = gram_at + h * n // 4
            out_ref[k : k + n // 4, q * LANES : (q + 1) * LANES] = g_ref[h, q * n // 4 : (q + 1) * n // 4, :]
    out_ref[base : base + misc_ref.shape[0], :] = misc_ref[...]
    used = gram_at + hops * n // 4
    if used < total:
        out_ref[used:, :] = jnp.zeros((total - used, out_ref.shape[1]), F32)


def pack(g, misc, bws, sums, unit):
    hid = misc.shape[1]
    total = pack_rows(g.shape[1], g.shape[0], misc.shape[0], unit)[2]
    return pl.pallas_call(
        pack_kernel,
        out_shape=jax.ShapeDtypeStruct((total, hid), F32),
        compiler_params=params(),
        name="pack",
        cost_estimate=cost(3),
    )(g, misc, *bws, *sums)


def fix_kernel(in_w, classes, misc, valid_ref, x_ref, p_ref, st_ref, gain_ref, shift_ref, wp_ref, *refs):
    step = pl.program_id(0)
    hops, hid = gain_ref.shape
    tile = x_ref.shape[1]
    n = wp_ref.shape[1] // 3
    dxs, rest = refs[:hops], refs[hops:]
    dx_ref, bw_ref, gain_out, shift_out, slope_out, mslope_out, oslope_out, hw_out, hb_out, loss_out, q_ref = rest
    base, gram_at, _ = pack_rows(n, hops, misc)
    mask = row_mask(valid_ref, step, tile, 1)

    @pl.when(step == 0)
    def _():
        count = count_of(st_ref)
        hw_out[...] = p_ref[base : base + classes, :]
        hb_out[...] = p_ref[base + classes : base + classes + 1, :classes]
        loss_out[...] = p_ref[base + classes : base + classes + 1, LANES : LANES + 1] / count
        oslope_out[...] = p_ref[base + classes + 1 : base + classes + 2, :]
        for h in range(hops):
            cols = slice(h * hid, (h + 1) * hid)
            mean, rstd = norm_of(st_ref, cols)
            gain = gain_ref[h : h + 1, :]
            at = base + misc + 4 * h
            total = LOG2E * p_ref[at : at + 1, :]
            gsum = (p_ref[at + 1 : at + 2, :] - shift_ref[h : h + 1, :] * total) / gain
            gain_out[h : h + 1, :] = gsum
            shift_out[h : h + 1, :] = total
            slope_out[h : h + 1, :] = p_ref[at + 2 : at + 3, :]
            mslope_out[h : h + 1, :] = p_ref[at + 3 : at + 4, :]
            a = gain * rstd / count
            c2 = a * gsum * rstd
            k0 = a * total - mean * c2
            wh, wl = wp_ref[h, :n, :], wp_ref[h, 2 * n :, :]
            wc = (wh.astype(F32) + wl.astype(F32)) * c2
            mask_row = lax.broadcasted_iota(jnp.int32, (n, hid), 0) == in_w
            wc = split(jnp.where(mask_row, k0, wc))
            q_ref[h, :, :n] = dot3((wh, wl), wc, NT)
            k = gram_at + h * n // 4
            g = jnp.concatenate(
                [p_ref[k : k + n // 4, q * LANES : q * LANES + n] for q in range(4)], axis=0
            )
            bw = p_ref[h * n : (h + 1) * n, :] - dot3(split(g), wc)
            bw_ref[:, h, :] = bw[:in_w]

    for h in range(hops):
        x = jnp.where(mask, hop_rows(x_ref, h, in_w, 1.0), 0.0)
        fix = dot3(split(q_ref[h, :, :n]), split(x))
        dx_ref[h * in_w : (h + 1) * in_w, :] = (dxs[h][...] - fix)[:in_w]


def fix(valid, x, packed, st, gain, shift, wp, dxs, in_w, classes, misc, tile):
    width, rows = x.shape
    hops, hid = gain.shape
    n = wp.shape[1] // 3
    cols = lambda r: pl.BlockSpec((r, tile), lambda i: (0, i))
    shapes = ((in_w, hops, hid),) + ((hops, hid),) * 4 + ((1, hid), (classes, hid), (1, classes), (1, 1))
    return pl.pallas_call(
        functools.partial(fix_kernel, in_w, classes, misc),
        grid=(rows // tile,),
        in_specs=[whole(valid), cols(width)]
        + [whole(t) for t in (packed, st, gain, shift, wp)]
        + [cols(n)] * hops,
        out_specs=[cols(width)] + [pl.BlockSpec(s, lambda i, s=s: (0,) * len(s)) for s in shapes],
        out_shape=[jax.ShapeDtypeStruct(s, F32) for s in ((width, rows),) + shapes],
        scratch_shapes=[pltpu.VMEM((hops, n, LANES), F32)],
        compiler_params=params(),
        name="fix",
        cost_estimate=cost(8),
    )(valid, x, packed, st, gain, shift, wp, *dxs)


def flip(v, axis, size, k):
    return lax.ppermute(v, axis, [(i, i ^ k) for i in range(size)])


def sum_small(v, sizes):
    steps = []
    for axis, size in sizes.items():
        k = 1
        if axis == "dp" and size >= 2:
            steps.append((axis, size, 1, 2))
            k = 2
        while k < size:
            wide = 4 if 4 * k <= size else 2
            steps.append((axis, size, k, wide))
            k *= wide
    for axis, size, k, wide in steps:
        if wide == 2:
            v = v + flip(v, axis, size, k)
        else:
            p1, p2, p3 = (flip(v, axis, size, k * m) for m in (1, 2, 3))
            v = (v + p1) + (p2 + p3)
    return v


def sum_tiny(v, sizes):
    n = sizes["dp"] * sizes["bucket"]
    copies = jnp.broadcast_to(v[None], (n,) + v.shape)
    return jnp.sum(lax.all_to_all(copies, ("dp", "bucket"), 0, 0, tiled=True), axis=0)


def pieces(v, n):
    size = v.shape[0] // n
    return [v[i * size : (i + 1) * size] for i in range(n)]


def take(v, index, n):
    size = v.shape[0] // n
    return lax.dynamic_slice_in_dim(v, index * size, size, 0)


def halve(v, axis, size, k):
    bit = lax.axis_index(axis) // k % 2
    return take(v, bit, 2) + flip(take(v, 1 - bit, 2), axis, size, k)


def double(v, axis, size, k):
    bit = lax.axis_index(axis) // k % 2
    got = flip(v, axis, size, k)
    return jnp.where(bit == 0, jnp.concatenate([v, got], 0), jnp.concatenate([got, v], 0))


def scatter_line(v, axis, size):
    if size != 4:
        for i in range(size.bit_length() - 1):
            v = halve(v, axis, size, 1 << i)
        return v
    me = lax.axis_index(axis)
    p0, p1, p2, p3 = (flip(take(v, me ^ k, 4), axis, 4, k) if k else take(v, me, 4) for k in range(4))
    return (p0 + p1) + (p2 + p3)


def gather_line(v, axis, size):
    if size != 4:
        for i in reversed(range(size.bit_length() - 1)):
            v = double(v, axis, size, 1 << i)
        return v
    me = lax.axis_index(axis)
    out = jnp.zeros((4 * v.shape[0],) + v.shape[1:], v.dtype)
    for k in range(4):
        got = flip(v, axis, 4, k) if k else v
        out = lax.dynamic_update_slice_in_dim(out, got, (me ^ k) * v.shape[0], 0)
    return out


def sum_stages(sizes):
    dp, bucket = sizes["dp"], sizes["bucket"]
    across = [("dp", dp, 1 << i) for i in range(1, dp.bit_length() - 1)]
    stages = []
    if dp > 1:
        stages.append(lambda v: halve(v, "dp", dp, 1))
    for a, b in zip(across, across[::-1]):
        stages.append(lambda v, a=a, b=b: jnp.concatenate([halve(pieces(v, 2)[0], *a), halve(pieces(v, 2)[1], *b)], 0))
    stages.append(lambda v: scatter_line(v, "bucket", bucket))
    stages.append(lambda v: gather_line(v, "bucket", bucket))
    for a, b in zip(across[::-1], across):
        stages.append(lambda v, a=a, b=b: jnp.concatenate([double(pieces(v, 2)[0], *a), double(pieces(v, 2)[1], *b)], 0))
    if dp > 1:
        stages.append(lambda v: double(v, "dp", dp, 1))
    return stages


def sum_large(v, sizes):
    for stage in sum_stages(sizes):
        v = stage(v)
    return v


def per_device(sizes, feats, labels, valid, branch_w, branch_gain, branch_shift, branch_slope, mix_slope,
               mix_w, mix_gain, mix_shift, out_slope, head_w, head_bias):
    rows, width = feats.shape
    hops, in_w, hid = branch_w.shape
    classes = head_w.shape[1]
    mix = hops * hid
    valid = valid.reshape(rows // LANES, LANES)
    labels = labels.reshape(rows // LANES, LANES)
    mslope = mix_slope.reshape(hops, hid)
    row = lambda t: t.reshape(1, -1)
    x = feats.T

    g, st, wp = gram(valid, x, branch_w.transpose(1, 0, 2), TILES["gram"])
    st = sum_small(st, sizes)
    j, uh, ul, v, st2, mwh, mwl = forward(
        valid, x, wp, st, branch_gain, branch_shift, branch_slope, mslope, mix_w, in_w, TILES["forward"]
    )
    st2 = sum_tiny(st2, sizes)
    dy2, st3, misc = head(
        valid, labels, v, st2, st, row(mix_gain), row(mix_shift), row(out_slope), head_w.T, row(head_bias),
        TILES["head"],
    )
    st3 = sum_tiny(st3, sizes)
    core = lax.axis_index("dp") % 2
    half = lambda i: jnp.reshape(i, (1,)).astype(jnp.int32)
    away, dvh, dvl = mix_back(
        half(1 - core), valid, dy2, v, st2, st, st3, row(mix_gain), uh, ul, TILES["mix"]
    )
    got = flip(away, "dp", sizes["dp"], 1) if sizes["dp"] > 1 else None
    m = mix_back_rest(half(core), dvh, dvl, uh, ul, TILES["mix"])
    if got is None:
        m = jnp.concatenate([m, away], 0)
    else:
        m, got, x = lax.optimization_barrier((m, got, x))
        m = m + got
    stages = sum_stages(sizes)
    rest = list(stages)
    if got is not None:
        stages = stages[1:]
    per_stage = [[] for _ in range(HOP_STAGES)]
    for h in range(hops):
        per_stage[h * HOP_STAGES // hops].append(h)
    dxs, bws, sums = [], [], []
    for i, now in enumerate(per_stage):
        m, x, bws, sums = lax.optimization_barrier((m, x, bws, sums))
        if i < len(stages):
            m = stages[i](m)
        for h in now:
            dx, bw, s = hop_back(
                h, in_w, x, wp, st, branch_gain, branch_shift, branch_slope, mslope, dvh, dvl, mwh, mwl,
                j, uh, ul, TILES["hop"],
            )
            dxs, bws, sums = dxs + [dx], bws + [bw], sums + [s]
    packed = pack(g, misc, bws, sums, max(128, 2 * sizes["dp"] * sizes["bucket"]))
    for stage in stages[HOP_STAGES:]:
        m, packed = lax.optimization_barrier((m, packed))
        m = stage(m)
        for _ in range(PACK_STAGES):
            if rest:
                packed = rest.pop(0)(packed)
    for stage in rest:
        packed = stage(packed)
    m, packed = lax.optimization_barrier((m, packed))
    d_x, bw, gain_grad, shift_grad, slope_grad, mslope_grad, oslope_grad, hw_grad, hb_grad, loss = fix(
        valid, x, packed, st, branch_gain, branch_shift, wp, dxs, in_w, classes, misc.shape[0], TILES["fix"]
    )
    return (
        loss.reshape(()),
        d_x.T,
        bw.transpose(1, 0, 2),
        gain_grad,
        shift_grad,
        slope_grad,
        mslope_grad.reshape(mix),
        m,
        st3[1],
        st3[0],
        oslope_grad.reshape(hid),
        hw_grad.T,
        hb_grad.reshape(classes),
    )


def solution(mesh):
    sizes = {axis: mesh.shape[axis] for axis in ("dp", "bucket")}
    split_rows = P(("dp", "bucket"), None)
    in_specs = (split_rows, P(("dp", "bucket")), P(("dp", "bucket"))) + (P(),) * 11
    out_specs = (P(), split_rows) + (P(),) * 11
    return jax.shard_map(
        functools.partial(per_device, sizes),
        mesh=mesh,
        in_specs=in_specs,
        out_specs=out_specs,
        check_vma=False,
    )
```

```python
import functools

import jax
import jax.numpy as jnp
from jax import lax
from jax.experimental import pallas as pl
from jax.experimental.pallas import tpu as pltpu
from jax.sharding import PartitionSpec as P

EPS = 1e-05
F32 = jnp.float32
BF16 = jnp.bfloat16
LANES = 128
LOG2E = 1.4426950408889634
LN2 = 0.6931471805599453
TILES = {"gram": 2048, "forward": 512, "head": 512, "mix": 512, "hop": 512, "fix": 1024}
PACK_STEPS = 2
SUB = 256
MIX_SUB = 256
COLS = 512
NN = (((1,), (0,)), ((), ()))
NT = (((1,), (1,)), ((), ()))
TN = (((0,), (0,)), ((), ()))


def split(x):
    hi = x.astype(BF16)
    return hi, (x - hi.astype(F32)).astype(BF16)


def dot3(a, b, dims=NN):
    ah, al = a
    bh, bl = b
    dot = functools.partial(lax.dot_general, dimension_numbers=dims, preferred_element_type=F32)
    return dot(ah, bh) + (dot(ah, bl) + dot(al, bh))


def act2(y, slope, rest):
    return jnp.maximum(slope * y + rest * jnp.log(1.0 + jnp.exp2(jnp.minimum(y, 30.0))), y)


def cost(us):
    return pl.CostEstimate(flops=0, bytes_accessed=int(us * 3.69e6), transcendentals=0)


def params(mib):
    return pltpu.CompilerParams(vmem_limit_bytes=mib * 1024 * 1024)


def near(x):
    return pltpu.with_memory_space_constraint(x, pltpu.VMEM)


def far(x):
    return pltpu.with_memory_space_constraint(x, pltpu.HBM)


def whole(x, buffers=2):
    mode = {} if buffers == 2 else {"pipeline_mode": pl.Buffered(buffers)}
    return pl.BlockSpec(x.shape, lambda *_: (0,) * len(x.shape), **mode)


def row_mask(valid_ref, step, tile, axis=0):
    n = jnp.sum(valid_ref[...])
    shape = (tile, 1) if axis == 0 else (1, tile)
    return step * tile + lax.broadcasted_iota(jnp.int32, shape, axis) < n


def hop_rows(x_ref, h, in_w, extra=None):
    x = x_ref[h * in_w : (h + 1) * in_w, :]
    pad = -(-(in_w + 1) // 16) * 16 - in_w
    tail = jnp.zeros((pad, x.shape[1]), F32)
    if extra is not None:
        first = lax.broadcasted_iota(jnp.int32, tail.shape, 0) == 0
        tail = jnp.where(first, extra, 0.0)
    return jnp.concatenate([x, tail], axis=0)


def stack3(a):
    hi, lo = split(a)
    return jnp.concatenate([hi, lo, hi], axis=0)


def gram_kernel(in_w, valid_ref, x_ref, w_ref, g_ref, st_ref, wp_ref):
    step = pl.program_id(0)
    tile = x_ref.shape[1]
    hops, hid = w_ref.shape[1:]
    mask = row_mask(valid_ref, step, tile, 1)

    @pl.when(step == 0)
    def _():
        g_ref[...] = jnp.zeros_like(g_ref)

    for h in range(hops):
        x = jnp.where(mask, hop_rows(x_ref, h, in_w, 1.0), 0.0)
        hi, lo = split(x)
        n = x.shape[0]
        dot = functools.partial(lax.dot_general, dimension_numbers=NT, preferred_element_type=F32)
        cross = dot(hi, lo)
        g_ref[h, :, :n] += dot(hi, hi) + (cross + cross.T)

    @pl.when(step == pl.num_programs(0) - 1)
    def _():
        for h in range(hops):
            n = g_ref.shape[1]
            w = w_ref[:, h, :]
            w = jnp.concatenate([w, jnp.zeros((n - in_w, hid), F32)], axis=0)
            ws = split(w)
            g = g_ref[h, :, :n]
            gw = dot3(split(g), ws)
            cols = slice(h * hid, (h + 1) * hid)
            st_ref[0:1, cols] = gw[in_w : in_w + 1, :]
            st_ref[1:2, cols] = jnp.sum(w * gw, axis=0, keepdims=True)
            wp_ref[h] = jnp.concatenate([ws[0], ws[0], ws[1]], axis=0)
        st_ref[:, hops * hid :] = jnp.broadcast_to(g_ref[0, in_w : in_w + 1, in_w : in_w + 1], (2, LANES))


def gram(valid, x, w, tile):
    width, rows = x.shape
    in_w, hops, hid = w.shape
    n = -(-(in_w + 1) // 16) * 16
    shapes = (hops, n, LANES), (2, hops * hid + LANES), (hops, 3 * n, hid)
    return pl.pallas_call(
        functools.partial(gram_kernel, in_w),
        grid=(rows // tile,),
        in_specs=[whole(valid), pl.BlockSpec((width, tile), lambda i: (0, i)), whole(w)],
        out_specs=[pl.BlockSpec(s, lambda i, s=s: (0,) * len(s)) for s in shapes],
        out_shape=[jax.ShapeDtypeStruct(s, F32) for s in shapes[:2]] + [pltpu.HBM(shapes[2], BF16)],
        compiler_params=params(32),
        name="gram",
        cost_estimate=cost(5),
    )(valid, far(x), w)


def count_of(st_ref):
    return st_ref[0:1, st_ref.shape[1] - 1 :]


def norm_of(st_ref, cols):
    count = count_of(st_ref)
    mean = st_ref[0:1, cols] / count
    var = st_ref[1:2, cols] / count - mean * mean
    return mean, lax.rsqrt(var + EPS)


def scale_of(st_ref, cols, gain_ref, shift_ref, h):
    mean, rstd = norm_of(st_ref, cols)
    a = gain_ref[h : h + 1, :] * rstd
    return LOG2E * a, LOG2E * (shift_ref[h : h + 1, :] - mean * a)


def forward_kernel(
    in_w, valid_ref, x_ref, wp_ref, st_ref, gain_ref, shift_ref, slope_ref, mslope_ref, w_ref,
    j_ref, uh_ref, ul_ref, v_ref, copies_ref, wh_ref, wl_ref, st2_ref,
):
    step = pl.program_id(0)
    tile = x_ref.shape[1]
    hops, hid = gain_ref.shape
    mask = row_mask(valid_ref, step, tile)

    @pl.when(step == 0)
    def _():
        st2_ref[...] = jnp.zeros_like(st2_ref)
        for h in range(hops):
            rows = slice(h * hid, (h + 1) * hid)
            wh_ref[rows, :], wl_ref[rows, :] = split(w_ref[rows, :])

    dot = functools.partial(lax.dot_general, preferred_element_type=F32)
    chunks = [(h, c) for h in range(hops) for c in range(0, hid, COLS)]
    scales, xs = {}, {}

    def project(i):
        h, c = chunks[i]
        if h not in xs:
            xs[h] = stack3(hop_rows(x_ref, h, in_w))
        return dot(xs[h], wp_ref[h, :, c : c + COLS], TN)

    def activate(i, z):
        h, c = chunks[i]
        if h not in scales:
            scales[h] = scale_of(st_ref, slice(h * hid, (h + 1) * hid), gain_ref, shift_ref, h)
        part = slice(c, c + COLS)
        cols = slice(h * hid + c, h * hid + c + COLS)
        a, b = (t[:, part] for t in scales[h])
        s1 = slope_ref[h : h + 1, part]
        s2 = mslope_ref[h : h + 1, part]
        j = act2(z * a + b, s1, LOG2E * (1.0 - s1))
        u = act2(j, s2, LOG2E * (1.0 - s2))
        j_ref[:, cols] = j
        us = split(u)
        uh_ref[:, cols], ul_ref[:, cols] = us
        return us

    def mix(i, us):
        h, c = chunks[i]
        cols = slice(h * hid + c, h * hid + c + COLS)
        part = dot3(us, (wh_ref[cols, :], wl_ref[cols, :]))
        v_ref[...] = part if i == 0 else v_ref[...] + part

    z = project(0)
    before = None
    for i in range(len(chunks)):
        ahead = project(i + 1) if i + 1 < len(chunks) else None
        if before is not None:
            mix(i - 1, before)
        before = activate(i, z)
        z = ahead
    mix(len(chunks) - 1, before)
    v = v_ref[...]
    v = LN2 * v
    v_ref[...] = v
    vm = jnp.where(mask, v, 0.0)
    st2_ref[0:1, :] += jnp.sum(vm, axis=0, keepdims=True)
    st2_ref[1:2, :] += jnp.sum(vm * vm, axis=0, keepdims=True)

    @pl.when(step == pl.num_programs(0) - 1)
    def _():
        copies_ref[...] = jnp.broadcast_to(st2_ref[...][None], copies_ref.shape)


def forward(valid, x, wp, st, gain, shift, slope, mslope, w, in_w, copies, tile):
    width, rows = x.shape
    mix, hid = w.shape
    by = lambda n: pl.BlockSpec((tile, n), lambda i: (i, 0))
    return pl.pallas_call(
        functools.partial(forward_kernel, in_w),
        grid=(rows // tile,),
        in_specs=[whole(valid), pl.BlockSpec((width, tile), lambda i: (0, i))]
        + [whole(t, 1) for t in (wp, st, gain, shift, slope, mslope, w)],
        out_specs=[by(mix), by(mix), by(mix), by(hid), pl.BlockSpec((copies, 2, hid), lambda i: (0, 0, 0))]
        + [pl.BlockSpec((mix, hid), lambda i: (0, 0), pipeline_mode=pl.Buffered(1))] * 2,
        out_shape=[
            pltpu.HBM((rows, mix), F32),
            pltpu.HBM((rows, mix), BF16),
            pltpu.HBM((rows, mix), BF16),
            pltpu.HBM((rows, hid), F32),
            jax.ShapeDtypeStruct((copies, 2, hid), F32),
            pltpu.HBM((mix, hid), BF16),
            pltpu.HBM((mix, hid), BF16),
        ],
        scratch_shapes=[pltpu.VMEM((2, hid), F32)],
        compiler_params=params(43),
        name="forward",
        cost_estimate=cost(30),
    )(valid, far(x), far(wp), st, gain, shift, slope, mslope, far(w))


def as_column(row):
    n = row.shape[1]
    same = lax.broadcasted_iota(jnp.int32, (n, n), 0) == lax.broadcasted_iota(jnp.int32, (n, n), 1)
    return jnp.sum(jnp.where(same, jnp.broadcast_to(row, (n, n)), 0.0), axis=1, keepdims=True)


def as_row(col):
    n = col.shape[0]
    same = lax.broadcasted_iota(jnp.int32, (n, n), 0) == lax.broadcasted_iota(jnp.int32, (n, n), 1)
    return jnp.sum(jnp.where(same, jnp.broadcast_to(col, (n, n)), 0.0), axis=0, keepdims=True)


def head_kernel(
    valid_ref, labels_ref, v_ref, st_ref, cnt_ref, gain_ref, shift_ref, slope_ref, hw_ref, hb_ref,
    dy_ref, copies_ref, misc_ref, st3_ref,
):
    step = pl.program_id(0)
    tile, hid = v_ref.shape
    classes = hw_ref.shape[0]
    padded = -(-classes // 16) * 16
    mask = row_mask(valid_ref, step, tile, 1)
    count = count_of(cnt_ref)

    @pl.when(step == 0)
    def _():
        st3_ref[...] = jnp.zeros_like(st3_ref)
        misc_ref[...] = jnp.zeros_like(misc_ref)

    sums = jnp.sum(st_ref[...], axis=0)
    mean = sums[0:1, :] / count
    rstd = lax.rsqrt(sums[1:2, :] / count - mean * mean + EPS)
    s = slope_ref[...]
    zn = (v_ref[...] - mean) * rstd
    y = gain_ref[...] * zn + shift_ref[...]
    e1 = 1.0 + jnp.exp(jnp.minimum(y, 20.0))
    sp = jnp.maximum(jnp.log(e1), y)
    w = s * y + (1.0 - s) * sp
    ws = split(w)
    hw = hw_ref[...]
    if padded > classes:
        hw = jnp.concatenate([hw, jnp.zeros((padded - classes, hid), F32)], axis=0)
    hh, hl = split(hw)
    dot = functools.partial(lax.dot_general, dimension_numbers=NT, preferred_element_type=F32)
    both = dot(jnp.concatenate([hh, hl], axis=0), ws[0])
    logits = both[:padded] + both[padded:] + dot(hh, ws[1])
    logits = logits[:classes] + as_column(hb_ref[...])
    peak = jnp.max(logits, axis=0, keepdims=True)
    ex = jnp.exp(logits - peak)
    tot = jnp.sum(ex, axis=0, keepdims=True)
    per = tile // LANES
    lab = jnp.concatenate([labels_ref[pl.ds(step * per + k, 1), :] for k in range(per)], axis=1)
    hit = lab == lax.broadcasted_iota(jnp.int32, (classes, tile), 0)
    picked = jnp.sum(jnp.where(hit, logits, 0.0), axis=0, keepdims=True)
    loss = jnp.sum(jnp.where(mask, peak + jnp.log(tot) - picked, 0.0))
    dl = jnp.where(mask, (ex / tot - hit.astype(F32)) / count, 0.0)
    bias = as_row(jnp.sum(dl, axis=1, keepdims=True))
    if padded > classes:
        dl = jnp.concatenate([dl, jnp.zeros((padded - classes, tile), F32)], axis=0)
    dh, dlo = split(dl)
    dot = functools.partial(lax.dot_general, dimension_numbers=NN, preferred_element_type=F32)
    both = dot(jnp.concatenate([dh, dlo], axis=0), ws[0])
    hwg = both[:padded] + both[padded:] + dot(dh, ws[1])
    misc_ref[0:classes, :] += hwg[:classes]
    misc_ref[classes : classes + 1, 0:classes] += bias
    misc_ref[classes : classes + 1, LANES : 2 * LANES] += jnp.broadcast_to(loss, (1, LANES))
    dw = lax.dot_general(
        jnp.concatenate([dh, dlo, dh], axis=0),
        jnp.concatenate([hh, hh, hl], axis=0),
        TN,
        preferred_element_type=F32,
    )
    dy = dw * (1.0 - (1.0 - s) / e1)
    dy_ref[...] = dy
    row = lambda t: jnp.sum(t, axis=0, keepdims=True)
    misc_ref[classes + 1 : classes + 2, :] += row(dw * (y - sp))
    st3_ref[0:1, :] += row(dy)
    st3_ref[1:2, :] += row(dy * zn)

    @pl.when(step == pl.num_programs(0) - 1)
    def _():
        copies_ref[...] = jnp.broadcast_to(st3_ref[...][None], copies_ref.shape)


def head(valid, labels, v, st2, st, gain, shift, slope, hw, hb, tile):
    rows, hid = v.shape
    by = lambda n: pl.BlockSpec((tile, n), lambda i: (i, 0))
    misc = -(-(hw.shape[0] + 2) // 8) * 8
    return pl.pallas_call(
        head_kernel,
        grid=(rows // tile,),
        in_specs=[whole(valid), whole(labels), by(hid)]
        + [whole(t) for t in (st2, st, gain, shift, slope, hw, hb)],
        out_specs=[
            by(hid),
            whole(st2),
            pl.BlockSpec((misc, hid), lambda i: (0, 0)),
        ],
        out_shape=[
            pltpu.HBM((rows, hid), F32),
            jax.ShapeDtypeStruct(st2.shape, F32),
            jax.ShapeDtypeStruct((misc, hid), F32),
        ],
        scratch_shapes=[pltpu.VMEM((2, hid), F32)],
        compiler_params=params(24),
        name="head",
        cost_estimate=cost(9),
    )(valid, labels, far(v), st2, st, gain, shift, slope, hw, hb)


def mix_product(parts, uh_ref, ul_ref, m_ref):
    @pl.when(pl.program_id(0) == 0)
    def _():
        m_ref[...] = jnp.zeros_like(m_ref)

    ahead = parts[0][1]()
    for k, (rows, _) in enumerate(parts):
        dvs = ahead
        if k + 1 < len(parts):
            ahead = parts[k + 1][1]()
        hid = dvs[0].shape[1]
        for h in range(uh_ref.shape[1] // hid):
            cols = slice(h * hid, (h + 1) * hid)
            m_ref[cols, :] += dot3((uh_ref[rows, cols], ul_ref[rows, cols]), dvs, TN)


def mix_first_kernel(
    half_ref, valid_ref, dy_ref, v_ref, st2_ref, cnt_ref, st3_ref, gain_ref, uh_ref, ul_ref,
    m_ref, dvh_ref, dvl_ref, st3_out,
):
    step = pl.program_id(0)
    tile = dy_ref.shape[0]
    mask = row_mask(valid_ref, step, tile)
    count = count_of(cnt_ref)
    st2 = jnp.sum(st2_ref[...], axis=0)
    st3 = jnp.sum(st3_ref[...], axis=0)
    mean = st2[0:1, :] / count
    rstd = lax.rsqrt(st2[1:2, :] / count - mean * mean + EPS)
    a = LN2 * gain_ref[...] * rstd
    c1 = a * st3[0:1, :] / count
    c2 = a * st3[1:2, :] / count

    @pl.when(step == 0)
    def _():
        st3_out[...] = st3

    def dv(rows):
        zn = (v_ref[rows, :] - mean) * rstd
        dvs = split(jnp.where(mask[rows], a * dy_ref[rows, :] - (c1 + zn * c2), 0.0))
        dvh_ref[rows, :], dvl_ref[rows, :] = dvs
        return dvs

    parts = [slice(k, k + MIX_SUB) for k in range(0, tile, MIX_SUB)]
    mix_product([(rows, functools.partial(dv, rows)) for rows in parts], uh_ref, ul_ref, m_ref)


def mix_second_kernel(half_ref, dvh_ref, dvl_ref, uh_ref, ul_ref, m_ref):
    mix_product([(slice(None), lambda: (dvh_ref[...], dvl_ref[...]))], uh_ref, ul_ref, m_ref)


def mix_back(half, valid, dy, v, st2, st, st3, gain, uh, ul, tile):
    rows, hid = dy.shape
    part = uh.shape[1] // 2
    by = lambda n: pl.BlockSpec((tile, n), lambda i, half: (i, 0))
    return pl.pallas_call(
        mix_first_kernel,
        grid_spec=pltpu.PrefetchScalarGridSpec(
            num_scalar_prefetch=1,
            grid=(rows // tile,),
            in_specs=[whole(valid), by(hid), by(hid)]
            + [whole(t) for t in (st2, st, st3, gain)]
            + [pl.BlockSpec((tile, part), lambda i, half: (i, half[0]))] * 2,
            out_specs=[pl.BlockSpec((part, hid), lambda i, half: (0, 0)), by(hid), by(hid)]
            + [pl.BlockSpec((2, hid), lambda i, half: (0, 0))],
        ),
        out_shape=[
            jax.ShapeDtypeStruct((part, hid), F32),
            pltpu.HBM((rows, hid), BF16),
            pltpu.HBM((rows, hid), BF16),
            jax.ShapeDtypeStruct((2, hid), F32),
        ],
        compiler_params=params(28),
        name="mix_back",
        cost_estimate=cost(14),
    )(half, valid, far(dy), far(v), st2, st, st3, gain, far(uh), far(ul))


def mix_back_rest(half, dvh, dvl, uh, ul, tile):
    rows, hid = dvh.shape
    part = uh.shape[1] // 2
    by = lambda n: pl.BlockSpec((tile, n), lambda i, half: (i, 0))
    return pl.pallas_call(
        mix_second_kernel,
        grid_spec=pltpu.PrefetchScalarGridSpec(
            num_scalar_prefetch=1,
            grid=(rows // tile,),
            in_specs=[by(hid), by(hid)]
            + [pl.BlockSpec((tile, part), lambda i, half: (i, half[0]))] * 2,
            out_specs=pl.BlockSpec((part, hid), lambda i, half: (0, 0)),
        ),
        out_shape=jax.ShapeDtypeStruct((part, hid), F32),
        compiler_params=params(28),
        name="mix_back_rest",
        cost_estimate=cost(12),
    )(half, far(dvh), far(dvl), far(uh), far(ul))


def hop_kernel(
    h, in_w, x_ref, wp_ref, st_ref, gain_ref, shift_ref, slope_ref, mslope_ref, dvh_ref, dvl_ref, mwh_ref, mwl_ref,
    j_ref,
    dx_ref, bw_ref, sums_ref,
):
    step = pl.program_id(0)
    n = wp_ref.shape[1] // 3
    hid = gain_ref.shape[1]
    tile = x_ref.shape[1]

    @pl.when(step == 0)
    def _():
        bw_ref[...] = jnp.zeros_like(bw_ref)
        sums_ref[...] = jnp.zeros_like(sums_ref)

    a, b = scale_of(st_ref, slice(h * hid, (h + 1) * hid), gain_ref, shift_ref, h)
    s1 = slope_ref[h : h + 1, :]
    s2 = mslope_ref[h : h + 1, :]
    xall = stack3(hop_rows(x_ref, h, in_w, 1.0))
    wp = wp_ref[0]
    wh, wl = split((wp[:n].astype(F32) + wp[2 * n :].astype(F32)) * a)
    whl = jnp.concatenate([wh, wl], axis=0)
    dot = functools.partial(lax.dot_general, preferred_element_type=F32)
    row = lambda t: jnp.sum(t, axis=0, keepdims=True)
    sums = [0.0] * 2
    parts = [slice(k, k + SUB) for k in range(0, tile, SUB)]

    def products(rs):
        y = dot(xall[:, rs], wp, TN)
        return y, dot3((dvh_ref[rs, :], dvl_ref[rs, :]), (mwh_ref[...], mwl_ref[...]), NT)

    def middle(rs, z, du):
        y = z * a + b
        j = j_ref[rs, :]
        dj = du * (1.0 - (1.0 - s2) / (1.0 + jnp.exp2(j)))
        dy = dj * (1.0 - (1.0 - s1) / (1.0 + jnp.exp2(y)))
        for q, t in enumerate((dj * (y - j), du * j)):
            sums[q] = sums[q] + row(t)
        return split(dy)

    def results(rs, dys):
        dh, dl = dys
        xs = xall[: 2 * n, rs]
        both = dot(xs, dh, NN)
        bw_ref[...] += both[:n] + both[n:] + dot(xs[:n], dl, NN)
        both = dot(whl, dh, NT)
        dx_ref[:, rs] = both[:n] + both[n:] + dot(wh, dl, NT)

    now = products(parts[0])
    before = None
    for k, rs in enumerate(parts):
        ahead = products(parts[k + 1]) if k + 1 < len(parts) else None
        if before is not None:
            results(parts[k - 1], before)
        before = middle(rs, *now)
        now = ahead
    results(parts[-1], before)
    for q in range(2):
        sums_ref[q : q + 1, :] += sums[q]


def hop_back(h, in_w, x, wp, st, gain, shift, slope, mslope, dvh, dvl, mwh, mwl, j, tile):
    width, rows = x.shape
    hid = dvh.shape[1]
    n = wp.shape[1] // 3
    by = lambda w, k=0: pl.BlockSpec((tile, w), lambda i: (i, k))
    block = lambda r: pl.BlockSpec((r, hid), lambda i: (h, 0))
    return pl.pallas_call(
        functools.partial(hop_kernel, h, in_w),
        grid=(rows // tile,),
        in_specs=[
            pl.BlockSpec((width, tile), lambda i: (0, i)),
            pl.BlockSpec((1, 3 * n, hid), lambda i: (h, 0, 0)),
        ]
        + [whole(t) for t in (st, gain, shift, slope, mslope)]
        + [by(hid), by(hid), block(hid), block(hid), by(hid, h)],
        out_specs=[
            pl.BlockSpec((n, tile), lambda i: (0, i)),
            pl.BlockSpec((n, hid), lambda i: (0, 0)),
            pl.BlockSpec((2, hid), lambda i: (0, 0)),
        ],
        out_shape=[
            pltpu.HBM((n, rows), F32),
            jax.ShapeDtypeStruct((n, hid), F32),
            jax.ShapeDtypeStruct((2, hid), F32),
        ],
        compiler_params=params(20),
        name=f"hop_back_{h}",
        cost_estimate=cost(11),
    )(far(x), far(wp), st, gain, shift, slope, mslope, far(dvh), far(dvl), far(mwh), far(mwl), far(j))


def assemble_kernel(first_ref, own_ref, got_ref, w_ref, m_ref, uu_ref):
    mine = (pl.program_id(0) // 2) == first_ref[0]
    m = jnp.where(mine, own_ref[...], got_ref[...])
    m_ref[...] = m
    ones = jnp.ones((8, m.shape[1]), BF16)
    dot = functools.partial(lax.dot_general, dimension_numbers=NT, preferred_element_type=F32)
    hi, lo = split(m * w_ref[...])
    uu_ref[0] = dot(ones, hi) + dot(ones, lo)


def assemble(first, own, got, w):
    rows, hid = w.shape
    block = rows // 4
    half = pl.BlockSpec((block, hid), lambda i, first: (i % 2, 0))
    by = pl.BlockSpec((block, hid), lambda i, first: (i, 0))
    return pl.pallas_call(
        assemble_kernel,
        grid_spec=pltpu.PrefetchScalarGridSpec(
            num_scalar_prefetch=1,
            grid=(4,),
            in_specs=[half, half, by],
            out_specs=[by, pl.BlockSpec((1, 8, block), lambda i, first: (i, 0, 0))],
        ),
        out_shape=[jax.ShapeDtypeStruct((rows, hid), F32), jax.ShapeDtypeStruct((4, 8, block), F32)],
        compiler_params=params(20),
        name="assemble",
        cost_estimate=cost(5),
    )(first, own, got, far(w))


def pack_rows(n, hops, misc, unit=1):
    base = hops * n
    gram_at = base + misc + 2 * hops
    used = gram_at + hops * n // 4
    return base, gram_at, -(-used // unit) * unit


def pack_kernel(g_ref, misc_ref, *refs):
    hops = g_ref.shape[0]
    n = g_ref.shape[1]
    out_ref = refs[-1]
    base, gram_at, _ = pack_rows(n, hops, misc_ref.shape[0])
    total = out_ref.shape[0]
    for h in range(hops):
        out_ref[h * n : (h + 1) * n, :] = refs[h][...]
        k = base + misc_ref.shape[0] + 2 * h
        out_ref[k : k + 2, :] = refs[hops + h][...]
        for q in range(4):
            k = gram_at + h * n // 4
            out_ref[k : k + n // 4, q * LANES : (q + 1) * LANES] = g_ref[h, q * n // 4 : (q + 1) * n // 4, :]
    out_ref[base : base + misc_ref.shape[0], :] = misc_ref[...]
    used = gram_at + hops * n // 4
    if used < total:
        out_ref[used:, :] = jnp.zeros((total - used, out_ref.shape[1]), F32)


def pack(g, misc, bws, sums, unit):
    hid = misc.shape[1]
    total = pack_rows(g.shape[1], g.shape[0], misc.shape[0], unit)[2]
    return pl.pallas_call(
        pack_kernel,
        out_shape=jax.ShapeDtypeStruct((total, hid), F32),
        compiler_params=params(24),
        name="pack",
        cost_estimate=cost(3),
    )(g, misc, *bws, *sums)


def fix_kernel(in_w, classes, misc, valid_ref, x_ref, p_ref, uu_ref, st_ref, gain_ref, slope_ref, mslope_ref, wp_ref, *refs):
    step = pl.program_id(0)
    hops, hid = gain_ref.shape
    tile = x_ref.shape[1]
    n = wp_ref.shape[1] // 3
    dxs, rest = refs[:hops], refs[hops:]
    dx_ref, bw_ref, gain_out, shift_out, slope_out, mslope_out, oslope_out, hw_out, hb_out, loss_out, q_ref = rest
    base, gram_at, _ = pack_rows(n, hops, misc)
    mask = row_mask(valid_ref, step, tile, 1)

    @pl.when(step == 0)
    def _():
        count = count_of(st_ref)
        hw_out[...] = p_ref[base : base + classes, :]
        hb_out[...] = p_ref[base + classes : base + classes + 1, :classes]
        loss_out[...] = p_ref[base + classes : base + classes + 1, LANES : LANES + 1] / count
        oslope_out[...] = p_ref[base + classes + 1 : base + classes + 2, :]
        for h in range(hops):
            cols = slice(h * hid, (h + 1) * hid)
            mean, rstd = norm_of(st_ref, cols)
            gain = gain_ref[h : h + 1, :]
            wh, wl = wp_ref[h, :n, :], wp_ref[h, 2 * n :, :]
            w = wh.astype(F32) + wl.astype(F32)
            raw = p_ref[h * n : (h + 1) * n, :]
            total = LOG2E * raw[in_w : in_w + 1, :]
            gsum = rstd * (LOG2E * jnp.sum(w * raw, axis=0, keepdims=True) - mean * total)
            gain_out[h : h + 1, :] = gsum
            shift_out[h : h + 1, :] = total
            at = base + misc + 2 * h
            slope_out[h : h + 1, :] = p_ref[at : at + 1, :] / (1.0 - slope_ref[h : h + 1, :])
            uu = uu_ref[h, 0:1, :]
            mslope_out[h : h + 1, :] = (p_ref[at + 1 : at + 2, :] - uu) / (1.0 - mslope_ref[h : h + 1, :])
            a = gain * rstd / count
            c2 = a * gsum * rstd
            k0 = a * total - mean * c2
            wc = w * c2
            mask_row = lax.broadcasted_iota(jnp.int32, (n, hid), 0) == in_w
            wc = split(jnp.where(mask_row, k0, wc))
            q_ref[h, :, :n] = dot3((wh, wl), wc, NT)
            k = gram_at + h * n // 4
            g = jnp.concatenate(
                [p_ref[k : k + n // 4, q * LANES : q * LANES + n] for q in range(4)], axis=0
            )
            bw = raw * (LOG2E * gain * rstd) - dot3(split(g), wc)
            bw_ref[:, h, :] = bw[:in_w]

    for h in range(hops):
        x = jnp.where(mask, hop_rows(x_ref, h, in_w, 1.0), 0.0)
        fix = dot3(split(q_ref[h, :, :n]), split(x))
        dx_ref[h * in_w : (h + 1) * in_w, :] = (dxs[h][...] - fix)[:in_w]


def fix(valid, x, packed, uu, st, gain, slope, mslope, wp, dxs, in_w, classes, misc, tile):
    width, rows = x.shape
    hops, hid = gain.shape
    n = wp.shape[1] // 3
    cols = lambda r: pl.BlockSpec((r, tile), lambda i: (0, i))
    shapes = ((in_w, hops, hid),) + ((hops, hid),) * 4 + ((1, hid), (classes, hid), (1, classes), (1, 1))
    return pl.pallas_call(
        functools.partial(fix_kernel, in_w, classes, misc),
        grid=(rows // tile,),
        in_specs=[whole(valid), cols(width)]
        + [whole(t) for t in (packed, uu, st, gain, slope, mslope, wp)]
        + [cols(n)] * hops,
        out_specs=[cols(width)] + [pl.BlockSpec(s, lambda i, s=s: (0,) * len(s)) for s in shapes],
        out_shape=[jax.ShapeDtypeStruct(s, F32) for s in ((width, rows),) + shapes],
        scratch_shapes=[pltpu.VMEM((hops, n, LANES), F32)],
        compiler_params=params(24),
        name="fix",
        cost_estimate=cost(8),
    )(valid, far(x), packed, uu, st, gain, slope, mslope, far(wp), *[far(d) for d in dxs])


def flip(v, axis, size, k):
    return lax.ppermute(v, axis, [(i, i ^ k) for i in range(size)])


def sum_small(v, sizes):
    steps = []
    for axis, size in sizes.items():
        k = 1
        if axis == "dp" and size >= 2:
            steps.append((axis, size, 1, 2))
            k = 2
        while k < size:
            wide = 4 if 4 * k <= size else 2
            steps.append((axis, size, k, wide))
            k *= wide
    for axis, size, k, wide in steps:
        if wide == 2:
            v = v + flip(v, axis, size, k)
        else:
            p1, p2, p3 = (flip(v, axis, size, k * m) for m in (1, 2, 3))
            v = (v + p1) + (p2 + p3)
    return v


def exchange(copies):
    return lax.all_to_all(copies, ("dp", "bucket"), 0, 0, tiled=True)


def pieces(v, n):
    size = v.shape[0] // n
    return [v[i * size : (i + 1) * size] for i in range(n)]


def take(v, index, n):
    size = v.shape[0] // n
    return lax.dynamic_slice_in_dim(v, index * size, size, 0)


def merge(v, got, axis, size, k):
    bit = lax.axis_index(axis) // k % 2
    return jnp.where(bit == 0, jnp.concatenate([v, got], 0), jnp.concatenate([got, v], 0))


def halve(parts, axis, size, k):
    bit = lax.axis_index(axis) // k % 2
    part = lambda i: functools.reduce(jnp.add, [take(p, i, 2) for p in parts])
    return part(bit), flip(part(1 - bit), axis, size, k)


def spread(v, axis, size, k):
    me = lax.axis_index(axis) // k
    return tuple(flip(take(v, me ^ i, 4), axis, size, k * i) if i else take(v, me, 4) for i in range(4))


def collect(v, axis, size, k):
    return (v,) + tuple(flip(v, axis, size, k * i) for i in range(1, 4))


def in_order(parts, axis, k):
    low, high = lax.axis_index(axis) // k % 2, lax.axis_index(axis) // (2 * k) % 2
    pair = lambda a, b: jnp.where(low == 0, jnp.concatenate([a, b], 0), jnp.concatenate([b, a], 0))
    near, far = pair(parts[0], parts[1]), pair(parts[2], parts[3])
    return jnp.where(high == 0, jnp.concatenate([near, far], 0), jnp.concatenate([far, near], 0))


def total(parts):
    if len(parts) == 4:
        return (parts[0] + parts[1]) + (parts[2] + parts[3])
    return functools.reduce(jnp.add, parts)


def sum_steps(parts, sizes, large, within):
    dp, bucket = sizes["dp"], sizes["bucket"]
    across = [("dp", dp, 1 << i) for i in range(1, dp.bit_length() - 1)]
    square = len(across) == 2 and not large
    line = [("bucket", bucket, 1 << i) for i in range(bucket.bit_length() - 1)]
    core = ("dp", dp, 1)
    within = within and dp > 1
    if within:
        parts = yield halve(parts, *core)
    if square:
        parts = yield spread(total(parts), "dp", dp, 2)
    elif across:
        top, bottom = ([pieces(p, 2)[i] for p in parts] for i in range(2))
        for a, b in zip(across, across[::-1]):
            top, bottom = yield halve(top, *a), halve(bottom, *b)
        parts = [jnp.concatenate([total(top), total(bottom)], 0)]
    if bucket == 4:
        parts = yield spread(total(parts), "bucket", bucket, 1)
        parts = yield collect(total(parts), "bucket", bucket, 1)
        v = in_order(parts, "bucket", 1)
    else:
        for s in line:
            parts = yield halve(parts, *s)
        v = total(parts)
        for s in line[::-1]:
            parts = yield v, flip(v, *s)
            v = merge(*parts, *s)
    if square:
        v = in_order((yield collect(v, "dp", dp, 2)), "dp", 2)
    elif across:
        top, bottom = pieces(v, 2)
        for a, b in zip(across[::-1], across):
            got = yield top, flip(top, *a), bottom, flip(bottom, *b)
            top, bottom = merge(*got[:2], *a), merge(*got[2:], *b)
        v = jnp.concatenate([top, bottom], 0)
    if within:
        v = merge(*(yield v, flip(v, *core)), *core)
    return v


class Steps:
    def __init__(self, steps):
        self.steps, self.state, self.done, self.value = steps, None, False, None

    def step(self):
        if not self.done:
            try:
                self.state = self.steps.send(self.state)
            except StopIteration as end:
                self.done, self.value, self.state = True, end.value, None


def per_device(sizes, feats, labels, valid, branch_w, branch_gain, branch_shift, branch_slope, mix_slope,
               mix_w, mix_gain, mix_shift, out_slope, head_w, head_bias):
    rows, width = feats.shape
    hops, in_w, hid = branch_w.shape
    classes = head_w.shape[1]
    mix = hops * hid
    valid = valid.reshape(rows // LANES, LANES)
    labels = labels.reshape(rows // LANES, LANES)
    mslope = mix_slope.reshape(hops, hid)
    row = lambda t: t.reshape(1, -1)
    x = feats.T

    g, st, wp = gram(valid, x, branch_w.transpose(1, 0, 2), TILES["gram"])
    st = sum_small(st, sizes)
    j, uh, ul, v, st2, mwh, mwl = forward(
        valid, x, wp, st, branch_gain, branch_shift, branch_slope, mslope, mix_w, in_w,
        sizes["dp"] * sizes["bucket"], TILES["forward"],
    )
    st2 = exchange(st2)
    dy2, st3, misc = head(
        valid, labels, v, st2, st, row(mix_gain), row(mix_shift), row(out_slope), head_w.T, row(head_bias),
        TILES["head"],
    )
    st3 = exchange(st3)
    core = lax.axis_index("dp") % 2
    half = lambda i: jnp.reshape(i, (1,)).astype(jnp.int32)
    away, dvh, dvl, st3 = mix_back(
        half(1 - core), valid, dy2, v, st2, st, st3, row(mix_gain), uh, ul, TILES["mix"]
    )
    within = sizes["dp"] > 1
    got = flip(away, "dp", sizes["dp"], 1) if within else None
    m = mix_back_rest(half(core), dvh, dvl, uh, ul, TILES["mix"])
    if within:
        m, got, x = lax.optimization_barrier((m, got, x))
        first = Steps(sum_steps((m, got), sizes, True, False))
    else:
        first = Steps(sum_steps((jnp.concatenate([m, away], 0),), sizes, True, False))
    dxs, bws, sums = [], [], []
    for h in range(hops):
        first.step()
        dx, bw, s = hop_back(
            h, in_w, x, wp, st, branch_gain, branch_shift, branch_slope, mslope, dvh, dvl, mwh, mwl,
            j, TILES["hop"],
        )
        dxs, bws, sums = dxs + [dx], bws + [bw], sums + [s]
        first.state, x, bws, sums = lax.optimization_barrier((first.state, x, bws, sums))
    packed = pack(g, misc, bws, sums, max(128, 2 * sizes["dp"] * sizes["bucket"]))
    last = Steps(sum_steps((packed,), sizes, False, True))
    while not first.done:
        first.step()
        for _ in range(PACK_STEPS):
            last.step()
        first.state, last.state = lax.optimization_barrier((first.state, last.state))
    m = first.value
    if within:
        m, other = m, flip(m, "dp", sizes["dp"], 1)
        last.step()
        m, other, last.state = lax.optimization_barrier((m, other, last.state))
    else:
        m, other = pieces(m, 2)
    last.step()
    m, uu = assemble(half(core), m, other, mix_w)
    m, uu, last.state = lax.optimization_barrier((m, uu, last.state))
    while not last.done:
        last.step()
    packed = last.value
    d_x, bw, gain_grad, shift_grad, slope_grad, mslope_grad, oslope_grad, hw_grad, hb_grad, loss = fix(
        valid, x, packed, uu, st, branch_gain, branch_slope, mslope, wp, dxs, in_w, classes, misc.shape[0],
        TILES["fix"],
    )
    return (
        loss.reshape(()),
        d_x.T,
        bw.transpose(1, 0, 2),
        gain_grad,
        shift_grad,
        slope_grad,
        mslope_grad.reshape(mix),
        m,
        st3[1],
        st3[0],
        oslope_grad.reshape(hid),
        hw_grad.T,
        hb_grad.reshape(classes),
    )


def solution(mesh):
    sizes = {axis: mesh.shape[axis] for axis in ("dp", "bucket")}
    split_rows = P(("dp", "bucket"), None)
    in_specs = (split_rows, P(("dp", "bucket")), P(("dp", "bucket"))) + (P(),) * 11
    out_specs = (P(), split_rows) + (P(),) * 11
    return jax.shard_map(
        functools.partial(per_device, sizes),
        mesh=mesh,
        in_specs=in_specs,
        out_specs=out_specs,
        check_vma=False,
    )
```

```python
import functools

import jax
import jax.numpy as jnp
from jax import lax
from jax.experimental import pallas as pl
from jax.experimental.pallas import tpu as pltpu
from jax.sharding import PartitionSpec as P

EPS = 1e-05
F32 = jnp.float32
BF16 = jnp.bfloat16
LANES = 128
LOG2E = 1.4426950408889634
LN2 = 0.6931471805599453
TILES = {"gram": 2048, "project": 512, "forward": 512, "head": 512, "mix": 512, "hop": 512, "fix": 1024}
PACK_STEPS = 2
SUB = 256
MIX_SUB = 256
NN = (((1,), (0,)), ((), ()))
NT = (((1,), (1,)), ((), ()))
TN = (((0,), (0,)), ((), ()))


def split(x):
    hi = x.astype(BF16)
    return hi, (x - hi.astype(F32)).astype(BF16)


def dot3(a, b, dims=NN):
    ah, al = a
    bh, bl = b
    dot = functools.partial(lax.dot_general, dimension_numbers=dims, preferred_element_type=F32)
    return dot(ah, bh) + (dot(ah, bl) + dot(al, bh))


def act2(y, slope, rest):
    return jnp.maximum(slope * y + rest * jnp.log(1.0 + jnp.exp2(jnp.minimum(y, 30.0))), y)


def cost(us):
    return pl.CostEstimate(flops=0, bytes_accessed=int(us * 3.69e6), transcendentals=0)


def params(mib):
    return pltpu.CompilerParams(vmem_limit_bytes=mib * 1024 * 1024)


def near(x):
    return pltpu.with_memory_space_constraint(x, pltpu.VMEM)


def far(x):
    return pltpu.with_memory_space_constraint(x, pltpu.HBM)


def whole(x, buffers=2):
    mode = {} if buffers == 2 else {"pipeline_mode": pl.Buffered(buffers)}
    return pl.BlockSpec(x.shape, lambda *_: (0,) * len(x.shape), **mode)


def row_mask(valid_ref, step, tile, axis=0):
    n = jnp.sum(valid_ref[...])
    shape = (tile, 1) if axis == 0 else (1, tile)
    return step * tile + lax.broadcasted_iota(jnp.int32, shape, axis) < n


def hop_rows(x_ref, h, in_w, extra=None):
    x = x_ref[h * in_w : (h + 1) * in_w, :]
    pad = -(-(in_w + 1) // 16) * 16 - in_w
    tail = jnp.zeros((pad, x.shape[1]), F32)
    if extra is not None:
        first = lax.broadcasted_iota(jnp.int32, tail.shape, 0) == 0
        tail = jnp.where(first, extra, 0.0)
    return jnp.concatenate([x, tail], axis=0)


def stack3(a):
    hi, lo = split(a)
    return jnp.concatenate([hi, lo, hi], axis=0)


def gram_kernel(in_w, valid_ref, x_ref, w_ref, g_ref, copies_ref, wp_ref):
    step = pl.program_id(0)
    tile = x_ref.shape[1]
    hops, hid = w_ref.shape[1:]
    copies = copies_ref.shape[0]
    mask = row_mask(valid_ref, step, tile, 1)

    @pl.when(step == 0)
    def _():
        g_ref[...] = jnp.zeros_like(g_ref)

    for h in range(hops):
        x = jnp.where(mask, hop_rows(x_ref, h, in_w, 1.0), 0.0)
        hi, lo = split(x)
        n = x.shape[0]
        dot = functools.partial(lax.dot_general, dimension_numbers=NT, preferred_element_type=F32)
        cross = dot(hi, lo)
        g_ref[h, :, :n] += dot(hi, hi) + (cross + cross.T)

    @pl.when(step == pl.num_programs(0) - 1)
    def _():
        for h in range(hops):
            n = g_ref.shape[1]
            w = w_ref[:, h, :]
            w = jnp.concatenate([w, jnp.zeros((n - in_w, hid), F32)], axis=0)
            ws = split(w)
            gw = dot3(split(g_ref[h, :, :n]), ws)
            squares = jnp.sum(w * gw, axis=0, keepdims=True)
            copies_ref[:, :, h * hid : (h + 1) * hid] = jnp.broadcast_to(squares[None], (copies, 1, hid))
            sums = g_ref[h, in_w : in_w + 1, :]
            at = hops * hid + h * LANES
            copies_ref[:, :, at : at + LANES] = jnp.broadcast_to(sums[None], (copies, 1, LANES))
            wp_ref[h] = jnp.concatenate([ws[0], ws[0], ws[1]], axis=0)


def gram(valid, x, w, copies, tile):
    width, rows = x.shape
    in_w, hops, hid = w.shape
    n = -(-(in_w + 1) // 16) * 16
    shapes = (hops, n, LANES), (copies, 1, hops * (hid + LANES)), (hops, 3 * n, hid)
    return pl.pallas_call(
        functools.partial(gram_kernel, in_w),
        grid=(rows // tile,),
        in_specs=[whole(valid), pl.BlockSpec((width, tile), lambda i: (0, i)), whole(w)],
        out_specs=[pl.BlockSpec(s, lambda i, s=s: (0,) * len(s)) for s in shapes],
        out_shape=[jax.ShapeDtypeStruct(s, F32) for s in shapes[:2]] + [pltpu.HBM(shapes[2], BF16)],
        compiler_params=params(32),
        name="gram",
        cost_estimate=cost(5),
    )(far(valid), far(x), far(w))


def project_kernel(in_w, x_ref, wp_ref, z_ref):
    hid = wp_ref.shape[2]
    for h in range(wp_ref.shape[0]):
        xs = stack3(hop_rows(x_ref, h, in_w))
        cols = slice(h * hid, (h + 1) * hid)
        z_ref[:, cols] = lax.dot_general(xs, wp_ref[h], TN, preferred_element_type=F32)


def project(x, wp, in_w, tile):
    width, rows = x.shape
    hops, _, hid = wp.shape
    return pl.pallas_call(
        functools.partial(project_kernel, in_w),
        grid=(rows // tile,),
        in_specs=[pl.BlockSpec((width, tile), lambda i: (0, i)), whole(wp, 1)],
        out_specs=pl.BlockSpec((tile, hops * hid), lambda i: (i, 0)),
        out_shape=pltpu.HBM((rows, hops * hid), F32),
        compiler_params=params(24),
        name="project",
        cost_estimate=cost(9),
    )(far(x), far(wp))


def count_of(st_ref):
    return st_ref[0:1, st_ref.shape[1] - 1 :]


def norm_of(st_ref, cols):
    count = count_of(st_ref)
    mean = st_ref[0:1, cols] / count
    var = st_ref[1:2, cols] / count - mean * mean
    return mean, lax.rsqrt(var + EPS)


def scale_of(st_ref, cols, gain_ref, shift_ref, h):
    mean, rstd = norm_of(st_ref, cols)
    a = gain_ref[h : h + 1, :] * rstd
    return LOG2E * a, LOG2E * (shift_ref[h : h + 1, :] - mean * a)


def forward_kernel(
    in_w, valid_ref, z_ref, wp_ref, all_ref, gain_ref, shift_ref, slope_ref, mslope_ref, w_ref,
    uh_ref, ul_ref, v_ref, copies_ref, wh_out, wl_out, st_ref, coef_ref,
    st2_ref, wh_ref, wl_ref,
):
    step = pl.program_id(0)
    tile = z_ref.shape[0]
    hops, hid = gain_ref.shape
    mask = row_mask(valid_ref, step, tile)

    @pl.when(step == 0)
    def _():
        st2_ref[...] = jnp.zeros_like(st2_ref)
        sums = jnp.sum(all_ref[...], axis=0)
        n = wp_ref.shape[1] // 3
        for h in range(hops):
            rows = slice(h * hid, (h + 1) * hid)
            wh_ref[rows, :], wl_ref[rows, :] = split(w_ref[rows, :])
            at = hops * hid + h * LANES
            xm = jnp.broadcast_to(sums[:, at : at + n], (8, n))
            st_ref[0:1, rows] = dot3(split(xm), (wp_ref[h, :n, :], wp_ref[h, 2 * n :, :]))[0:1, :]
            st_ref[1:2, rows] = sums[:, rows]
        at = hops * hid + in_w
        st_ref[:, hops * hid :] = jnp.broadcast_to(sums[:, at : at + 1], (2, LANES))
        for h in range(hops):
            a, b = scale_of(st_ref, slice(h * hid, (h + 1) * hid), gain_ref, shift_ref, h)
            coef_ref[h] = jnp.concatenate(
                [a, b, slope_ref[h : h + 1, :], mslope_ref[h : h + 1, :], jnp.zeros((4, hid), F32)], axis=0
            )

    def activate(h, z):
        cols = slice(h * hid, (h + 1) * hid)
        a, b = scale_of(st_ref, cols, gain_ref, shift_ref, h)
        s1 = slope_ref[h : h + 1, :]
        s2 = mslope_ref[h : h + 1, :]
        j = act2(z * a + b, s1, LOG2E * (1.0 - s1))
        u = act2(j, s2, LOG2E * (1.0 - s2))
        us = split(u)
        uh_ref[:, cols], ul_ref[:, cols] = us
        return us

    def mix(h, us):
        cols = slice(h * hid, (h + 1) * hid)
        part = dot3(us, (wh_ref[cols, :], wl_ref[cols, :]))
        v_ref[...] = part if h == 0 else v_ref[...] + part

    before = None
    for h in range(hops):
        if before is not None:
            mix(h - 1, before)
        before = activate(h, z_ref[:, h * hid : (h + 1) * hid])
    mix(hops - 1, before)
    piece = pl.ds(pl.multiple_of(step * wh_out.shape[0], wh_out.shape[0]), wh_out.shape[0])
    wh_out[...], wl_out[...] = wh_ref[piece, :], wl_ref[piece, :]
    v = v_ref[...]
    v = LN2 * v
    v_ref[...] = v
    vm = jnp.where(mask, v, 0.0)
    st2_ref[0:1, :] += jnp.sum(vm, axis=0, keepdims=True)
    st2_ref[1:2, :] += jnp.sum(vm * vm, axis=0, keepdims=True)

    @pl.when(step == pl.num_programs(0) - 1)
    def _():
        copies_ref[...] = jnp.broadcast_to(st2_ref[...][None], copies_ref.shape)


def forward(valid, z, wp, sums, gain, shift, slope, mslope, w, in_w, copies, tile):
    rows = z.shape[0]
    mix, hid = w.shape
    by = lambda n: pl.BlockSpec((tile, n), lambda i: (i, 0))
    return pl.pallas_call(
        functools.partial(forward_kernel, in_w),
        grid=(rows // tile,),
        in_specs=[whole(valid), by(mix)]
        + [whole(t, 1) for t in (wp, sums, gain, shift, slope, mslope, w)],
        out_specs=[by(mix)] * 2
        + [by(hid), pl.BlockSpec((copies, 2, hid), lambda i: (0, 0, 0))]
        + [pl.BlockSpec((mix * tile // rows, hid), lambda i: (i, 0))] * 2
        + [pl.BlockSpec((2, mix + LANES), lambda i: (0, 0))]
        + [pl.BlockSpec((mix // hid, 8, hid), lambda i: (0, 0, 0))],
        out_shape=[
            pltpu.HBM((rows, mix), BF16),
            pltpu.HBM((rows, mix), BF16),
            pltpu.HBM((rows, hid), F32),
            jax.ShapeDtypeStruct((copies, 2, hid), F32),
            pltpu.HBM((mix, hid), BF16),
            pltpu.HBM((mix, hid), BF16),
            jax.ShapeDtypeStruct((2, mix + LANES), F32),
            jax.ShapeDtypeStruct((mix // hid, 8, hid), F32),
        ],
        scratch_shapes=[
            pltpu.VMEM((2, hid), F32),
            pltpu.VMEM((mix, hid), BF16),
            pltpu.VMEM((mix, hid), BF16),
        ],
        compiler_params=params(48),
        name="forward",
        cost_estimate=cost(30),
    )(valid, far(z), far(wp), sums, gain, shift, slope, mslope, far(w))


def as_column(row):
    n = row.shape[1]
    same = lax.broadcasted_iota(jnp.int32, (n, n), 0) == lax.broadcasted_iota(jnp.int32, (n, n), 1)
    return jnp.sum(jnp.where(same, jnp.broadcast_to(row, (n, n)), 0.0), axis=1, keepdims=True)


def as_row(col):
    n = col.shape[0]
    same = lax.broadcasted_iota(jnp.int32, (n, n), 0) == lax.broadcasted_iota(jnp.int32, (n, n), 1)
    return jnp.sum(jnp.where(same, jnp.broadcast_to(col, (n, n)), 0.0), axis=0, keepdims=True)


def head_kernel(
    valid_ref, labels_ref, v_ref, st_ref, cnt_ref, gain_ref, shift_ref, slope_ref, hw_ref, hb_ref,
    dy_ref, copies_ref, misc_ref, st3_ref,
):
    step = pl.program_id(0)
    tile, hid = v_ref.shape
    classes = hw_ref.shape[0]
    padded = -(-classes // 16) * 16
    mask = row_mask(valid_ref, step, tile, 1)
    count = count_of(cnt_ref)

    @pl.when(step == 0)
    def _():
        st3_ref[...] = jnp.zeros_like(st3_ref)
        misc_ref[...] = jnp.zeros_like(misc_ref)

    sums = jnp.sum(st_ref[...], axis=0)
    mean = sums[0:1, :] / count
    rstd = lax.rsqrt(sums[1:2, :] / count - mean * mean + EPS)
    s = slope_ref[...]
    zn = (v_ref[...] - mean) * rstd
    y = gain_ref[...] * zn + shift_ref[...]
    e1 = 1.0 + jnp.exp(jnp.minimum(y, 20.0))
    sp = jnp.maximum(jnp.log(e1), y)
    w = s * y + (1.0 - s) * sp
    ws = split(w)
    hw = hw_ref[...]
    if padded > classes:
        hw = jnp.concatenate([hw, jnp.zeros((padded - classes, hid), F32)], axis=0)
    hh, hl = split(hw)
    dot = functools.partial(lax.dot_general, dimension_numbers=NT, preferred_element_type=F32)
    both = dot(jnp.concatenate([hh, hl], axis=0), ws[0])
    logits = both[:padded] + both[padded:] + dot(hh, ws[1])
    logits = logits[:classes] + as_column(hb_ref[...])
    peak = jnp.max(logits, axis=0, keepdims=True)
    ex = jnp.exp(logits - peak)
    tot = jnp.sum(ex, axis=0, keepdims=True)
    per = tile // LANES
    lab = jnp.concatenate([labels_ref[pl.ds(step * per + k, 1), :] for k in range(per)], axis=1)
    hit = lab == lax.broadcasted_iota(jnp.int32, (classes, tile), 0)
    picked = jnp.sum(jnp.where(hit, logits, 0.0), axis=0, keepdims=True)
    loss = jnp.sum(jnp.where(mask, peak + jnp.log(tot) - picked, 0.0))
    dl = jnp.where(mask, (ex / tot - hit.astype(F32)) / count, 0.0)
    bias = as_row(jnp.sum(dl, axis=1, keepdims=True))
    if padded > classes:
        dl = jnp.concatenate([dl, jnp.zeros((padded - classes, tile), F32)], axis=0)
    dh, dlo = split(dl)
    dot = functools.partial(lax.dot_general, dimension_numbers=NN, preferred_element_type=F32)
    both = dot(jnp.concatenate([dh, dlo], axis=0), ws[0])
    hwg = both[:padded] + both[padded:] + dot(dh, ws[1])
    misc_ref[0:classes, :] += hwg[:classes]
    misc_ref[classes : classes + 1, 0:classes] += bias
    misc_ref[classes : classes + 1, LANES : 2 * LANES] += jnp.broadcast_to(loss, (1, LANES))
    dw = lax.dot_general(
        jnp.concatenate([dh, dlo, dh], axis=0),
        jnp.concatenate([hh, hh, hl], axis=0),
        TN,
        preferred_element_type=F32,
    )
    dy = dw * (1.0 - (1.0 - s) / e1)
    dy_ref[...] = dy
    row = lambda t: jnp.sum(t, axis=0, keepdims=True)
    misc_ref[classes + 1 : classes + 2, :] += row(dw * (y - sp))
    st3_ref[0:1, :] += row(dy)
    st3_ref[1:2, :] += row(dy * zn)

    @pl.when(step == pl.num_programs(0) - 1)
    def _():
        copies_ref[...] = jnp.broadcast_to(st3_ref[...][None], copies_ref.shape)


def head(valid, labels, v, st2, st, gain, shift, slope, hw, hb, tile):
    rows, hid = v.shape
    by = lambda n: pl.BlockSpec((tile, n), lambda i: (i, 0))
    misc = -(-(hw.shape[0] + 2) // 8) * 8
    return pl.pallas_call(
        head_kernel,
        grid=(rows // tile,),
        in_specs=[whole(valid), whole(labels), by(hid)]
        + [whole(t) for t in (st2, st, gain, shift, slope, hw, hb)],
        out_specs=[
            by(hid),
            whole(st2),
            pl.BlockSpec((misc, hid), lambda i: (0, 0)),
        ],
        out_shape=[
            pltpu.HBM((rows, hid), F32),
            jax.ShapeDtypeStruct(st2.shape, F32),
            jax.ShapeDtypeStruct((misc, hid), F32),
        ],
        scratch_shapes=[pltpu.VMEM((2, hid), F32)],
        compiler_params=params(24),
        name="head",
        cost_estimate=cost(9),
    )(valid, labels, far(v), st2, st, gain, shift, slope, hw, hb)


def mix_product(parts, uh_ref, ul_ref, m_ref):
    @pl.when(pl.program_id(0) == 0)
    def _():
        m_ref[...] = jnp.zeros_like(m_ref)

    ahead = parts[0][1]()
    for k, (rows, _) in enumerate(parts):
        dvs = ahead
        if k + 1 < len(parts):
            ahead = parts[k + 1][1]()
        hid = dvs[0].shape[1]
        for h in range(uh_ref.shape[1] // hid):
            cols = slice(h * hid, (h + 1) * hid)
            m_ref[cols, :] += dot3((uh_ref[rows, cols], ul_ref[rows, cols]), dvs, TN)


def mix_first_kernel(
    half_ref, valid_ref, dy_ref, v_ref, st2_ref, cnt_ref, st3_ref, gain_ref, uh_ref, ul_ref,
    m_ref, dvh_ref, dvl_ref, st3_out,
):
    step = pl.program_id(0)
    tile = dy_ref.shape[0]
    mask = row_mask(valid_ref, step, tile)
    count = count_of(cnt_ref)
    st2 = jnp.sum(st2_ref[...], axis=0)
    st3 = jnp.sum(st3_ref[...], axis=0)
    mean = st2[0:1, :] / count
    rstd = lax.rsqrt(st2[1:2, :] / count - mean * mean + EPS)
    a = LN2 * gain_ref[...] * rstd
    c1 = a * st3[0:1, :] / count
    c2 = a * st3[1:2, :] / count

    @pl.when(step == 0)
    def _():
        st3_out[...] = st3

    def dv(rows):
        zn = (v_ref[rows, :] - mean) * rstd
        dvs = split(jnp.where(mask[rows], a * dy_ref[rows, :] - (c1 + zn * c2), 0.0))
        dvh_ref[rows, :], dvl_ref[rows, :] = dvs
        return dvs

    parts = [slice(k, k + MIX_SUB) for k in range(0, tile, MIX_SUB)]
    mix_product([(rows, functools.partial(dv, rows)) for rows in parts], uh_ref, ul_ref, m_ref)


def mix_second_kernel(half_ref, dvh_ref, dvl_ref, uh_ref, ul_ref, m_ref):
    mix_product([(slice(None), lambda: (dvh_ref[...], dvl_ref[...]))], uh_ref, ul_ref, m_ref)


def mix_back(half, valid, dy, v, st2, st, st3, gain, uh, ul, tile):
    rows, hid = dy.shape
    part = uh.shape[1] // 2
    by = lambda n: pl.BlockSpec((tile, n), lambda i, half: (i, 0))
    return pl.pallas_call(
        mix_first_kernel,
        grid_spec=pltpu.PrefetchScalarGridSpec(
            num_scalar_prefetch=1,
            grid=(rows // tile,),
            in_specs=[whole(valid), by(hid), by(hid)]
            + [whole(t) for t in (st2, st, st3, gain)]
            + [pl.BlockSpec((tile, part), lambda i, half: (i, half[0]))] * 2,
            out_specs=[pl.BlockSpec((part, hid), lambda i, half: (0, 0)), by(hid), by(hid)]
            + [pl.BlockSpec((2, hid), lambda i, half: (0, 0))],
        ),
        out_shape=[
            jax.ShapeDtypeStruct((part, hid), F32),
            pltpu.HBM((rows, hid), BF16),
            pltpu.HBM((rows, hid), BF16),
            jax.ShapeDtypeStruct((2, hid), F32),
        ],
        compiler_params=params(28),
        name="mix_back",
        cost_estimate=cost(14),
    )(half, valid, far(dy), far(v), st2, st, st3, gain, far(uh), far(ul))


def mix_back_rest(half, dvh, dvl, uh, ul, tile):
    rows, hid = dvh.shape
    part = uh.shape[1] // 2
    by = lambda n: pl.BlockSpec((tile, n), lambda i, half: (i, 0))
    return pl.pallas_call(
        mix_second_kernel,
        grid_spec=pltpu.PrefetchScalarGridSpec(
            num_scalar_prefetch=1,
            grid=(rows // tile,),
            in_specs=[by(hid), by(hid)]
            + [pl.BlockSpec((tile, part), lambda i, half: (i, half[0]))] * 2,
            out_specs=pl.BlockSpec((part, hid), lambda i, half: (0, 0)),
        ),
        out_shape=jax.ShapeDtypeStruct((part, hid), F32),
        compiler_params=params(28),
        name="mix_back_rest",
        cost_estimate=cost(12),
    )(half, far(dvh), far(dvl), far(uh), far(ul))


def hop_kernel(
    h, in_w, x_ref, wp_ref, coef_ref, dvh_ref, dvl_ref, mwh_ref, mwl_ref,
    dx_ref, bw_ref, sums_ref,
):
    step = pl.program_id(0)
    n = wp_ref.shape[1] // 3
    tile = x_ref.shape[1]

    @pl.when(step == 0)
    def _():
        bw_ref[...] = jnp.zeros_like(bw_ref)
        sums_ref[...] = jnp.zeros_like(sums_ref)

    a, b, s1, s2 = (coef_ref[0, k : k + 1, :] for k in range(4))
    xall = stack3(hop_rows(x_ref, h % (x_ref.shape[0] // in_w), in_w, 1.0))
    wp = wp_ref[0]
    wh, wl = split((wp[:n].astype(F32) + wp[2 * n :].astype(F32)) * a)
    whl = jnp.concatenate([wh, wl], axis=0)
    dot = functools.partial(lax.dot_general, preferred_element_type=F32)
    row = lambda t: jnp.sum(t, axis=0, keepdims=True)
    sums = [0.0] * 2
    parts = [slice(k, k + SUB) for k in range(0, tile, SUB)]

    def products(rs):
        y = dot(xall[:, rs], wp, TN)
        return y, dot3((dvh_ref[rs, :], dvl_ref[rs, :]), (mwh_ref[...], mwl_ref[...]), NT)

    def middle(rs, z, du):
        y = z * a + b
        e = 1.0 + jnp.exp2(jnp.minimum(y, 30.0))
        j = jnp.maximum(s1 * y + (LOG2E * (1.0 - s1)) * jnp.log(e), y)
        dj = du * (1.0 - (1.0 - s2) / (1.0 + jnp.exp2(j)))
        dy = dj * (1.0 - (1.0 - s1) / e)
        for q, t in enumerate((dj * (y - j), du * j)):
            sums[q] = sums[q] + row(t)
        return split(dy)

    def results(rs, dys):
        dh, dl = dys
        xs = xall[: 2 * n, rs]
        both = dot(xs, dh, NN)
        bw_ref[...] += both[:n] + both[n:] + dot(xs[:n], dl, NN)
        both = dot(whl, dh, NT)
        dx_ref[:, rs] = both[:n] + both[n:] + dot(wh, dl, NT)

    now = products(parts[0])
    before = None
    for k, rs in enumerate(parts):
        ahead = products(parts[k + 1]) if k + 1 < len(parts) else None
        if before is not None:
            results(parts[k - 1], before)
        before = middle(rs, *now)
        now = ahead
    results(parts[-1], before)
    for q in range(2):
        sums_ref[q : q + 1, :] += sums[q]


def hop_back(h, in_w, x, wp, coef, dvh, dvl, mwh, mwl, tile):
    width, rows = x.shape
    some = 2 * in_w if width % (2 * in_w) == 0 and in_w % 4 == 0 else width
    at = h * in_w // some
    hid = dvh.shape[1]
    n = wp.shape[1] // 3
    by = lambda w, k=0: pl.BlockSpec((tile, w), lambda i: (i, k))
    block = lambda r: pl.BlockSpec((r, hid), lambda i: (h, 0))
    return pl.pallas_call(
        functools.partial(hop_kernel, h, in_w),
        grid=(rows // tile,),
        in_specs=[
            pl.BlockSpec((some, tile), lambda i: (at, i)),
            pl.BlockSpec((1, 3 * n, hid), lambda i: (h, 0, 0)),
            pl.BlockSpec((1, 8, hid), lambda i: (h, 0, 0)),
        ]
        + [by(hid), by(hid), block(hid), block(hid)],
        out_specs=[
            pl.BlockSpec((n, tile), lambda i: (0, i)),
            pl.BlockSpec((n, hid), lambda i: (0, 0)),
            pl.BlockSpec((2, hid), lambda i: (0, 0)),
        ],
        out_shape=[
            pltpu.HBM((n, rows), F32),
            jax.ShapeDtypeStruct((n, hid), F32),
            jax.ShapeDtypeStruct((2, hid), F32),
        ],
        compiler_params=params(20),
        name=f"hop_back_{h}",
        cost_estimate=cost(11),
    )(far(x), far(wp), coef, far(dvh), far(dvl), far(mwh), far(mwl))


def assemble_kernel(first_ref, own_ref, got_ref, w_ref, m_ref, uu_ref):
    mine = (pl.program_id(0) // 2) == first_ref[0]
    m = jnp.where(mine, own_ref[...], got_ref[...])
    m_ref[...] = m
    ones = jnp.ones((8, m.shape[1]), BF16)
    dot = functools.partial(lax.dot_general, dimension_numbers=NT, preferred_element_type=F32)
    hi, lo = split(m * w_ref[...])
    uu_ref[0] = dot(ones, hi) + dot(ones, lo)


def assemble(first, own, got, w):
    rows, hid = w.shape
    block = rows // 4
    half = pl.BlockSpec((block, hid), lambda i, first: (i % 2, 0))
    by = pl.BlockSpec((block, hid), lambda i, first: (i, 0))
    return pl.pallas_call(
        assemble_kernel,
        grid_spec=pltpu.PrefetchScalarGridSpec(
            num_scalar_prefetch=1,
            grid=(4,),
            in_specs=[half, half, by],
            out_specs=[by, pl.BlockSpec((1, 8, block), lambda i, first: (i, 0, 0))],
        ),
        out_shape=[jax.ShapeDtypeStruct((rows, hid), F32), jax.ShapeDtypeStruct((4, 8, block), F32)],
        compiler_params=params(20),
        name="assemble",
        cost_estimate=cost(5),
    )(first, own, got, far(w))


def pack_rows(n, hops, misc, unit=1):
    base = hops * n
    gram_at = base + misc + 2 * hops
    used = gram_at + hops * n // 4
    return base, gram_at, -(-used // unit) * unit


def pack_kernel(g_ref, misc_ref, *refs):
    hops = g_ref.shape[0]
    n = g_ref.shape[1]
    out_ref = refs[-1]
    base, gram_at, _ = pack_rows(n, hops, misc_ref.shape[0])
    total = out_ref.shape[0]
    for h in range(hops):
        out_ref[h * n : (h + 1) * n, :] = refs[h][...]
        k = base + misc_ref.shape[0] + 2 * h
        out_ref[k : k + 2, :] = refs[hops + h][...]
        for q in range(4):
            k = gram_at + h * n // 4
            out_ref[k : k + n // 4, q * LANES : (q + 1) * LANES] = g_ref[h, q * n // 4 : (q + 1) * n // 4, :]
    out_ref[base : base + misc_ref.shape[0], :] = misc_ref[...]
    used = gram_at + hops * n // 4
    if used < total:
        out_ref[used:, :] = jnp.zeros((total - used, out_ref.shape[1]), F32)


def pack(g, misc, bws, sums, unit):
    hid = misc.shape[1]
    total = pack_rows(g.shape[1], g.shape[0], misc.shape[0], unit)[2]
    return pl.pallas_call(
        pack_kernel,
        out_shape=jax.ShapeDtypeStruct((total, hid), F32),
        compiler_params=params(24),
        name="pack",
        cost_estimate=cost(3),
    )(g, misc, *bws, *sums)


def fix_kernel(in_w, classes, misc, valid_ref, x_ref, p_ref, uu_ref, st_ref, gain_ref, slope_ref, mslope_ref, wp_ref, *refs):
    step = pl.program_id(0)
    hops, hid = gain_ref.shape
    tile = x_ref.shape[1]
    n = wp_ref.shape[1] // 3
    dxs, rest = refs[:hops], refs[hops:]
    dx_ref, bw_ref, gain_out, shift_out, slope_out, mslope_out, oslope_out, hw_out, hb_out, loss_out, q_ref = rest
    base, gram_at, _ = pack_rows(n, hops, misc)
    mask = row_mask(valid_ref, step, tile, 1)

    @pl.when(step == 0)
    def _():
        count = count_of(st_ref)
        hw_out[...] = p_ref[base : base + classes, :]
        hb_out[...] = p_ref[base + classes : base + classes + 1, :classes]
        loss_out[...] = p_ref[base + classes : base + classes + 1, LANES : LANES + 1] / count
        oslope_out[...] = p_ref[base + classes + 1 : base + classes + 2, :]
        for h in range(hops):
            cols = slice(h * hid, (h + 1) * hid)
            mean, rstd = norm_of(st_ref, cols)
            gain = gain_ref[h : h + 1, :]
            wh, wl = wp_ref[h, :n, :], wp_ref[h, 2 * n :, :]
            w = wh.astype(F32) + wl.astype(F32)
            raw = p_ref[h * n : (h + 1) * n, :]
            total = LOG2E * raw[in_w : in_w + 1, :]
            gsum = rstd * (LOG2E * jnp.sum(w * raw, axis=0, keepdims=True) - mean * total)
            gain_out[h : h + 1, :] = gsum
            shift_out[h : h + 1, :] = total
            at = base + misc + 2 * h
            slope_out[h : h + 1, :] = p_ref[at : at + 1, :] / (1.0 - slope_ref[h : h + 1, :])
            uu = uu_ref[h, 0:1, :]
            mslope_out[h : h + 1, :] = (p_ref[at + 1 : at + 2, :] - uu) / (1.0 - mslope_ref[h : h + 1, :])
            a = gain * rstd / count
            c2 = a * gsum * rstd
            k0 = a * total - mean * c2
            wc = w * c2
            mask_row = lax.broadcasted_iota(jnp.int32, (n, hid), 0) == in_w
            wc = split(jnp.where(mask_row, k0, wc))
            q_ref[h, :, :n] = dot3((wh, wl), wc, NT)
            k = gram_at + h * n // 4
            g = jnp.concatenate(
                [p_ref[k : k + n // 4, q * LANES : q * LANES + n] for q in range(4)], axis=0
            )
            bw = raw * (LOG2E * gain * rstd) - dot3(split(g), wc)
            bw_ref[:, h, :] = bw[:in_w]

    for h in range(hops):
        x = jnp.where(mask, hop_rows(x_ref, h, in_w, 1.0), 0.0)
        fix = dot3(split(q_ref[h, :, :n]), split(x))
        dx_ref[h * in_w : (h + 1) * in_w, :] = (dxs[h][...] - fix)[:in_w]


def fix(valid, x, packed, uu, st, gain, slope, mslope, wp, dxs, in_w, classes, misc, tile):
    width, rows = x.shape
    hops, hid = gain.shape
    n = wp.shape[1] // 3
    cols = lambda r: pl.BlockSpec((r, tile), lambda i: (0, i))
    shapes = ((in_w, hops, hid),) + ((hops, hid),) * 4 + ((1, hid), (classes, hid), (1, classes), (1, 1))
    return pl.pallas_call(
        functools.partial(fix_kernel, in_w, classes, misc),
        grid=(rows // tile,),
        in_specs=[whole(valid), cols(width)]
        + [whole(t) for t in (packed, uu, st, gain, slope, mslope, wp)]
        + [cols(n)] * hops,
        out_specs=[cols(width)] + [pl.BlockSpec(s, lambda i, s=s: (0,) * len(s)) for s in shapes],
        out_shape=[jax.ShapeDtypeStruct(s, F32) for s in ((width, rows),) + shapes],
        scratch_shapes=[pltpu.VMEM((hops, n, LANES), F32)],
        compiler_params=params(24),
        name="fix",
        cost_estimate=cost(8),
    )(valid, far(x), packed, uu, st, gain, slope, mslope, far(wp), *[far(d) for d in dxs])


def flip(v, axis, size, k):
    return lax.ppermute(v, axis, [(i, i ^ k) for i in range(size)])


def exchange(copies):
    return lax.all_to_all(copies, ("dp", "bucket"), 0, 0, tiled=True)


def pieces(v, n):
    size = v.shape[0] // n
    return [v[i * size : (i + 1) * size] for i in range(n)]


def take(v, index, n):
    size = v.shape[0] // n
    return lax.dynamic_slice_in_dim(v, index * size, size, 0)


def merge(v, got, axis, size, k):
    bit = lax.axis_index(axis) // k % 2
    return jnp.where(bit == 0, jnp.concatenate([v, got], 0), jnp.concatenate([got, v], 0))


def halve(v, axis, size, k):
    bit = lax.axis_index(axis) // k % 2
    return v, flip(take(v, 1 - bit, 2), axis, size, k)


def kept(v, got, axis, size, k):
    return take(v, lax.axis_index(axis) // k % 2, 2) + got


def spread(v, axis, size, k):
    me = lax.axis_index(axis) // k
    return tuple(flip(take(v, me ^ i, 4), axis, size, k * i) if i else take(v, me, 4) for i in range(4))


def collect(v, axis, size, k):
    return (v,) + tuple(flip(v, axis, size, k * i) for i in range(1, 4))


def in_order(parts, axis, k):
    low, high = lax.axis_index(axis) // k % 2, lax.axis_index(axis) // (2 * k) % 2
    pair = lambda a, b: jnp.where(low == 0, jnp.concatenate([a, b], 0), jnp.concatenate([b, a], 0))
    near, far = pair(parts[0], parts[1]), pair(parts[2], parts[3])
    return jnp.where(high == 0, jnp.concatenate([near, far], 0), jnp.concatenate([far, near], 0))


def total(parts):
    if len(parts) == 4:
        return (parts[0] + parts[1]) + (parts[2] + parts[3])
    return functools.reduce(jnp.add, parts)


def sum_steps(parts, sizes, large, within):
    dp, bucket = sizes["dp"], sizes["bucket"]
    across = [("dp", dp, 1 << i) for i in range(1, dp.bit_length() - 1)]
    square = len(across) == 2 and not large
    line = [("bucket", bucket, 1 << i) for i in range(bucket.bit_length() - 1)]
    core = ("dp", dp, 1)
    within = within and dp > 1
    if within:
        parts = [kept(*(yield halve(total(parts), *core)), *core)]
    if square:
        parts = yield spread(total(parts), "dp", dp, 2)
    elif across:
        a, b = across[0], across[-1]
        bits = [lax.axis_index("dp") // s[2] % 2 for s in (a, b)]
        quarter = lambda i: functools.reduce(jnp.add, [take(p, i, 4) for p in parts])
        gone = flip(quarter(1 - bits[0]), *a), flip(quarter(3 - bits[1]), *b)
        parts, got = yield tuple(parts), gone
        top, bottom = quarter(bits[0]) + got[0], quarter(2 + bits[1]) + got[1]
        for a, b in list(zip(across, across[::-1]))[1:]:
            got = yield halve(top, *a), halve(bottom, *b)
            top, bottom = kept(*got[0], *a), kept(*got[1], *b)
        parts = [jnp.concatenate([top, bottom], 0)]
    if bucket == 4:
        parts = yield spread(total(parts), "bucket", bucket, 1)
        parts = yield collect(total(parts), "bucket", bucket, 1)
        v = in_order(parts, "bucket", 1)
    else:
        v = total(parts)
        for s in line:
            v = kept(*(yield halve(v, *s)), *s)
        for s in line[::-1]:
            parts = yield v, flip(v, *s)
            v = merge(*parts, *s)
    if square:
        v = in_order((yield collect(v, "dp", dp, 2)), "dp", 2)
    elif across:
        top, bottom = pieces(v, 2)
        for a, b in zip(across[::-1], across):
            got = yield top, flip(top, *a), bottom, flip(bottom, *b)
            top, bottom = merge(*got[:2], *a), merge(*got[2:], *b)
        v = jnp.concatenate([top, bottom], 0)
    if within:
        v = merge(*(yield v, flip(v, *core)), *core)
    return v


class Steps:
    def __init__(self, steps):
        self.steps, self.state, self.done, self.value = steps, None, False, None

    def step(self):
        if not self.done:
            try:
                self.state = self.steps.send(self.state)
            except StopIteration as end:
                self.done, self.value, self.state = True, end.value, None


def per_device(sizes, feats, labels, valid, branch_w, branch_gain, branch_shift, branch_slope, mix_slope,
               mix_w, mix_gain, mix_shift, out_slope, head_w, head_bias):
    rows, width = feats.shape
    hops, in_w, hid = branch_w.shape
    classes = head_w.shape[1]
    mix = hops * hid
    valid = valid.reshape(rows // LANES, LANES)
    labels = labels.reshape(rows // LANES, LANES)
    mslope = mix_slope.reshape(hops, hid)
    row = lambda t: t.reshape(1, -1)
    x = feats.T

    devices = sizes["dp"] * sizes["bucket"]
    g, sums, wp = gram(valid, x, branch_w.transpose(1, 0, 2), devices, TILES["gram"])
    sums = exchange(sums)
    z = project(x, wp, in_w, TILES["project"])
    uh, ul, v, st2, mwh, mwl, st, coef = forward(
        valid, z, wp, sums, branch_gain, branch_shift, branch_slope, mslope, mix_w, in_w, devices,
        TILES["forward"],
    )
    st2 = exchange(st2)
    dy2, st3, misc = head(
        valid, labels, v, st2, st, row(mix_gain), row(mix_shift), row(out_slope), head_w.T, row(head_bias),
        TILES["head"],
    )
    st3 = exchange(st3)
    core = lax.axis_index("dp") % 2
    half = lambda i: jnp.reshape(i, (1,)).astype(jnp.int32)
    away, dvh, dvl, st3 = mix_back(
        half(1 - core), valid, dy2, v, st2, st, st3, row(mix_gain), uh, ul, TILES["mix"]
    )
    within = sizes["dp"] > 1
    got = flip(away, "dp", sizes["dp"], 1) if within else None
    m = mix_back_rest(half(core), dvh, dvl, uh, ul, TILES["mix"])
    if within:
        m, got, x = lax.optimization_barrier((m, got, x))
        first = Steps(sum_steps((m, got), sizes, True, False))
    else:
        first = Steps(sum_steps((jnp.concatenate([m, away], 0),), sizes, True, False))
    dxs, bws, sums = [], [], []
    for h in range(hops):
        first.step()
        dx, bw, s = hop_back(
            h, in_w, x, wp, coef, dvh, dvl, mwh, mwl, TILES["hop"],
        )
        dxs, bws, sums = dxs + [dx], bws + [bw], sums + [s]
        first.state, x, bws, sums = lax.optimization_barrier((first.state, x, bws, sums))
    packed = pack(g, misc, bws, sums, max(128, 2 * sizes["dp"] * sizes["bucket"]))
    last = Steps(sum_steps((packed,), sizes, False, True))
    first.step()
    last.step()
    last.step()
    first.state, last.state = lax.optimization_barrier((first.state, last.state))
    first.step()
    last.step()
    first.state, last.state = lax.optimization_barrier((first.state, last.state))
    while not first.done:
        first.step()
    m = first.value
    m, other = (m, flip(m, "dp", sizes["dp"], 1)) if within else pieces(m, 2)
    last.step()
    m, other, last.state = lax.optimization_barrier((m, other, last.state))
    last.step()
    m, uu = assemble(half(core), m, other, mix_w)
    m, uu, last.state = lax.optimization_barrier((m, uu, last.state))
    while not last.done:
        last.step()
    packed = last.value
    d_x, bw, gain_grad, shift_grad, slope_grad, mslope_grad, oslope_grad, hw_grad, hb_grad, loss = fix(
        valid, x, packed, uu, st, branch_gain, branch_slope, mslope, wp, dxs, in_w, classes, misc.shape[0],
        TILES["fix"],
    )
    return (
        loss.reshape(()),
        d_x.T,
        bw.transpose(1, 0, 2),
        gain_grad,
        shift_grad,
        slope_grad,
        mslope_grad.reshape(mix),
        m,
        st3[1],
        st3[0],
        oslope_grad.reshape(hid),
        hw_grad.T,
        hb_grad.reshape(classes),
    )


def solution(mesh):
    sizes = {axis: mesh.shape[axis] for axis in ("dp", "bucket")}
    split_rows = P(("dp", "bucket"), None)
    in_specs = (split_rows, P(("dp", "bucket")), P(("dp", "bucket"))) + (P(),) * 11
    out_specs = (P(), split_rows) + (P(),) * 11
    return jax.shard_map(
        functools.partial(per_device, sizes),
        mesh=mesh,
        in_specs=in_specs,
        out_specs=out_specs,
        check_vma=False,
    )
```

```python
import functools

import jax
import jax.numpy as jnp
from jax import lax
from jax.experimental import pallas as pl
from jax.experimental.pallas import tpu as pltpu
from jax.sharding import PartitionSpec as P

EPS = 1e-05
F32 = jnp.float32
BF16 = jnp.bfloat16
LANES = 128
LOG2E = 1.4426950408889634
LN2 = 0.6931471805599453
TILES = {"gram": 2048, "project": 512, "forward": 512, "head": 1024, "mix": 512, "hop": 512, "fix": 1024}
PACK_STEPS = 2
SUB = 256
MIX_SUB = 256
NN = (((1,), (0,)), ((), ()))
NT = (((1,), (1,)), ((), ()))
TN = (((0,), (0,)), ((), ()))


def split(x):
    hi = x.astype(BF16)
    return hi, (x - hi.astype(F32)).astype(BF16)


def dot3(a, b, dims=NN):
    ah, al = a
    bh, bl = b
    dot = functools.partial(lax.dot_general, dimension_numbers=dims, preferred_element_type=F32)
    return dot(ah, bh) + (dot(ah, bl) + dot(al, bh))


def act2(y, slope, rest):
    return jnp.maximum(slope * y + rest * jnp.log(1.0 + jnp.exp2(jnp.minimum(y, 30.0))), y)


def cost(us):
    return pl.CostEstimate(flops=0, bytes_accessed=int(us * 3.69e6), transcendentals=0)


def params(mib):
    return pltpu.CompilerParams(vmem_limit_bytes=mib * 1024 * 1024)


def near(x):
    return pltpu.with_memory_space_constraint(x, pltpu.VMEM)


def far(x):
    return pltpu.with_memory_space_constraint(x, pltpu.HBM)


def whole(x, buffers=2):
    mode = {} if buffers == 2 else {"pipeline_mode": pl.Buffered(buffers)}
    return pl.BlockSpec(x.shape, lambda *_: (0,) * len(x.shape), **mode)


def row_mask(valid_ref, step, tile, axis=0):
    n = jnp.sum(valid_ref[...])
    shape = (tile, 1) if axis == 0 else (1, tile)
    return step * tile + lax.broadcasted_iota(jnp.int32, shape, axis) < n


def hop_rows(x_ref, h, in_w, extra=None):
    x = x_ref[h * in_w : (h + 1) * in_w, :]
    pad = -(-(in_w + 1) // 16) * 16 - in_w
    tail = jnp.zeros((pad, x.shape[1]), F32)
    if extra is not None:
        first = lax.broadcasted_iota(jnp.int32, tail.shape, 0) == 0
        tail = jnp.where(first, extra, 0.0)
    return jnp.concatenate([x, tail], axis=0)


def stack3(a):
    hi, lo = split(a)
    return jnp.concatenate([hi, lo, hi], axis=0)


def gram_kernel(in_w, valid_ref, x_ref, w_ref, g_ref, copies_ref, wp_ref):
    step = pl.program_id(0)
    tile = x_ref.shape[1]
    hops, hid = w_ref.shape[1:]
    copies = copies_ref.shape[0]
    mask = row_mask(valid_ref, step, tile, 1)

    @pl.when(step == 0)
    def _():
        g_ref[...] = jnp.zeros_like(g_ref)

    for h in range(hops):
        x = jnp.where(mask, hop_rows(x_ref, h, in_w, 1.0), 0.0)
        hi, lo = split(x)
        n = x.shape[0]
        dot = functools.partial(lax.dot_general, dimension_numbers=NT, preferred_element_type=F32)
        cross = dot(hi, lo)
        g_ref[h, :, :n] += dot(hi, hi) + (cross + cross.T)

    @pl.when(step == pl.num_programs(0) - 1)
    def _():
        for h in range(hops):
            n = g_ref.shape[1]
            w = w_ref[:, h, :]
            w = jnp.concatenate([w, jnp.zeros((n - in_w, hid), F32)], axis=0)
            ws = split(w)
            gw = dot3(split(g_ref[h, :, :n]), ws)
            squares = jnp.sum(w * gw, axis=0, keepdims=True)
            copies_ref[:, :, h * hid : (h + 1) * hid] = jnp.broadcast_to(squares[None], (copies, 1, hid))
            sums = g_ref[h, in_w : in_w + 1, :]
            at = hops * hid + h * LANES
            copies_ref[:, :, at : at + LANES] = jnp.broadcast_to(sums[None], (copies, 1, LANES))
            wp_ref[h] = jnp.concatenate([ws[0], ws[0], ws[1]], axis=0)


def gram(valid, x, w, copies, tile):
    width, rows = x.shape
    in_w, hops, hid = w.shape
    n = -(-(in_w + 1) // 16) * 16
    shapes = (hops, n, LANES), (copies, 1, hops * (hid + LANES)), (hops, 3 * n, hid)
    return pl.pallas_call(
        functools.partial(gram_kernel, in_w),
        grid=(rows // tile,),
        in_specs=[whole(valid), pl.BlockSpec((width, tile), lambda i: (0, i)), whole(w)],
        out_specs=[pl.BlockSpec(s, lambda i, s=s: (0,) * len(s)) for s in shapes],
        out_shape=[jax.ShapeDtypeStruct(s, F32) for s in shapes[:2]] + [pltpu.HBM(shapes[2], BF16)],
        compiler_params=params(32),
        name="gram",
        cost_estimate=cost(5),
    )(far(valid), far(x), far(w))


def project_kernel(in_w, x_ref, wp_ref, z_ref):
    hid = wp_ref.shape[2]
    for h in range(wp_ref.shape[0]):
        xs = stack3(hop_rows(x_ref, h, in_w))
        cols = slice(h * hid, (h + 1) * hid)
        z_ref[:, cols] = lax.dot_general(xs, wp_ref[h], TN, preferred_element_type=F32)


def project(x, wp, in_w, tile):
    width, rows = x.shape
    hops, _, hid = wp.shape
    return pl.pallas_call(
        functools.partial(project_kernel, in_w),
        grid=(rows // tile,),
        in_specs=[pl.BlockSpec((width, tile), lambda i: (0, i)), whole(wp, 1)],
        out_specs=pl.BlockSpec((tile, hops * hid), lambda i: (i, 0)),
        out_shape=pltpu.HBM((rows, hops * hid), F32),
        compiler_params=params(24),
        name="project",
        cost_estimate=cost(9),
    )(far(x), far(wp))


def count_of(st_ref):
    return st_ref[0:1, st_ref.shape[1] - 1 :]


def norm_of(st_ref, cols):
    count = count_of(st_ref)
    mean = st_ref[0:1, cols] / count
    var = st_ref[1:2, cols] / count - mean * mean
    return mean, lax.rsqrt(var + EPS)


def scale_of(st_ref, cols, gain_ref, shift_ref, h):
    mean, rstd = norm_of(st_ref, cols)
    a = gain_ref[h : h + 1, :] * rstd
    return LOG2E * a, LOG2E * (shift_ref[h : h + 1, :] - mean * a)


def forward_kernel(
    in_w, valid_ref, z_ref, wp_ref, all_ref, gain_ref, shift_ref, slope_ref, mslope_ref, w_ref,
    uh_ref, ul_ref, v_ref, copies_ref, wh_out, wl_out, st_ref, coef_ref,
    st2_ref, wh_ref, wl_ref,
):
    step = pl.program_id(0)
    tile = z_ref.shape[0]
    hops, hid = gain_ref.shape
    mask = row_mask(valid_ref, step, tile)

    @pl.when(step == 0)
    def _():
        st2_ref[...] = jnp.zeros_like(st2_ref)
        sums = jnp.sum(all_ref[...], axis=0)
        n = wp_ref.shape[1] // 3
        for h in range(hops):
            rows = slice(h * hid, (h + 1) * hid)
            wh_ref[rows, :], wl_ref[rows, :] = split(w_ref[rows, :])
            at = hops * hid + h * LANES
            xm = jnp.broadcast_to(sums[:, at : at + n], (8, n))
            st_ref[0:1, rows] = dot3(split(xm), (wp_ref[h, :n, :], wp_ref[h, 2 * n :, :]))[0:1, :]
            st_ref[1:2, rows] = sums[:, rows]
        at = hops * hid + in_w
        st_ref[:, hops * hid :] = jnp.broadcast_to(sums[:, at : at + 1], (2, LANES))
        for h in range(hops):
            a, b = scale_of(st_ref, slice(h * hid, (h + 1) * hid), gain_ref, shift_ref, h)
            coef_ref[h] = jnp.concatenate(
                [a, b, slope_ref[h : h + 1, :], mslope_ref[h : h + 1, :], jnp.zeros((4, hid), F32)], axis=0
            )

    def activate(h, z):
        cols = slice(h * hid, (h + 1) * hid)
        a, b = scale_of(st_ref, cols, gain_ref, shift_ref, h)
        s1 = slope_ref[h : h + 1, :]
        s2 = mslope_ref[h : h + 1, :]
        j = act2(z * a + b, s1, LOG2E * (1.0 - s1))
        u = act2(j, s2, LOG2E * (1.0 - s2))
        us = split(u)
        uh_ref[:, cols], ul_ref[:, cols] = us
        return us

    def mix(h, us):
        cols = slice(h * hid, (h + 1) * hid)
        part = dot3(us, (wh_ref[cols, :], wl_ref[cols, :]))
        v_ref[...] = part if h == 0 else v_ref[...] + part

    before = None
    for h in range(hops):
        if before is not None:
            mix(h - 1, before)
        before = activate(h, z_ref[:, h * hid : (h + 1) * hid])
    mix(hops - 1, before)
    piece = pl.ds(pl.multiple_of(step * wh_out.shape[0], wh_out.shape[0]), wh_out.shape[0])
    wh_out[...], wl_out[...] = wh_ref[piece, :], wl_ref[piece, :]
    v = v_ref[...]
    v = LN2 * v
    v_ref[...] = v
    vm = jnp.where(mask, v, 0.0)
    st2_ref[0:1, :] += jnp.sum(vm, axis=0, keepdims=True)
    st2_ref[1:2, :] += jnp.sum(vm * vm, axis=0, keepdims=True)

    @pl.when(step == pl.num_programs(0) - 1)
    def _():
        copies_ref[...] = jnp.broadcast_to(st2_ref[...][None], copies_ref.shape)


def forward(valid, z, wp, sums, gain, shift, slope, mslope, w, in_w, copies, tile):
    rows = z.shape[0]
    mix, hid = w.shape
    by = lambda n: pl.BlockSpec((tile, n), lambda i: (i, 0))
    return pl.pallas_call(
        functools.partial(forward_kernel, in_w),
        grid=(rows // tile,),
        in_specs=[whole(valid), by(mix)]
        + [whole(t, 1) for t in (wp, sums, gain, shift, slope, mslope, w)],
        out_specs=[by(mix)] * 2
        + [by(hid), pl.BlockSpec((copies, 2, hid), lambda i: (0, 0, 0))]
        + [pl.BlockSpec((mix * tile // rows, hid), lambda i: (i, 0))] * 2
        + [pl.BlockSpec((2, mix + LANES), lambda i: (0, 0))]
        + [pl.BlockSpec((mix // hid, 8, hid), lambda i: (0, 0, 0))],
        out_shape=[
            pltpu.HBM((rows, mix), BF16),
            pltpu.HBM((rows, mix), BF16),
            pltpu.HBM((rows, hid), F32),
            jax.ShapeDtypeStruct((copies, 2, hid), F32),
            pltpu.HBM((mix, hid), BF16),
            pltpu.HBM((mix, hid), BF16),
            jax.ShapeDtypeStruct((2, mix + LANES), F32),
            jax.ShapeDtypeStruct((mix // hid, 8, hid), F32),
        ],
        scratch_shapes=[
            pltpu.VMEM((2, hid), F32),
            pltpu.VMEM((mix, hid), BF16),
            pltpu.VMEM((mix, hid), BF16),
        ],
        compiler_params=params(48),
        name="forward",
        cost_estimate=cost(30),
    )(valid, far(z), far(wp), sums, gain, shift, slope, mslope, far(w))


def as_column(row):
    n = row.shape[1]
    same = lax.broadcasted_iota(jnp.int32, (n, n), 0) == lax.broadcasted_iota(jnp.int32, (n, n), 1)
    return jnp.sum(jnp.where(same, jnp.broadcast_to(row, (n, n)), 0.0), axis=1, keepdims=True)


def as_row(col):
    n = col.shape[0]
    same = lax.broadcasted_iota(jnp.int32, (n, n), 0) == lax.broadcasted_iota(jnp.int32, (n, n), 1)
    return jnp.sum(jnp.where(same, jnp.broadcast_to(col, (n, n)), 0.0), axis=0, keepdims=True)


def head_kernel(
    valid_ref, labels_ref, v_ref, st_ref, cnt_ref, gain_ref, shift_ref, slope_ref, hw_ref, hb_ref,
    dy_ref, copies_ref, misc_ref, st3_ref,
):
    step = pl.program_id(0)
    tile, hid = v_ref.shape
    classes = hw_ref.shape[0]
    padded = -(-classes // 16) * 16
    mask = row_mask(valid_ref, step, tile, 1)
    count = count_of(cnt_ref)

    @pl.when(step == 0)
    def _():
        st3_ref[...] = jnp.zeros_like(st3_ref)
        misc_ref[...] = jnp.zeros_like(misc_ref)

    sums = jnp.sum(st_ref[...], axis=0)
    mean = sums[0:1, :] / count
    rstd = lax.rsqrt(sums[1:2, :] / count - mean * mean + EPS)
    s = slope_ref[...]
    zn = (v_ref[...] - mean) * rstd
    y = gain_ref[...] * zn + shift_ref[...]
    e1 = 1.0 + jnp.exp(jnp.minimum(y, 20.0))
    sp = jnp.maximum(jnp.log(e1), y)
    w = s * y + (1.0 - s) * sp
    ws = split(w)
    hw = hw_ref[...]
    if padded > classes:
        hw = jnp.concatenate([hw, jnp.zeros((padded - classes, hid), F32)], axis=0)
    hh, hl = split(hw)
    dot = functools.partial(lax.dot_general, dimension_numbers=NT, preferred_element_type=F32)
    both = dot(jnp.concatenate([hh, hl], axis=0), ws[0])
    logits = both[:padded] + both[padded:] + dot(hh, ws[1])
    logits = logits[:classes] + as_column(hb_ref[...])
    peak = jnp.max(logits, axis=0, keepdims=True)
    ex = jnp.exp(logits - peak)
    tot = jnp.sum(ex, axis=0, keepdims=True)
    per = tile // LANES
    lab = jnp.concatenate([labels_ref[pl.ds(step * per + k, 1), :] for k in range(per)], axis=1)
    hit = lab == lax.broadcasted_iota(jnp.int32, (classes, tile), 0)
    picked = jnp.sum(jnp.where(hit, logits, 0.0), axis=0, keepdims=True)
    loss = jnp.sum(jnp.where(mask, peak + jnp.log(tot) - picked, 0.0))
    dl = jnp.where(mask, (ex / tot - hit.astype(F32)) / count, 0.0)
    bias = as_row(jnp.sum(dl, axis=1, keepdims=True))
    if padded > classes:
        dl = jnp.concatenate([dl, jnp.zeros((padded - classes, tile), F32)], axis=0)
    dh, dlo = split(dl)
    dot = functools.partial(lax.dot_general, dimension_numbers=NN, preferred_element_type=F32)
    both = dot(jnp.concatenate([dh, dlo], axis=0), ws[0])
    hwg = both[:padded] + both[padded:] + dot(dh, ws[1])
    misc_ref[0:classes, :] += hwg[:classes]
    misc_ref[classes : classes + 1, 0:classes] += bias
    misc_ref[classes : classes + 1, LANES : 2 * LANES] += jnp.broadcast_to(loss, (1, LANES))
    dw = lax.dot_general(
        jnp.concatenate([dh, dlo, dh], axis=0),
        jnp.concatenate([hh, hh, hl], axis=0),
        TN,
        preferred_element_type=F32,
    )
    dy = dw * (1.0 - (1.0 - s) / e1)
    dy_ref[...] = dy
    row = lambda t: jnp.sum(t, axis=0, keepdims=True)
    misc_ref[classes + 1 : classes + 2, :] += row(dw * (y - sp))
    st3_ref[0:1, :] += row(dy)
    st3_ref[1:2, :] += row(dy * zn)

    @pl.when(step == pl.num_programs(0) - 1)
    def _():
        copies_ref[...] = jnp.broadcast_to(st3_ref[...][None], copies_ref.shape)


def head(valid, labels, v, st2, st, gain, shift, slope, hw, hb, tile):
    rows, hid = v.shape
    by = lambda n: pl.BlockSpec((tile, n), lambda i: (i, 0))
    misc = -(-(hw.shape[0] + 2) // 8) * 8
    return pl.pallas_call(
        head_kernel,
        grid=(rows // tile,),
        in_specs=[whole(valid), whole(labels), by(hid)]
        + [whole(t) for t in (st2, st, gain, shift, slope, hw, hb)],
        out_specs=[
            by(hid),
            whole(st2),
            pl.BlockSpec((misc, hid), lambda i: (0, 0)),
        ],
        out_shape=[
            pltpu.HBM((rows, hid), F32),
            jax.ShapeDtypeStruct(st2.shape, F32),
            jax.ShapeDtypeStruct((misc, hid), F32),
        ],
        scratch_shapes=[pltpu.VMEM((2, hid), F32)],
        compiler_params=params(24),
        name="head",
        cost_estimate=cost(9),
    )(valid, labels, far(v), st2, st, gain, shift, slope, hw, hb)


def mix_product(parts, half_ref, g_ref, uh_ref, ul_ref, m_ref):
    mix = uh_ref.shape[1]
    some, n = g_ref.shape[0] // 2, g_ref.shape[1]

    @pl.when(pl.program_id(0) == 0)
    def _():
        m_ref[...] = jnp.zeros_like(m_ref)
        for h in range(some):
            g = g_ref[half_ref[0] * some + h]
            at = mix + h * n // 4
            m_ref[at : at + n // 4, :] = jnp.concatenate(
                [g[q * n // 4 : (q + 1) * n // 4] for q in range(4)], axis=1
            )

    ahead = parts[0][1]()
    for k, (rows, _) in enumerate(parts):
        dvs = ahead
        if k + 1 < len(parts):
            ahead = parts[k + 1][1]()
        hid = dvs[0].shape[1]
        for h in range(uh_ref.shape[1] // hid):
            cols = slice(h * hid, (h + 1) * hid)
            m_ref[cols, :] += dot3((uh_ref[rows, cols], ul_ref[rows, cols]), dvs, TN)


def mix_first_kernel(
    half_ref, valid_ref, dy_ref, v_ref, st2_ref, cnt_ref, st3_ref, gain_ref, g_ref, uh_ref, ul_ref,
    m_ref, dvh_ref, dvl_ref, st3_out,
):
    step = pl.program_id(0)
    tile = dy_ref.shape[0]
    mask = row_mask(valid_ref, step, tile)
    count = count_of(cnt_ref)
    st2 = jnp.sum(st2_ref[...], axis=0)
    st3 = jnp.sum(st3_ref[...], axis=0)
    mean = st2[0:1, :] / count
    rstd = lax.rsqrt(st2[1:2, :] / count - mean * mean + EPS)
    a = LN2 * gain_ref[...] * rstd
    c1 = a * st3[0:1, :] / count
    c2 = a * st3[1:2, :] / count

    @pl.when(step == 0)
    def _():
        st3_out[...] = st3

    def dv(rows):
        zn = (v_ref[rows, :] - mean) * rstd
        dvs = split(jnp.where(mask[rows], a * dy_ref[rows, :] - (c1 + zn * c2), 0.0))
        dvh_ref[rows, :], dvl_ref[rows, :] = dvs
        return dvs

    parts = [slice(k, k + MIX_SUB) for k in range(0, tile, MIX_SUB)]
    mix_product([(rows, functools.partial(dv, rows)) for rows in parts], half_ref, g_ref, uh_ref, ul_ref, m_ref)


def mix_second_kernel(half_ref, dvh_ref, dvl_ref, g_ref, uh_ref, ul_ref, m_ref):
    mix_product([(slice(None), lambda: (dvh_ref[...], dvl_ref[...]))], half_ref, g_ref, uh_ref, ul_ref, m_ref)


def mix_back(half, valid, dy, v, st2, st, st3, gain, g, uh, ul, extra, tile):
    rows, hid = dy.shape
    part = uh.shape[1] // 2
    by = lambda n: pl.BlockSpec((tile, n), lambda i, half: (i, 0))
    return pl.pallas_call(
        mix_first_kernel,
        grid_spec=pltpu.PrefetchScalarGridSpec(
            num_scalar_prefetch=1,
            grid=(rows // tile,),
            in_specs=[whole(valid), by(hid), by(hid)]
            + [whole(t) for t in (st2, st, st3, gain, g)]
            + [pl.BlockSpec((tile, part), lambda i, half: (i, half[0]))] * 2,
            out_specs=[pl.BlockSpec((part + extra, hid), lambda i, half: (0, 0)), by(hid), by(hid)]
            + [pl.BlockSpec((2, hid), lambda i, half: (0, 0))],
        ),
        out_shape=[
            jax.ShapeDtypeStruct((part + extra, hid), F32),
            pltpu.HBM((rows, hid), BF16),
            pltpu.HBM((rows, hid), BF16),
            jax.ShapeDtypeStruct((2, hid), F32),
        ],
        compiler_params=params(28),
        name="mix_back",
        cost_estimate=cost(14),
    )(half, valid, far(dy), far(v), st2, st, st3, gain, g, far(uh), far(ul))


def mix_back_rest(half, dvh, dvl, g, uh, ul, extra, tile):
    rows, hid = dvh.shape
    part = uh.shape[1] // 2
    by = lambda n: pl.BlockSpec((tile, n), lambda i, half: (i, 0))
    return pl.pallas_call(
        mix_second_kernel,
        grid_spec=pltpu.PrefetchScalarGridSpec(
            num_scalar_prefetch=1,
            grid=(rows // tile,),
            in_specs=[by(hid), by(hid), whole(g)]
            + [pl.BlockSpec((tile, part), lambda i, half: (i, half[0]))] * 2,
            out_specs=pl.BlockSpec((part + extra, hid), lambda i, half: (0, 0)),
        ),
        out_shape=jax.ShapeDtypeStruct((part + extra, hid), F32),
        compiler_params=params(28),
        name="mix_back_rest",
        cost_estimate=cost(12),
    )(half, far(dvh), far(dvl), g, far(uh), far(ul))


def hop_kernel(
    h, in_w, x_ref, wp_ref, coef_ref, dvh_ref, dvl_ref, mwh_ref, mwl_ref,
    dx_ref, bw_ref, sums_ref,
):
    step = pl.program_id(0)
    n = wp_ref.shape[1] // 3
    tile = x_ref.shape[1]

    @pl.when(step == 0)
    def _():
        bw_ref[...] = jnp.zeros_like(bw_ref)
        sums_ref[...] = jnp.zeros_like(sums_ref)

    a, b, s1, s2 = (coef_ref[0, k : k + 1, :] for k in range(4))
    xall = stack3(hop_rows(x_ref, h % (x_ref.shape[0] // in_w), in_w, 1.0))
    wp = wp_ref[0]
    wh, wl = split((wp[:n].astype(F32) + wp[2 * n :].astype(F32)) * a)
    whl = jnp.concatenate([wh, wl], axis=0)
    dot = functools.partial(lax.dot_general, preferred_element_type=F32)
    row = lambda t: jnp.sum(t, axis=0, keepdims=True)
    sums = [0.0] * 2
    parts = [slice(k, k + SUB) for k in range(0, tile, SUB)]

    def products(rs):
        y = dot(xall[:, rs], wp, TN)
        return y, dot3((dvh_ref[rs, :], dvl_ref[rs, :]), (mwh_ref[...], mwl_ref[...]), NT)

    def middle(rs, z, du):
        y = z * a + b
        e = 1.0 + jnp.exp2(jnp.minimum(y, 30.0))
        j = jnp.maximum(s1 * y + (LOG2E * (1.0 - s1)) * jnp.log(e), y)
        dj = du * (1.0 - (1.0 - s2) / (1.0 + jnp.exp2(j)))
        dy = dj * (1.0 - (1.0 - s1) / e)
        for q, t in enumerate((dj * (y - j), du * j)):
            sums[q] = sums[q] + row(t)
        return split(dy)

    def results(rs, dys):
        dh, dl = dys
        xs = xall[: 2 * n, rs]
        both = dot(xs, dh, NN)
        bw_ref[...] += both[:n] + both[n:] + dot(xs[:n], dl, NN)
        both = dot(whl, dh, NT)
        dx_ref[:, rs] = both[:n] + both[n:] + dot(wh, dl, NT)

    now = products(parts[0])
    before = None
    for k, rs in enumerate(parts):
        ahead = products(parts[k + 1]) if k + 1 < len(parts) else None
        if before is not None:
            results(parts[k - 1], before)
        before = middle(rs, *now)
        now = ahead
    results(parts[-1], before)
    for q in range(2):
        sums_ref[q : q + 1, :] += sums[q]


def hop_back(h, in_w, x, wp, coef, dvh, dvl, mwh, mwl, tile):
    width, rows = x.shape
    some = 2 * in_w if width % (2 * in_w) == 0 and in_w % 4 == 0 else width
    at = h * in_w // some
    hid = dvh.shape[1]
    n = wp.shape[1] // 3
    by = lambda w, k=0: pl.BlockSpec((tile, w), lambda i: (i, k))
    block = lambda r: pl.BlockSpec((r, hid), lambda i: (h, 0))
    return pl.pallas_call(
        functools.partial(hop_kernel, h, in_w),
        grid=(rows // tile,),
        in_specs=[
            pl.BlockSpec((some, tile), lambda i: (at, i)),
            pl.BlockSpec((1, 3 * n, hid), lambda i: (h, 0, 0)),
            pl.BlockSpec((1, 8, hid), lambda i: (h, 0, 0)),
        ]
        + [by(hid), by(hid), block(hid), block(hid)],
        out_specs=[
            pl.BlockSpec((n, tile), lambda i: (0, i)),
            pl.BlockSpec((n, hid), lambda i: (0, 0)),
            pl.BlockSpec((2, hid), lambda i: (0, 0)),
        ],
        out_shape=[
            pltpu.HBM((n, rows), F32),
            jax.ShapeDtypeStruct((n, hid), F32),
            jax.ShapeDtypeStruct((2, hid), F32),
        ],
        compiler_params=params(20),
        name=f"hop_back_{h}",
        cost_estimate=cost(11),
    )(far(x), far(wp), coef, far(dvh), far(dvl), far(mwh), far(mwl))


def assemble_kernel(first_ref, own_ref, got_ref, own_g_ref, got_g_ref, w_ref, m_ref, uu_ref, g_ref):
    mine = (pl.program_id(0) // 2) == first_ref[0]
    m = jnp.where(mine, own_ref[...], got_ref[...])
    m_ref[...] = m
    ones = jnp.ones((8, m.shape[1]), BF16)
    dot = functools.partial(lax.dot_general, dimension_numbers=NT, preferred_element_type=F32)
    hi, lo = split(m * w_ref[...])
    uu_ref[0] = dot(ones, hi) + dot(ones, lo)

    @pl.when(pl.program_id(0) % 2 == 0)
    def _():
        g_ref[...] = jnp.where(mine, own_g_ref[...], got_g_ref[...])


def assemble(first, own, got, w):
    rows, hid = w.shape
    block = rows // 4
    extra = own.shape[0] - rows // 2
    half = pl.BlockSpec((block, hid), lambda i, first: (i % 2, 0))
    tail = pl.BlockSpec((extra, hid), lambda i, first: (rows // 2 // extra, 0))
    by = pl.BlockSpec((block, hid), lambda i, first: (i, 0))
    return pl.pallas_call(
        assemble_kernel,
        grid_spec=pltpu.PrefetchScalarGridSpec(
            num_scalar_prefetch=1,
            grid=(4,),
            in_specs=[half, half, tail, tail, by],
            out_specs=[
                by,
                pl.BlockSpec((1, 8, block), lambda i, first: (i, 0, 0)),
                pl.BlockSpec((extra, hid), lambda i, first: (i // 2, 0)),
            ],
        ),
        out_shape=[
            jax.ShapeDtypeStruct((rows, hid), F32),
            jax.ShapeDtypeStruct((4, 8, block), F32),
            jax.ShapeDtypeStruct((2 * extra, hid), F32),
        ],
        compiler_params=params(20),
        name="assemble",
        cost_estimate=cost(5),
    )(first, own, got, own, got, far(w))


def pack_kernel(misc_ref, *refs):
    hops = (len(refs) - 1) // 2
    n = refs[0].shape[0]
    out_ref = refs[-1]
    base = hops * n
    at = base + misc_ref.shape[0]
    for h in range(hops):
        out_ref[h * n : (h + 1) * n, :] = refs[h][...]
        out_ref[at + 2 * h : at + 2 * h + 2, :] = refs[hops + h][...]
    out_ref[base:at, :] = misc_ref[...]
    used = at + 2 * hops
    if used < out_ref.shape[0]:
        out_ref[used:, :] = jnp.zeros((out_ref.shape[0] - used, out_ref.shape[1]), F32)


def pack(misc, bws, sums, unit):
    used = len(bws) * (bws[0].shape[0] + 2) + misc.shape[0]
    return pl.pallas_call(
        pack_kernel,
        out_shape=jax.ShapeDtypeStruct((-(-used // unit) * unit, misc.shape[1]), F32),
        compiler_params=params(24),
        name="pack",
        cost_estimate=cost(3),
    )(misc, *bws, *sums)


def fix_kernel(in_w, classes, misc, valid_ref, x_ref, p_ref, uu_ref, g_ref, st_ref, gain_ref, slope_ref, mslope_ref, wp_ref, *refs):
    step = pl.program_id(0)
    hops, hid = gain_ref.shape
    tile = x_ref.shape[1]
    n = wp_ref.shape[1] // 3
    dxs, rest = refs[:hops], refs[hops:]
    dx_ref, bw_ref, gain_out, shift_out, slope_out, mslope_out, oslope_out, hw_out, hb_out, loss_out, q_ref = rest
    base = hops * n
    mask = row_mask(valid_ref, step, tile, 1)

    @pl.when(step == 0)
    def _():
        count = count_of(st_ref)
        hw_out[...] = p_ref[base : base + classes, :]
        hb_out[...] = p_ref[base + classes : base + classes + 1, :classes]
        loss_out[...] = p_ref[base + classes : base + classes + 1, LANES : LANES + 1] / count
        oslope_out[...] = p_ref[base + classes + 1 : base + classes + 2, :]
        for h in range(hops):
            cols = slice(h * hid, (h + 1) * hid)
            mean, rstd = norm_of(st_ref, cols)
            gain = gain_ref[h : h + 1, :]
            wh, wl = wp_ref[h, :n, :], wp_ref[h, 2 * n :, :]
            w = wh.astype(F32) + wl.astype(F32)
            raw = p_ref[h * n : (h + 1) * n, :]
            total = LOG2E * raw[in_w : in_w + 1, :]
            gsum = rstd * (LOG2E * jnp.sum(w * raw, axis=0, keepdims=True) - mean * total)
            gain_out[h : h + 1, :] = gsum
            shift_out[h : h + 1, :] = total
            at = base + misc + 2 * h
            slope_out[h : h + 1, :] = p_ref[at : at + 1, :] / (1.0 - slope_ref[h : h + 1, :])
            uu = uu_ref[h, 0:1, :]
            mslope_out[h : h + 1, :] = (p_ref[at + 1 : at + 2, :] - uu) / (1.0 - mslope_ref[h : h + 1, :])
            a = gain * rstd / count
            c2 = a * gsum * rstd
            k0 = a * total - mean * c2
            wc = w * c2
            mask_row = lax.broadcasted_iota(jnp.int32, (n, hid), 0) == in_w
            wc = split(jnp.where(mask_row, k0, wc))
            q_ref[h, :, :n] = dot3((wh, wl), wc, NT)
            k = h // (hops // 2) * (g_ref.shape[0] // 2) + h % (hops // 2) * n // 4
            g = jnp.concatenate(
                [g_ref[k : k + n // 4, q * LANES : q * LANES + n] for q in range(4)], axis=0
            )
            bw = raw * (LOG2E * gain * rstd) - dot3(split(g), wc)
            bw_ref[:, h, :] = bw[:in_w]

    for h in range(hops):
        x = jnp.where(mask, hop_rows(x_ref, h, in_w, 1.0), 0.0)
        fix = dot3(split(q_ref[h, :, :n]), split(x))
        dx_ref[h * in_w : (h + 1) * in_w, :] = (dxs[h][...] - fix)[:in_w]


def fix(valid, x, packed, uu, g, st, gain, slope, mslope, wp, dxs, in_w, classes, misc, tile):
    width, rows = x.shape
    hops, hid = gain.shape
    n = wp.shape[1] // 3
    cols = lambda r: pl.BlockSpec((r, tile), lambda i: (0, i))
    shapes = ((in_w, hops, hid),) + ((hops, hid),) * 4 + ((1, hid), (classes, hid), (1, classes), (1, 1))
    return pl.pallas_call(
        functools.partial(fix_kernel, in_w, classes, misc),
        grid=(rows // tile,),
        in_specs=[whole(valid), cols(width)]
        + [whole(t) for t in (packed, uu, g, st, gain, slope, mslope, wp)]
        + [cols(n)] * hops,
        out_specs=[cols(width)] + [pl.BlockSpec(s, lambda i, s=s: (0,) * len(s)) for s in shapes],
        out_shape=[jax.ShapeDtypeStruct(s, F32) for s in ((width, rows),) + shapes],
        scratch_shapes=[pltpu.VMEM((hops, n, LANES), F32)],
        compiler_params=params(24),
        name="fix",
        cost_estimate=cost(8),
    )(valid, far(x), packed, uu, g, st, gain, slope, mslope, far(wp), *[far(d) for d in dxs])


def flip(v, axis, size, k):
    return lax.ppermute(v, axis, [(i, i ^ k) for i in range(size)])


def exchange(copies):
    return lax.all_to_all(copies, ("dp", "bucket"), 0, 0, tiled=True)


def pieces(v, n):
    size = v.shape[0] // n
    return [v[i * size : (i + 1) * size] for i in range(n)]


def take(v, index, n):
    size = v.shape[0] // n
    return lax.dynamic_slice_in_dim(v, index * size, size, 0)


def merge(v, got, axis, size, k):
    bit = lax.axis_index(axis) // k % 2
    return jnp.where(bit == 0, jnp.concatenate([v, got], 0), jnp.concatenate([got, v], 0))


def halve(v, axis, size, k):
    bit = lax.axis_index(axis) // k % 2
    return v, flip(take(v, 1 - bit, 2), axis, size, k)


def kept(v, got, axis, size, k):
    return take(v, lax.axis_index(axis) // k % 2, 2) + got


def spread(v, axis, size, k):
    me = lax.axis_index(axis) // k
    return tuple(flip(take(v, me ^ i, 4), axis, size, k * i) if i else take(v, me, 4) for i in range(4))


def collect(v, axis, size, k):
    return (v,) + tuple(flip(v, axis, size, k * i) for i in range(1, 4))


def in_order(parts, axis, k):
    low, high = lax.axis_index(axis) // k % 2, lax.axis_index(axis) // (2 * k) % 2
    pair = lambda a, b: jnp.where(low == 0, jnp.concatenate([a, b], 0), jnp.concatenate([b, a], 0))
    near, far = pair(parts[0], parts[1]), pair(parts[2], parts[3])
    return jnp.where(high == 0, jnp.concatenate([near, far], 0), jnp.concatenate([far, near], 0))


def total(parts):
    if len(parts) == 4:
        return (parts[0] + parts[1]) + (parts[2] + parts[3])
    return functools.reduce(jnp.add, parts)


def sum_steps(parts, sizes, large, within):
    dp, bucket = sizes["dp"], sizes["bucket"]
    across = [("dp", dp, 1 << i) for i in range(1, dp.bit_length() - 1)]
    square = len(across) == 2 and not large
    line = [("bucket", bucket, 1 << i) for i in range(bucket.bit_length() - 1)]
    core = ("dp", dp, 1)
    within = within and dp > 1
    if within:
        parts = [kept(*(yield halve(total(parts), *core)), *core)]
    if square:
        parts = yield spread(total(parts), "dp", dp, 2)
    elif across:
        a, b = across[0], across[-1]
        bits = [lax.axis_index("dp") // s[2] % 2 for s in (a, b)]
        quarter = lambda i: functools.reduce(jnp.add, [take(p, i, 4) for p in parts])
        gone = flip(quarter(1 - bits[0]), *a), flip(quarter(3 - bits[1]), *b)
        parts, got = yield tuple(parts), gone
        top, bottom = quarter(bits[0]) + got[0], quarter(2 + bits[1]) + got[1]
        for a, b in list(zip(across, across[::-1]))[1:]:
            got = yield halve(top, *a), halve(bottom, *b)
            top, bottom = kept(*got[0], *a), kept(*got[1], *b)
        parts = [jnp.concatenate([top, bottom], 0)]
    if bucket == 4:
        parts = yield spread(total(parts), "bucket", bucket, 1)
        parts = yield collect(total(parts), "bucket", bucket, 1)
        v = in_order(parts, "bucket", 1)
    else:
        v = total(parts)
        for s in line:
            v = kept(*(yield halve(v, *s)), *s)
        for s in line[::-1]:
            parts = yield v, flip(v, *s)
            v = merge(*parts, *s)
    if square:
        v = in_order((yield collect(v, "dp", dp, 2)), "dp", 2)
    elif across:
        top, bottom = pieces(v, 2)
        for a, b in zip(across[::-1], across):
            got = yield top, flip(top, *a), bottom, flip(bottom, *b)
            top, bottom = merge(*got[:2], *a), merge(*got[2:], *b)
        v = jnp.concatenate([top, bottom], 0)
    if within:
        v = merge(*(yield v, flip(v, *core)), *core)
    return v


class Steps:
    def __init__(self, steps):
        self.steps, self.state, self.done, self.value = steps, None, False, None

    def step(self):
        if not self.done:
            try:
                self.state = self.steps.send(self.state)
            except StopIteration as end:
                self.done, self.value, self.state = True, end.value, None


def per_device(sizes, feats, labels, valid, branch_w, branch_gain, branch_shift, branch_slope, mix_slope,
               mix_w, mix_gain, mix_shift, out_slope, head_w, head_bias):
    rows, width = feats.shape
    hops, in_w, hid = branch_w.shape
    classes = head_w.shape[1]
    mix = hops * hid
    valid = valid.reshape(rows // LANES, LANES)
    labels = labels.reshape(rows // LANES, LANES)
    mslope = mix_slope.reshape(hops, hid)
    row = lambda t: t.reshape(1, -1)
    x = feats.T

    devices = sizes["dp"] * sizes["bucket"]
    g, sums, wp = gram(valid, x, branch_w.transpose(1, 0, 2), devices, TILES["gram"])
    sums = exchange(sums)
    z = project(x, wp, in_w, TILES["project"])
    uh, ul, v, st2, mwh, mwl, st, coef = forward(
        valid, z, wp, sums, branch_gain, branch_shift, branch_slope, mslope, mix_w, in_w, devices,
        TILES["forward"],
    )
    st2 = exchange(st2)
    dy2, st3, misc = head(
        valid, labels, v, st2, st, row(mix_gain), row(mix_shift), row(out_slope), head_w.T, row(head_bias),
        TILES["head"],
    )
    st3 = exchange(st3)
    core = lax.axis_index("dp") % 2
    unit = max(devices, 64)
    extra = -(-(hops // 2 * g.shape[1] // 4) // unit) * unit
    half = lambda i: jnp.reshape(i, (1,)).astype(jnp.int32)
    away, dvh, dvl, st3 = mix_back(
        half(1 - core), valid, dy2, v, st2, st, st3, row(mix_gain), g, uh, ul, extra, TILES["mix"]
    )
    within = sizes["dp"] > 1
    got = flip(away, "dp", sizes["dp"], 1) if within else None
    m = mix_back_rest(half(core), dvh, dvl, g, uh, ul, extra, TILES["mix"])
    if within:
        m, got, x = lax.optimization_barrier((m, got, x))
        first = Steps(sum_steps((m, got), sizes, True, False))
    else:
        first = Steps(sum_steps((jnp.concatenate([m, away], 0),), sizes, True, False))
    dxs, bws, sums = [], [], []
    for h in range(hops):
        first.step()
        dx, bw, s = hop_back(
            h, in_w, x, wp, coef, dvh, dvl, mwh, mwl, TILES["hop"],
        )
        dxs, bws, sums = dxs + [dx], bws + [bw], sums + [s]
        first.state, x, bws, sums = lax.optimization_barrier((first.state, x, bws, sums))
    packed = pack(misc, bws, sums, max(128, 2 * devices))
    last = Steps(sum_steps((packed,), sizes, False, True))
    first.step()
    last.step()
    last.step()
    first.state, last.state = lax.optimization_barrier((first.state, last.state))
    first.step()
    last.step()
    last.step()
    first.state, last.state = lax.optimization_barrier((first.state, last.state))
    while not first.done:
        first.step()
    m = first.value
    m, other = (m, flip(m, "dp", sizes["dp"], 1)) if within else pieces(m, 2)
    last.step()
    m, uu, g = assemble(half(core), m, other, mix_w)
    m, uu, last.state = lax.optimization_barrier((m, uu, last.state))
    while not last.done:
        last.step()
    packed = last.value
    d_x, bw, gain_grad, shift_grad, slope_grad, mslope_grad, oslope_grad, hw_grad, hb_grad, loss = fix(
        valid, x, packed, uu, g, st, branch_gain, branch_slope, mslope, wp, dxs, in_w, classes, misc.shape[0],
        TILES["fix"],
    )
    return (
        loss.reshape(()),
        d_x.T,
        bw.transpose(1, 0, 2),
        gain_grad,
        shift_grad,
        slope_grad,
        mslope_grad.reshape(mix),
        m,
        st3[1],
        st3[0],
        oslope_grad.reshape(hid),
        hw_grad.T,
        hb_grad.reshape(classes),
    )


def solution(mesh):
    sizes = {axis: mesh.shape[axis] for axis in ("dp", "bucket")}
    split_rows = P(("dp", "bucket"), None)
    in_specs = (split_rows, P(("dp", "bucket")), P(("dp", "bucket"))) + (P(),) * 11
    out_specs = (P(), split_rows) + (P(),) * 11
    return jax.shard_map(
        functools.partial(per_device, sizes),
        mesh=mesh,
        in_specs=in_specs,
        out_specs=out_specs,
        check_vma=False,
    )
```

```python
import functools

import jax
import jax.numpy as jnp
from jax import lax
from jax.experimental import pallas as pl
from jax.experimental.pallas import tpu as pltpu
from jax.sharding import PartitionSpec as P

EPS = 1e-05
F32 = jnp.float32
BF16 = jnp.bfloat16
LANES = 128
LOG2E = 1.4426950408889634
LN2 = 0.6931471805599453
TILES = {"gram": 2048, "project": 512, "forward": 512, "head": 1024, "mix": 512, "hop": 512, "fix": 1024}
PACK_STEPS = 2
SUB = 256
MIX_SUB = 256
NN = (((1,), (0,)), ((), ()))
NT = (((1,), (1,)), ((), ()))
TN = (((0,), (0,)), ((), ()))


def split(x):
    hi = x.astype(BF16)
    return hi, (x - hi.astype(F32)).astype(BF16)


def dot3(a, b, dims=NN):
    ah, al = a
    bh, bl = b
    dot = functools.partial(lax.dot_general, dimension_numbers=dims, preferred_element_type=F32)
    return dot(ah, bh) + (dot(ah, bl) + dot(al, bh))


def act2(y, slope, rest):
    return jnp.maximum(slope * y + rest * jnp.log(1.0 + jnp.exp2(jnp.minimum(y, 30.0))), y)


def cost(us):
    return pl.CostEstimate(flops=0, bytes_accessed=int(us * 3.69e6), transcendentals=0)


def params(mib):
    return pltpu.CompilerParams(vmem_limit_bytes=mib * 1024 * 1024)


def near(x):
    return pltpu.with_memory_space_constraint(x, pltpu.VMEM)


def far(x):
    return pltpu.with_memory_space_constraint(x, pltpu.HBM)


def whole(x, buffers=2):
    mode = {} if buffers == 2 else {"pipeline_mode": pl.Buffered(buffers)}
    return pl.BlockSpec(x.shape, lambda *_: (0,) * len(x.shape), **mode)


def row_mask(valid_ref, step, tile, axis=0):
    n = jnp.sum(valid_ref[...])
    shape = (tile, 1) if axis == 0 else (1, tile)
    return step * tile + lax.broadcasted_iota(jnp.int32, shape, axis) < n


def hop_rows(x_ref, h, in_w, extra=None):
    x = x_ref[h * in_w : (h + 1) * in_w, :]
    pad = -(-(in_w + 1) // 16) * 16 - in_w
    tail = jnp.zeros((pad, x.shape[1]), F32)
    if extra is not None:
        first = lax.broadcasted_iota(jnp.int32, tail.shape, 0) == 0
        tail = jnp.where(first, extra, 0.0)
    return jnp.concatenate([x, tail], axis=0)


def stack3(a):
    hi, lo = split(a)
    return jnp.concatenate([hi, lo, hi], axis=0)


def gram_kernel(in_w, valid_ref, x_ref, w_ref, g_ref, copies_ref, wp_ref):
    step = pl.program_id(0)
    tile = x_ref.shape[1]
    hops, hid = w_ref.shape[1:]
    copies = copies_ref.shape[0]
    mask = row_mask(valid_ref, step, tile, 1)

    @pl.when(step == 0)
    def _():
        g_ref[...] = jnp.zeros_like(g_ref)

    for h in range(hops):
        x = jnp.where(mask, hop_rows(x_ref, h, in_w, 1.0), 0.0)
        hi, lo = split(x)
        n = x.shape[0]
        dot = functools.partial(lax.dot_general, dimension_numbers=NT, preferred_element_type=F32)
        cross = dot(hi, lo)
        g_ref[h, :, :n] += dot(hi, hi) + (cross + cross.T)

    @pl.when(step == pl.num_programs(0) - 1)
    def _():
        for h in range(hops):
            n = g_ref.shape[1]
            w = w_ref[:, h, :]
            w = jnp.concatenate([w, jnp.zeros((n - in_w, hid), F32)], axis=0)
            ws = split(w)
            gw = dot3(split(g_ref[h, :, :n]), ws)
            squares = jnp.sum(w * gw, axis=0, keepdims=True)
            copies_ref[:, :, h * hid : (h + 1) * hid] = jnp.broadcast_to(squares[None], (copies, 1, hid))
            sums = g_ref[h, in_w : in_w + 1, :]
            at = hops * hid + h * LANES
            copies_ref[:, :, at : at + LANES] = jnp.broadcast_to(sums[None], (copies, 1, LANES))
            wp_ref[h] = jnp.concatenate([ws[0], ws[0], ws[1]], axis=0)


def gram(valid, x, w, copies, tile):
    width, rows = x.shape
    in_w, hops, hid = w.shape
    n = -(-(in_w + 1) // 16) * 16
    shapes = (hops, n, LANES), (copies, 1, hops * (hid + LANES)), (hops, 3 * n, hid)
    return pl.pallas_call(
        functools.partial(gram_kernel, in_w),
        grid=(rows // tile,),
        in_specs=[whole(valid), pl.BlockSpec((width, tile), lambda i: (0, i)), whole(w)],
        out_specs=[pl.BlockSpec(s, lambda i, s=s: (0,) * len(s)) for s in shapes],
        out_shape=[jax.ShapeDtypeStruct(s, F32) for s in shapes[:2]] + [pltpu.HBM(shapes[2], BF16)],
        compiler_params=params(32),
        name="gram",
        cost_estimate=cost(5),
    )(far(valid), far(x), far(w))


def project_kernel(in_w, x_ref, wp_ref, z_ref):
    hid = wp_ref.shape[2]
    for h in range(wp_ref.shape[0]):
        xs = stack3(hop_rows(x_ref, h, in_w))
        cols = slice(h * hid, (h + 1) * hid)
        z_ref[:, cols] = lax.dot_general(xs, wp_ref[h], TN, preferred_element_type=F32)


def project(x, wp, in_w, tile):
    width, rows = x.shape
    hops, _, hid = wp.shape
    return pl.pallas_call(
        functools.partial(project_kernel, in_w),
        grid=(rows // tile,),
        in_specs=[pl.BlockSpec((width, tile), lambda i: (0, i)), whole(wp, 1)],
        out_specs=pl.BlockSpec((tile, hops * hid), lambda i: (i, 0)),
        out_shape=pltpu.HBM((rows, hops * hid), F32),
        compiler_params=params(24),
        name="project",
        cost_estimate=cost(9),
    )(far(x), far(wp))


def count_of(st_ref):
    return st_ref[0:1, st_ref.shape[1] - 1 :]


def norm_of(st_ref, cols):
    count = count_of(st_ref)
    mean = st_ref[0:1, cols] / count
    var = st_ref[1:2, cols] / count - mean * mean
    return mean, lax.rsqrt(var + EPS)


def scale_of(st_ref, cols, gain_ref, shift_ref, h):
    mean, rstd = norm_of(st_ref, cols)
    a = gain_ref[h : h + 1, :] * rstd
    return LOG2E * a, LOG2E * (shift_ref[h : h + 1, :] - mean * a)


def forward_kernel(
    in_w, valid_ref, z_ref, wp_ref, all_ref, gain_ref, shift_ref, slope_ref, mslope_ref, w_ref,
    uh_ref, ul_ref, v_ref, copies_ref, wh_out, wl_out, st_ref, coef_ref,
    st2_ref, wh_ref, wl_ref,
):
    step = pl.program_id(0)
    tile = z_ref.shape[0]
    hops, hid = gain_ref.shape
    mask = row_mask(valid_ref, step, tile)

    @pl.when(step == 0)
    def _():
        st2_ref[...] = jnp.zeros_like(st2_ref)
        sums = jnp.sum(all_ref[...], axis=0)
        n = wp_ref.shape[1] // 3
        for h in range(hops):
            rows = slice(h * hid, (h + 1) * hid)
            wh_ref[rows, :], wl_ref[rows, :] = split(w_ref[rows, :])
            at = hops * hid + h * LANES
            xm = jnp.broadcast_to(sums[:, at : at + n], (8, n))
            st_ref[0:1, rows] = dot3(split(xm), (wp_ref[h, :n, :], wp_ref[h, 2 * n :, :]))[0:1, :]
            st_ref[1:2, rows] = sums[:, rows]
        at = hops * hid + in_w
        st_ref[:, hops * hid :] = jnp.broadcast_to(sums[:, at : at + 1], (2, LANES))
        for h in range(hops):
            a, b = scale_of(st_ref, slice(h * hid, (h + 1) * hid), gain_ref, shift_ref, h)
            coef_ref[h] = jnp.concatenate(
                [a, b, slope_ref[h : h + 1, :], mslope_ref[h : h + 1, :], jnp.zeros((4, hid), F32)], axis=0
            )

    def activate(h, z):
        cols = slice(h * hid, (h + 1) * hid)
        a, b = scale_of(st_ref, cols, gain_ref, shift_ref, h)
        s1 = slope_ref[h : h + 1, :]
        s2 = mslope_ref[h : h + 1, :]
        j = act2(z * a + b, s1, LOG2E * (1.0 - s1))
        u = act2(j, s2, LOG2E * (1.0 - s2))
        us = split(u)
        uh_ref[:, cols], ul_ref[:, cols] = us
        return us

    def mix(h, us):
        cols = slice(h * hid, (h + 1) * hid)
        part = dot3(us, (wh_ref[cols, :], wl_ref[cols, :]))
        v_ref[...] = part if h == 0 else v_ref[...] + part

    before = None
    for h in range(hops):
        if before is not None:
            mix(h - 1, before)
        before = activate(h, z_ref[:, h * hid : (h + 1) * hid])
    mix(hops - 1, before)
    piece = pl.ds(pl.multiple_of(step * wh_out.shape[0], wh_out.shape[0]), wh_out.shape[0])
    wh_out[...], wl_out[...] = wh_ref[piece, :], wl_ref[piece, :]
    v = v_ref[...]
    v = LN2 * v
    v_ref[...] = v
    vm = jnp.where(mask, v, 0.0)
    st2_ref[0:1, :] += jnp.sum(vm, axis=0, keepdims=True)
    st2_ref[1:2, :] += jnp.sum(vm * vm, axis=0, keepdims=True)

    @pl.when(step == pl.num_programs(0) - 1)
    def _():
        copies_ref[...] = jnp.broadcast_to(st2_ref[...][None], copies_ref.shape)


def forward(valid, z, wp, sums, gain, shift, slope, mslope, w, in_w, copies, tile):
    rows = z.shape[0]
    mix, hid = w.shape
    by = lambda n: pl.BlockSpec((tile, n), lambda i: (i, 0))
    return pl.pallas_call(
        functools.partial(forward_kernel, in_w),
        grid=(rows // tile,),
        in_specs=[whole(valid), by(mix)]
        + [whole(t, 1) for t in (wp, sums, gain, shift, slope, mslope, w)],
        out_specs=[by(mix)] * 2
        + [by(hid), pl.BlockSpec((copies, 2, hid), lambda i: (0, 0, 0))]
        + [pl.BlockSpec((mix * tile // rows, hid), lambda i: (i, 0))] * 2
        + [pl.BlockSpec((2, mix + LANES), lambda i: (0, 0))]
        + [pl.BlockSpec((mix // hid, 8, hid), lambda i: (0, 0, 0))],
        out_shape=[
            pltpu.HBM((rows, mix), BF16),
            pltpu.HBM((rows, mix), BF16),
            pltpu.HBM((rows, hid), F32),
            jax.ShapeDtypeStruct((copies, 2, hid), F32),
            pltpu.HBM((mix, hid), BF16),
            pltpu.HBM((mix, hid), BF16),
            jax.ShapeDtypeStruct((2, mix + LANES), F32),
            jax.ShapeDtypeStruct((mix // hid, 8, hid), F32),
        ],
        scratch_shapes=[
            pltpu.VMEM((2, hid), F32),
            pltpu.VMEM((mix, hid), BF16),
            pltpu.VMEM((mix, hid), BF16),
        ],
        compiler_params=params(48),
        name="forward",
        cost_estimate=cost(30),
    )(valid, far(z), far(wp), sums, gain, shift, slope, mslope, far(w))


def as_column(row):
    n = row.shape[1]
    same = lax.broadcasted_iota(jnp.int32, (n, n), 0) == lax.broadcasted_iota(jnp.int32, (n, n), 1)
    return jnp.sum(jnp.where(same, jnp.broadcast_to(row, (n, n)), 0.0), axis=1, keepdims=True)


def as_row(col):
    n = col.shape[0]
    same = lax.broadcasted_iota(jnp.int32, (n, n), 0) == lax.broadcasted_iota(jnp.int32, (n, n), 1)
    return jnp.sum(jnp.where(same, jnp.broadcast_to(col, (n, n)), 0.0), axis=0, keepdims=True)


def head_kernel(
    valid_ref, labels_ref, v_ref, st_ref, cnt_ref, gain_ref, shift_ref, slope_ref, hw_ref, hb_ref,
    dy_ref, copies_ref, misc_ref, st3_ref,
):
    step = pl.program_id(0)
    tile, hid = v_ref.shape
    classes = hw_ref.shape[0]
    padded = -(-classes // 16) * 16
    mask = row_mask(valid_ref, step, tile, 1)
    count = count_of(cnt_ref)

    @pl.when(step == 0)
    def _():
        st3_ref[...] = jnp.zeros_like(st3_ref)
        misc_ref[...] = jnp.zeros_like(misc_ref)

    sums = jnp.sum(st_ref[...], axis=0)
    mean = sums[0:1, :] / count
    rstd = lax.rsqrt(sums[1:2, :] / count - mean * mean + EPS)
    s = slope_ref[...]
    zn = (v_ref[...] - mean) * rstd
    y = gain_ref[...] * zn + shift_ref[...]
    e1 = 1.0 + jnp.exp(jnp.minimum(y, 20.0))
    sp = jnp.maximum(jnp.log(e1), y)
    w = s * y + (1.0 - s) * sp
    ws = split(w)
    hw = hw_ref[...]
    if padded > classes:
        hw = jnp.concatenate([hw, jnp.zeros((padded - classes, hid), F32)], axis=0)
    hh, hl = split(hw)
    dot = functools.partial(lax.dot_general, dimension_numbers=NT, preferred_element_type=F32)
    both = dot(jnp.concatenate([hh, hl], axis=0), ws[0])
    logits = both[:padded] + both[padded:] + dot(hh, ws[1])
    logits = logits[:classes] + as_column(hb_ref[...])
    peak = jnp.max(logits, axis=0, keepdims=True)
    ex = jnp.exp(logits - peak)
    tot = jnp.sum(ex, axis=0, keepdims=True)
    per = tile // LANES
    lab = jnp.concatenate([labels_ref[pl.ds(step * per + k, 1), :] for k in range(per)], axis=1)
    hit = lab == lax.broadcasted_iota(jnp.int32, (classes, tile), 0)
    picked = jnp.sum(jnp.where(hit, logits, 0.0), axis=0, keepdims=True)
    loss = jnp.sum(jnp.where(mask, peak + jnp.log(tot) - picked, 0.0))
    dl = jnp.where(mask, (ex / tot - hit.astype(F32)) / count, 0.0)
    bias = as_row(jnp.sum(dl, axis=1, keepdims=True))
    if padded > classes:
        dl = jnp.concatenate([dl, jnp.zeros((padded - classes, tile), F32)], axis=0)
    dh, dlo = split(dl)
    dot = functools.partial(lax.dot_general, dimension_numbers=NN, preferred_element_type=F32)
    both = dot(jnp.concatenate([dh, dlo], axis=0), ws[0])
    hwg = both[:padded] + both[padded:] + dot(dh, ws[1])
    misc_ref[0:classes, :] += hwg[:classes]
    misc_ref[classes : classes + 1, 0:classes] += bias
    misc_ref[classes : classes + 1, LANES : 2 * LANES] += jnp.broadcast_to(loss, (1, LANES))
    dw = lax.dot_general(
        jnp.concatenate([dh, dlo, dh], axis=0),
        jnp.concatenate([hh, hh, hl], axis=0),
        TN,
        preferred_element_type=F32,
    )
    dy = dw * (1.0 - (1.0 - s) / e1)
    dy_ref[...] = dy
    row = lambda t: jnp.sum(t, axis=0, keepdims=True)
    misc_ref[classes + 1 : classes + 2, :] += row(dw * (y - sp))
    st3_ref[0:1, :] += row(dy)
    st3_ref[1:2, :] += row(dy * zn)

    @pl.when(step == pl.num_programs(0) - 1)
    def _():
        copies_ref[...] = jnp.broadcast_to(st3_ref[...][None], copies_ref.shape)


def head(valid, labels, v, st2, st, gain, shift, slope, hw, hb, tile):
    rows, hid = v.shape
    by = lambda n: pl.BlockSpec((tile, n), lambda i: (i, 0))
    misc = -(-(hw.shape[0] + 2) // 8) * 8
    return pl.pallas_call(
        head_kernel,
        grid=(rows // tile,),
        in_specs=[whole(valid), whole(labels), by(hid)]
        + [whole(t) for t in (st2, st, gain, shift, slope, hw, hb)],
        out_specs=[
            by(hid),
            whole(st2),
            pl.BlockSpec((misc, hid), lambda i: (0, 0)),
        ],
        out_shape=[
            pltpu.HBM((rows, hid), F32),
            jax.ShapeDtypeStruct(st2.shape, F32),
            jax.ShapeDtypeStruct((misc, hid), F32),
        ],
        scratch_shapes=[pltpu.VMEM((2, hid), F32)],
        compiler_params=params(24),
        name="head",
        cost_estimate=cost(9),
    )(valid, labels, far(v), st2, st, gain, shift, slope, hw, hb)


def mix_product(parts, half_ref, g_ref, uh_ref, ul_ref, m_ref):
    mix = uh_ref.shape[1]
    some, n = g_ref.shape[0] // 2, g_ref.shape[1]

    @pl.when(pl.program_id(0) == 0)
    def _():
        m_ref[...] = jnp.zeros_like(m_ref)
        for h in range(some):
            g = g_ref[half_ref[0] * some + h]
            at = mix + h * n // 4
            m_ref[at : at + n // 4, :] = jnp.concatenate(
                [g[q * n // 4 : (q + 1) * n // 4] for q in range(4)], axis=1
            )

    ahead = parts[0][1]()
    for k, (rows, _) in enumerate(parts):
        dvs = ahead
        if k + 1 < len(parts):
            ahead = parts[k + 1][1]()
        hid = dvs[0].shape[1]
        for h in range(uh_ref.shape[1] // hid):
            cols = slice(h * hid, (h + 1) * hid)
            m_ref[cols, :] += dot3((uh_ref[rows, cols], ul_ref[rows, cols]), dvs, TN)


def mix_first_kernel(
    half_ref, valid_ref, dy_ref, v_ref, st2_ref, cnt_ref, st3_ref, gain_ref, g_ref, uh_ref, ul_ref,
    m_ref, dvh_ref, dvl_ref, st3_out,
):
    step = pl.program_id(0)
    tile = dy_ref.shape[0]
    mask = row_mask(valid_ref, step, tile)
    count = count_of(cnt_ref)
    st2 = jnp.sum(st2_ref[...], axis=0)
    st3 = jnp.sum(st3_ref[...], axis=0)
    mean = st2[0:1, :] / count
    rstd = lax.rsqrt(st2[1:2, :] / count - mean * mean + EPS)
    a = LN2 * gain_ref[...] * rstd
    c1 = a * st3[0:1, :] / count
    c2 = a * st3[1:2, :] / count

    @pl.when(step == 0)
    def _():
        st3_out[...] = st3

    def dv(rows):
        zn = (v_ref[rows, :] - mean) * rstd
        dvs = split(jnp.where(mask[rows], a * dy_ref[rows, :] - (c1 + zn * c2), 0.0))
        dvh_ref[rows, :], dvl_ref[rows, :] = dvs
        return dvs

    parts = [slice(k, k + MIX_SUB) for k in range(0, tile, MIX_SUB)]
    mix_product([(rows, functools.partial(dv, rows)) for rows in parts], half_ref, g_ref, uh_ref, ul_ref, m_ref)


def mix_second_kernel(half_ref, dvh_ref, dvl_ref, g_ref, uh_ref, ul_ref, m_ref):
    mix_product([(slice(None), lambda: (dvh_ref[...], dvl_ref[...]))], half_ref, g_ref, uh_ref, ul_ref, m_ref)


def mix_back(half, valid, dy, v, st2, st, st3, gain, g, uh, ul, extra, tile):
    rows, hid = dy.shape
    part = uh.shape[1] // 2
    by = lambda n: pl.BlockSpec((tile, n), lambda i, half: (i, 0))
    return pl.pallas_call(
        mix_first_kernel,
        grid_spec=pltpu.PrefetchScalarGridSpec(
            num_scalar_prefetch=1,
            grid=(rows // tile,),
            in_specs=[whole(valid), by(hid), by(hid)]
            + [whole(t) for t in (st2, st, st3, gain, g)]
            + [pl.BlockSpec((tile, part), lambda i, half: (i, half[0]))] * 2,
            out_specs=[pl.BlockSpec((part + extra, hid), lambda i, half: (0, 0)), by(hid), by(hid)]
            + [pl.BlockSpec((2, hid), lambda i, half: (0, 0))],
        ),
        out_shape=[
            jax.ShapeDtypeStruct((part + extra, hid), F32),
            pltpu.HBM((rows, hid), BF16),
            pltpu.HBM((rows, hid), BF16),
            jax.ShapeDtypeStruct((2, hid), F32),
        ],
        compiler_params=params(28),
        name="mix_back",
        cost_estimate=cost(14),
    )(half, valid, far(dy), far(v), st2, st, st3, gain, g, far(uh), far(ul))


def mix_back_rest(half, dvh, dvl, g, uh, ul, extra, tile):
    rows, hid = dvh.shape
    part = uh.shape[1] // 2
    by = lambda n: pl.BlockSpec((tile, n), lambda i, half: (i, 0))
    return pl.pallas_call(
        mix_second_kernel,
        grid_spec=pltpu.PrefetchScalarGridSpec(
            num_scalar_prefetch=1,
            grid=(rows // tile,),
            in_specs=[by(hid), by(hid), whole(g)]
            + [pl.BlockSpec((tile, part), lambda i, half: (i, half[0]))] * 2,
            out_specs=pl.BlockSpec((part + extra, hid), lambda i, half: (0, 0)),
        ),
        out_shape=jax.ShapeDtypeStruct((part + extra, hid), F32),
        compiler_params=params(28),
        name="mix_back_rest",
        cost_estimate=cost(12),
    )(half, far(dvh), far(dvl), g, far(uh), far(ul))


def scale_kernel(wp_ref, coef_ref, ws_ref):
    n = wp_ref.shape[1] // 3
    for h in range(wp_ref.shape[0]):
        w = wp_ref[h, :n, :].astype(F32) + wp_ref[h, 2 * n :, :].astype(F32)
        ws_ref[h] = jnp.concatenate(split(w * coef_ref[h, 0:1, :]), axis=0)


def scale_weights(wp, coef):
    hops, n, hid = wp.shape
    return pl.pallas_call(
        scale_kernel,
        out_shape=pltpu.HBM((hops, n // 3 * 2, hid), BF16),
        compiler_params=params(16),
        name="scale_weights",
        cost_estimate=cost(3),
    )(wp, coef)


def hop_kernel(
    h, in_w, x_ref, wp_ref, ws_ref, coef_ref, dvh_ref, dvl_ref, mwh_ref, mwl_ref,
    dx_ref, bw_ref, sums_ref,
):
    step = pl.program_id(0)
    n = wp_ref.shape[1] // 3
    tile = x_ref.shape[1]

    @pl.when(step == 0)
    def _():
        bw_ref[...] = jnp.zeros_like(bw_ref)
        sums_ref[...] = jnp.zeros_like(sums_ref)

    a, b, s1, s2 = (coef_ref[0, k : k + 1, :] for k in range(4))
    xall = stack3(hop_rows(x_ref, h % (x_ref.shape[0] // in_w), in_w, 1.0))
    wp = wp_ref[0]
    whl = ws_ref[0]
    wh = whl[:n]
    dot = functools.partial(lax.dot_general, preferred_element_type=F32)
    row = lambda t: jnp.sum(t, axis=0, keepdims=True)
    sums = [0.0] * 2
    parts = [slice(k, k + SUB) for k in range(0, tile, SUB)]

    def products(rs):
        y = dot(xall[:, rs], wp, TN)
        return y, dot3((dvh_ref[rs, :], dvl_ref[rs, :]), (mwh_ref[...], mwl_ref[...]), NT)

    def middle(rs, z, du):
        y = z * a + b
        e = 1.0 + jnp.exp2(jnp.minimum(y, 30.0))
        j = jnp.maximum(s1 * y + (LOG2E * (1.0 - s1)) * jnp.log(e), y)
        dj = du * (1.0 - (1.0 - s2) / (1.0 + jnp.exp2(j)))
        dy = dj * (1.0 - (1.0 - s1) / e)
        for q, t in enumerate((dj * (y - j), du * j)):
            sums[q] = sums[q] + row(t)
        return split(dy)

    def results(rs, dys):
        dh, dl = dys
        xs = xall[: 2 * n, rs]
        both = dot(xs, dh, NN)
        bw_ref[...] += both[:n] + both[n:] + dot(xs[:n], dl, NN)
        both = dot(whl, dh, NT)
        dx_ref[:, rs] = both[:n] + both[n:] + dot(wh, dl, NT)

    now = products(parts[0])
    before = None
    for k, rs in enumerate(parts):
        ahead = products(parts[k + 1]) if k + 1 < len(parts) else None
        if before is not None:
            results(parts[k - 1], before)
        before = middle(rs, *now)
        now = ahead
    results(parts[-1], before)
    for q in range(2):
        sums_ref[q : q + 1, :] += sums[q]


def hop_back(h, in_w, x, wp, ws, coef, dvh, dvl, mwh, mwl, tile):
    width, rows = x.shape
    some = 2 * in_w if width % (2 * in_w) == 0 and in_w % 4 == 0 else width
    at = h * in_w // some
    hid = dvh.shape[1]
    n = wp.shape[1] // 3
    by = lambda w, k=0: pl.BlockSpec((tile, w), lambda i: (i, k))
    block = lambda r: pl.BlockSpec((r, hid), lambda i: (h, 0))
    return pl.pallas_call(
        functools.partial(hop_kernel, h, in_w),
        grid=(rows // tile,),
        in_specs=[
            pl.BlockSpec((some, tile), lambda i: (at, i)),
            pl.BlockSpec((1, 3 * n, hid), lambda i: (h, 0, 0)),
            pl.BlockSpec((1, 2 * n, hid), lambda i: (h, 0, 0)),
            pl.BlockSpec((1, 8, hid), lambda i: (h, 0, 0)),
        ]
        + [by(hid), by(hid), block(hid), block(hid)],
        out_specs=[
            pl.BlockSpec((n, tile), lambda i: (0, i)),
            pl.BlockSpec((n, hid), lambda i: (0, 0)),
            pl.BlockSpec((2, hid), lambda i: (0, 0)),
        ],
        out_shape=[
            pltpu.HBM((n, rows), F32),
            jax.ShapeDtypeStruct((n, hid), F32),
            jax.ShapeDtypeStruct((2, hid), F32),
        ],
        compiler_params=params(20),
        name=f"hop_back_{h}",
        cost_estimate=cost(11),
    )(far(x), far(wp), far(ws), coef, far(dvh), far(dvl), far(mwh), far(mwl))


def assemble_kernel(first_ref, own_ref, got_ref, own_g_ref, got_g_ref, w_ref, m_ref, uu_ref, g_ref):
    mine = (pl.program_id(0) // 2) == first_ref[0]
    m = jnp.where(mine, own_ref[...], got_ref[...])
    m_ref[...] = m
    ones = jnp.ones((8, m.shape[1]), BF16)
    dot = functools.partial(lax.dot_general, dimension_numbers=NT, preferred_element_type=F32)
    hi, lo = split(m * w_ref[...])
    uu_ref[0] = dot(ones, hi) + dot(ones, lo)

    @pl.when(pl.program_id(0) % 2 == 0)
    def _():
        g_ref[...] = jnp.where(mine, own_g_ref[...], got_g_ref[...])


def assemble(first, own, got, w):
    rows, hid = w.shape
    block = rows // 4
    extra = own.shape[0] - rows // 2
    half = pl.BlockSpec((block, hid), lambda i, first: (i % 2, 0))
    tail = pl.BlockSpec((extra, hid), lambda i, first: (rows // 2 // extra, 0))
    by = pl.BlockSpec((block, hid), lambda i, first: (i, 0))
    return pl.pallas_call(
        assemble_kernel,
        grid_spec=pltpu.PrefetchScalarGridSpec(
            num_scalar_prefetch=1,
            grid=(4,),
            in_specs=[half, half, tail, tail, by],
            out_specs=[
                by,
                pl.BlockSpec((1, 8, block), lambda i, first: (i, 0, 0)),
                pl.BlockSpec((extra, hid), lambda i, first: (i // 2, 0)),
            ],
        ),
        out_shape=[
            jax.ShapeDtypeStruct((rows, hid), F32),
            jax.ShapeDtypeStruct((4, 8, block), F32),
            jax.ShapeDtypeStruct((2 * extra, hid), F32),
        ],
        compiler_params=params(20),
        name="assemble",
        cost_estimate=cost(5),
    )(first, own, got, own, got, far(w))


def pack_kernel(misc_ref, *refs):
    hops = (len(refs) - 1) // 2
    n = refs[0].shape[0]
    out_ref = refs[-1]
    base = hops * n
    at = base + misc_ref.shape[0]
    for h in range(hops):
        out_ref[h * n : (h + 1) * n, :] = refs[h][...]
        out_ref[at + 2 * h : at + 2 * h + 2, :] = refs[hops + h][...]
    out_ref[base:at, :] = misc_ref[...]
    used = at + 2 * hops
    if used < out_ref.shape[0]:
        out_ref[used:, :] = jnp.zeros((out_ref.shape[0] - used, out_ref.shape[1]), F32)


def pack(misc, bws, sums, unit):
    used = len(bws) * (bws[0].shape[0] + 2) + misc.shape[0]
    return pl.pallas_call(
        pack_kernel,
        out_shape=jax.ShapeDtypeStruct((-(-used // unit) * unit, misc.shape[1]), F32),
        compiler_params=params(24),
        name="pack",
        cost_estimate=cost(3),
    )(misc, *bws, *sums)


def fix_kernel(in_w, classes, misc, valid_ref, x_ref, p_ref, uu_ref, g_ref, st_ref, gain_ref, slope_ref, mslope_ref, wp_ref, *refs):
    step = pl.program_id(0)
    hops, hid = gain_ref.shape
    tile = x_ref.shape[1]
    n = wp_ref.shape[1] // 3
    dxs, rest = refs[:hops], refs[hops:]
    dx_ref, bw_ref, gain_out, shift_out, slope_out, mslope_out, oslope_out, hw_out, hb_out, loss_out, q_ref = rest
    base = hops * n
    mask = row_mask(valid_ref, step, tile, 1)

    @pl.when(step == 0)
    def _():
        count = count_of(st_ref)
        hw_out[...] = p_ref[base : base + classes, :]
        hb_out[...] = p_ref[base + classes : base + classes + 1, :classes]
        loss_out[...] = p_ref[base + classes : base + classes + 1, LANES : LANES + 1] / count
        oslope_out[...] = p_ref[base + classes + 1 : base + classes + 2, :]
        for h in range(hops):
            cols = slice(h * hid, (h + 1) * hid)
            mean, rstd = norm_of(st_ref, cols)
            gain = gain_ref[h : h + 1, :]
            wh, wl = wp_ref[h, :n, :], wp_ref[h, 2 * n :, :]
            w = wh.astype(F32) + wl.astype(F32)
            raw = p_ref[h * n : (h + 1) * n, :]
            total = LOG2E * raw[in_w : in_w + 1, :]
            gsum = rstd * (LOG2E * jnp.sum(w * raw, axis=0, keepdims=True) - mean * total)
            gain_out[h : h + 1, :] = gsum
            shift_out[h : h + 1, :] = total
            at = base + misc + 2 * h
            slope_out[h : h + 1, :] = p_ref[at : at + 1, :] / (1.0 - slope_ref[h : h + 1, :])
            uu = uu_ref[h, 0:1, :]
            mslope_out[h : h + 1, :] = (p_ref[at + 1 : at + 2, :] - uu) / (1.0 - mslope_ref[h : h + 1, :])
            a = gain * rstd / count
            c2 = a * gsum * rstd
            k0 = a * total - mean * c2
            wc = w * c2
            mask_row = lax.broadcasted_iota(jnp.int32, (n, hid), 0) == in_w
            wc = split(jnp.where(mask_row, k0, wc))
            q_ref[h, :, :n] = dot3((wh, wl), wc, NT)
            k = h // (hops // 2) * (g_ref.shape[0] // 2) + h % (hops // 2) * n // 4
            g = jnp.concatenate(
                [g_ref[k : k + n // 4, q * LANES : q * LANES + n] for q in range(4)], axis=0
            )
            bw = raw * (LOG2E * gain * rstd) - dot3(split(g), wc)
            bw_ref[:, h, :] = bw[:in_w]

    for h in range(hops):
        x = jnp.where(mask, hop_rows(x_ref, h, in_w, 1.0), 0.0)
        fix = dot3(split(q_ref[h, :, :n]), split(x))
        dx_ref[h * in_w : (h + 1) * in_w, :] = (dxs[h][...] - fix)[:in_w]


def fix(valid, x, packed, uu, g, st, gain, slope, mslope, wp, dxs, in_w, classes, misc, tile):
    width, rows = x.shape
    hops, hid = gain.shape
    n = wp.shape[1] // 3
    cols = lambda r: pl.BlockSpec((r, tile), lambda i: (0, i))
    shapes = ((in_w, hops, hid),) + ((hops, hid),) * 4 + ((1, hid), (classes, hid), (1, classes), (1, 1))
    return pl.pallas_call(
        functools.partial(fix_kernel, in_w, classes, misc),
        grid=(rows // tile,),
        in_specs=[whole(valid), cols(width)]
        + [whole(t) for t in (packed, uu, g, st, gain, slope, mslope, wp)]
        + [cols(n)] * hops,
        out_specs=[cols(width)] + [pl.BlockSpec(s, lambda i, s=s: (0,) * len(s)) for s in shapes],
        out_shape=[jax.ShapeDtypeStruct(s, F32) for s in ((width, rows),) + shapes],
        scratch_shapes=[pltpu.VMEM((hops, n, LANES), F32)],
        compiler_params=params(24),
        name="fix",
        cost_estimate=cost(8),
    )(valid, far(x), packed, uu, g, st, gain, slope, mslope, far(wp), *[far(d) for d in dxs])


def flip(v, axis, size, k):
    return lax.ppermute(v, axis, [(i, i ^ k) for i in range(size)])


def exchange(copies):
    return lax.all_to_all(copies, ("dp", "bucket"), 0, 0, tiled=True)


def pieces(v, n):
    size = v.shape[0] // n
    return [v[i * size : (i + 1) * size] for i in range(n)]


def take(v, index, n):
    size = v.shape[0] // n
    return lax.dynamic_slice_in_dim(v, index * size, size, 0)


def merge(v, got, axis, size, k):
    bit = lax.axis_index(axis) // k % 2
    return jnp.where(bit == 0, jnp.concatenate([v, got], 0), jnp.concatenate([got, v], 0))


def halve(v, axis, size, k):
    bit = lax.axis_index(axis) // k % 2
    return v, flip(take(v, 1 - bit, 2), axis, size, k)


def kept(v, got, axis, size, k):
    return take(v, lax.axis_index(axis) // k % 2, 2) + got


def spread(v, axis, size, k):
    me = lax.axis_index(axis) // k
    return tuple(flip(take(v, me ^ i, 4), axis, size, k * i) if i else take(v, me, 4) for i in range(4))


def collect(v, axis, size, k):
    return (v,) + tuple(flip(v, axis, size, k * i) for i in range(1, 4))


def in_order(parts, axis, k):
    low, high = lax.axis_index(axis) // k % 2, lax.axis_index(axis) // (2 * k) % 2
    pair = lambda a, b: jnp.where(low == 0, jnp.concatenate([a, b], 0), jnp.concatenate([b, a], 0))
    near, far = pair(parts[0], parts[1]), pair(parts[2], parts[3])
    return jnp.where(high == 0, jnp.concatenate([near, far], 0), jnp.concatenate([far, near], 0))


def total(parts):
    if len(parts) == 4:
        return (parts[0] + parts[1]) + (parts[2] + parts[3])
    return functools.reduce(jnp.add, parts)


def sum_steps(parts, sizes, large, within):
    dp, bucket = sizes["dp"], sizes["bucket"]
    across = [("dp", dp, 1 << i) for i in range(1, dp.bit_length() - 1)]
    square = len(across) == 2 and not large
    line = [("bucket", bucket, 1 << i) for i in range(bucket.bit_length() - 1)]
    core = ("dp", dp, 1)
    within = within and dp > 1
    if within:
        parts = [kept(*(yield halve(total(parts), *core)), *core)]
    if square:
        parts = yield spread(total(parts), "dp", dp, 2)
    elif across:
        a, b = across[0], across[-1]
        bits = [lax.axis_index("dp") // s[2] % 2 for s in (a, b)]
        quarter = lambda i: functools.reduce(jnp.add, [take(p, i, 4) for p in parts])
        gone = flip(quarter(1 - bits[0]), *a), flip(quarter(3 - bits[1]), *b)
        parts, got = yield tuple(parts), gone
        top, bottom = quarter(bits[0]) + got[0], quarter(2 + bits[1]) + got[1]
        for a, b in list(zip(across, across[::-1]))[1:]:
            got = yield halve(top, *a), halve(bottom, *b)
            top, bottom = kept(*got[0], *a), kept(*got[1], *b)
        parts = [jnp.concatenate([top, bottom], 0)]
    if bucket == 4:
        parts = yield spread(total(parts), "bucket", bucket, 1)
        parts = yield collect(total(parts), "bucket", bucket, 1)
        v = in_order(parts, "bucket", 1)
    else:
        v = total(parts)
        for s in line:
            v = kept(*(yield halve(v, *s)), *s)
        for s in line[::-1]:
            parts = yield v, flip(v, *s)
            v = merge(*parts, *s)
    if square:
        v = in_order((yield collect(v, "dp", dp, 2)), "dp", 2)
    elif across:
        top, bottom = pieces(v, 2)
        for a, b in zip(across[::-1], across):
            got = yield top, flip(top, *a), bottom, flip(bottom, *b)
            top, bottom = merge(*got[:2], *a), merge(*got[2:], *b)
        v = jnp.concatenate([top, bottom], 0)
    if within:
        v = merge(*(yield v, flip(v, *core)), *core)
    return v


class Steps:
    def __init__(self, steps):
        self.steps, self.state, self.done, self.value = steps, None, False, None

    def step(self):
        if not self.done:
            try:
                self.state = self.steps.send(self.state)
            except StopIteration as end:
                self.done, self.value, self.state = True, end.value, None


def per_device(sizes, feats, labels, valid, branch_w, branch_gain, branch_shift, branch_slope, mix_slope,
               mix_w, mix_gain, mix_shift, out_slope, head_w, head_bias):
    rows, width = feats.shape
    hops, in_w, hid = branch_w.shape
    classes = head_w.shape[1]
    mix = hops * hid
    valid = valid.reshape(rows // LANES, LANES)
    labels = labels.reshape(rows // LANES, LANES)
    mslope = mix_slope.reshape(hops, hid)
    row = lambda t: t.reshape(1, -1)
    x = feats.T

    devices = sizes["dp"] * sizes["bucket"]
    g, sums, wp = gram(valid, x, branch_w.transpose(1, 0, 2), devices, TILES["gram"])
    sums = exchange(sums)
    z = project(x, wp, in_w, TILES["project"])
    uh, ul, v, st2, mwh, mwl, st, coef = forward(
        valid, z, wp, sums, branch_gain, branch_shift, branch_slope, mslope, mix_w, in_w, devices,
        TILES["forward"],
    )
    st2 = exchange(st2)
    st2, ws = lax.optimization_barrier((st2, scale_weights(wp, coef)))
    dy2, st3, misc = head(
        valid, labels, v, st2, st, row(mix_gain), row(mix_shift), row(out_slope), head_w.T, row(head_bias),
        TILES["head"],
    )
    st3 = exchange(st3)
    core = lax.axis_index("dp") % 2
    unit = max(devices, 64)
    extra = -(-(hops // 2 * g.shape[1] // 4) // unit) * unit
    half = lambda i: jnp.reshape(i, (1,)).astype(jnp.int32)
    away, dvh, dvl, st3 = mix_back(
        half(1 - core), valid, dy2, v, st2, st, st3, row(mix_gain), g, uh, ul, extra, TILES["mix"]
    )
    within = sizes["dp"] > 1
    got = flip(away, "dp", sizes["dp"], 1) if within else None
    m = mix_back_rest(half(core), dvh, dvl, g, uh, ul, extra, TILES["mix"])
    if within:
        m, got, x = lax.optimization_barrier((m, got, x))
        first = Steps(sum_steps((m, got), sizes, True, False))
    else:
        first = Steps(sum_steps((jnp.concatenate([m, away], 0),), sizes, True, False))
    dxs, bws, sums = [], [], []
    for h in range(hops):
        first.step()
        dx, bw, s = hop_back(
            h, in_w, x, wp, ws, coef, dvh, dvl, mwh, mwl, TILES["hop"],
        )
        dxs, bws, sums = dxs + [dx], bws + [bw], sums + [s]
        first.state, x, bws, sums = lax.optimization_barrier((first.state, x, bws, sums))
    packed = pack(misc, bws, sums, max(128, 2 * devices))
    last = Steps(sum_steps((packed,), sizes, False, True))
    first.step()
    last.step()
    last.step()
    first.state, last.state = lax.optimization_barrier((first.state, last.state))
    first.step()
    last.step()
    last.step()
    first.state, last.state = lax.optimization_barrier((first.state, last.state))
    while not first.done:
        first.step()
    m = first.value
    m, other = (m, flip(m, "dp", sizes["dp"], 1)) if within else pieces(m, 2)
    last.step()
    m, uu, g = assemble(half(core), m, other, mix_w)
    m, uu, last.state = lax.optimization_barrier((m, uu, last.state))
    while not last.done:
        last.step()
    packed = last.value
    d_x, bw, gain_grad, shift_grad, slope_grad, mslope_grad, oslope_grad, hw_grad, hb_grad, loss = fix(
        valid, x, packed, uu, g, st, branch_gain, branch_slope, mslope, wp, dxs, in_w, classes, misc.shape[0],
        TILES["fix"],
    )
    return (
        loss.reshape(()),
        d_x.T,
        bw.transpose(1, 0, 2),
        gain_grad,
        shift_grad,
        slope_grad,
        mslope_grad.reshape(mix),
        m,
        st3[1],
        st3[0],
        oslope_grad.reshape(hid),
        hw_grad.T,
        hb_grad.reshape(classes),
    )


def solution(mesh):
    sizes = {axis: mesh.shape[axis] for axis in ("dp", "bucket")}
    split_rows = P(("dp", "bucket"), None)
    in_specs = (split_rows, P(("dp", "bucket")), P(("dp", "bucket"))) + (P(),) * 11
    out_specs = (P(), split_rows) + (P(),) * 11
    return jax.shard_map(
        functools.partial(per_device, sizes),
        mesh=mesh,
        in_specs=in_specs,
        out_specs=out_specs,
        check_vma=False,
    )
```

```python
import functools

import jax
import jax.numpy as jnp
from jax import lax
from jax.experimental import pallas as pl
from jax.experimental.pallas import tpu as pltpu
from jax.sharding import PartitionSpec as P

EPS = 1e-05
F32 = jnp.float32
BF16 = jnp.bfloat16
LANES = 128
LOG2E = 1.4426950408889634
LN2 = 0.6931471805599453
TILES = {"gram": 2048, "project": 512, "forward": 512, "head": 1024, "mix": 512, "hop": 512, "fix": 1024}
PACK_STEPS = 2
SUB = 256
MIX_SUB = 512
NN = (((1,), (0,)), ((), ()))
NT = (((1,), (1,)), ((), ()))
TN = (((0,), (0,)), ((), ()))


def split(x):
    hi = x.astype(BF16)
    return hi, (x - hi.astype(F32)).astype(BF16)


def dot3(a, b, dims=NN):
    ah, al = a
    bh, bl = b
    dot = functools.partial(lax.dot_general, dimension_numbers=dims, preferred_element_type=F32)
    return dot(ah, bh) + (dot(ah, bl) + dot(al, bh))


def act2(y, slope, rest):
    return jnp.maximum(slope * y + rest * jnp.log(1.0 + jnp.exp2(jnp.minimum(y, 30.0))), y)


def cost(us):
    return pl.CostEstimate(flops=0, bytes_accessed=int(us * 3.69e6), transcendentals=0)


def params(mib):
    return pltpu.CompilerParams(vmem_limit_bytes=mib * 1024 * 1024)


def near(x):
    return pltpu.with_memory_space_constraint(x, pltpu.VMEM)


def far(x):
    return pltpu.with_memory_space_constraint(x, pltpu.HBM)


def whole(x, buffers=2):
    mode = {} if buffers == 2 else {"pipeline_mode": pl.Buffered(buffers)}
    return pl.BlockSpec(x.shape, lambda *_: (0,) * len(x.shape), **mode)


def row_mask(valid_ref, step, tile, axis=0):
    n = jnp.sum(valid_ref[...])
    shape = (tile, 1) if axis == 0 else (1, tile)
    return step * tile + lax.broadcasted_iota(jnp.int32, shape, axis) < n


def hop_rows(x_ref, h, in_w, extra=None):
    x = x_ref[h * in_w : (h + 1) * in_w, :]
    pad = -(-(in_w + 1) // 16) * 16 - in_w
    tail = jnp.zeros((pad, x.shape[1]), F32)
    if extra is not None:
        first = lax.broadcasted_iota(jnp.int32, tail.shape, 0) == 0
        tail = jnp.where(first, extra, 0.0)
    return jnp.concatenate([x, tail], axis=0)


def stack3(a):
    hi, lo = split(a)
    return jnp.concatenate([hi, lo, hi], axis=0)


def gram_kernel(in_w, valid_ref, x_ref, w_ref, g_ref, copies_ref, wp_ref):
    step = pl.program_id(0)
    tile = x_ref.shape[1]
    hops, hid = w_ref.shape[1:]
    copies = copies_ref.shape[0]
    mask = row_mask(valid_ref, step, tile, 1)

    @pl.when(step == 0)
    def _():
        g_ref[...] = jnp.zeros_like(g_ref)

    for h in range(hops):
        x = jnp.where(mask, hop_rows(x_ref, h, in_w, 1.0), 0.0)
        hi, lo = split(x)
        n = x.shape[0]
        dot = functools.partial(lax.dot_general, dimension_numbers=NT, preferred_element_type=F32)
        cross = dot(hi, lo)
        g_ref[h, :, :n] += dot(hi, hi) + (cross + cross.T)

    @pl.when(step == pl.num_programs(0) - 1)
    def _():
        for h in range(hops):
            n = g_ref.shape[1]
            w = w_ref[:, h, :]
            w = jnp.concatenate([w, jnp.zeros((n - in_w, hid), F32)], axis=0)
            ws = split(w)
            gw = dot3(split(g_ref[h, :, :n]), ws)
            squares = jnp.sum(w * gw, axis=0, keepdims=True)
            copies_ref[:, :, h * hid : (h + 1) * hid] = jnp.broadcast_to(squares[None], (copies, 1, hid))
            sums = g_ref[h, in_w : in_w + 1, :]
            at = hops * hid + h * LANES
            copies_ref[:, :, at : at + LANES] = jnp.broadcast_to(sums[None], (copies, 1, LANES))
            wp_ref[h] = jnp.concatenate([ws[0], ws[0], ws[1]], axis=0)


def gram(valid, x, w, copies, tile):
    width, rows = x.shape
    in_w, hops, hid = w.shape
    n = -(-(in_w + 1) // 16) * 16
    shapes = (hops, n, LANES), (copies, 1, hops * (hid + LANES)), (hops, 3 * n, hid)
    return pl.pallas_call(
        functools.partial(gram_kernel, in_w),
        grid=(rows // tile,),
        in_specs=[whole(valid), pl.BlockSpec((width, tile), lambda i: (0, i)), whole(w)],
        out_specs=[pl.BlockSpec(s, lambda i, s=s: (0,) * len(s)) for s in shapes],
        out_shape=[jax.ShapeDtypeStruct(s, F32) for s in shapes[:2]] + [pltpu.HBM(shapes[2], BF16)],
        compiler_params=params(32),
        name="gram",
        cost_estimate=cost(5),
    )(far(valid), far(x), far(w))


def project_kernel(in_w, x_ref, wp_ref, z_ref):
    hid = wp_ref.shape[2]
    for h in range(wp_ref.shape[0]):
        xs = stack3(hop_rows(x_ref, h, in_w))
        cols = slice(h * hid, (h + 1) * hid)
        z_ref[:, cols] = lax.dot_general(xs, wp_ref[h], TN, preferred_element_type=F32)


def project(x, wp, in_w, tile):
    width, rows = x.shape
    hops, _, hid = wp.shape
    return pl.pallas_call(
        functools.partial(project_kernel, in_w),
        grid=(rows // tile,),
        in_specs=[pl.BlockSpec((width, tile), lambda i: (0, i)), whole(wp, 1)],
        out_specs=pl.BlockSpec((tile, hops * hid), lambda i: (i, 0)),
        out_shape=pltpu.HBM((rows, hops * hid), F32),
        compiler_params=params(24),
        name="project",
        cost_estimate=cost(9),
    )(far(x), far(wp))


def count_of(st_ref):
    return st_ref[0:1, st_ref.shape[1] - 1 :]


def norm_of(st_ref, cols):
    count = count_of(st_ref)
    mean = st_ref[0:1, cols] / count
    var = st_ref[1:2, cols] / count - mean * mean
    return mean, lax.rsqrt(var + EPS)


def scale_of(st_ref, cols, gain_ref, shift_ref, h):
    mean, rstd = norm_of(st_ref, cols)
    a = gain_ref[h : h + 1, :] * rstd
    return LOG2E * a, LOG2E * (shift_ref[h : h + 1, :] - mean * a)


def forward_kernel(
    in_w, valid_ref, z_ref, wp_ref, all_ref, gain_ref, shift_ref, slope_ref, mslope_ref, w_ref,
    uh_ref, ul_ref, v_ref, copies_ref, wh_out, wl_out, st_ref, coef_ref,
    st2_ref, wh_ref, wl_ref,
):
    step = pl.program_id(0)
    tile = z_ref.shape[0]
    hops, hid = gain_ref.shape
    mask = row_mask(valid_ref, step, tile)

    @pl.when(step == 0)
    def _():
        st2_ref[...] = jnp.zeros_like(st2_ref)
        sums = jnp.sum(all_ref[...], axis=0)
        n = wp_ref.shape[1] // 3
        for h in range(hops):
            rows = slice(h * hid, (h + 1) * hid)
            wh_ref[rows, :], wl_ref[rows, :] = split(w_ref[rows, :])
            at = hops * hid + h * LANES
            xm = jnp.broadcast_to(sums[:, at : at + n], (8, n))
            st_ref[0:1, rows] = dot3(split(xm), (wp_ref[h, :n, :], wp_ref[h, 2 * n :, :]))[0:1, :]
            st_ref[1:2, rows] = sums[:, rows]
        at = hops * hid + in_w
        st_ref[:, hops * hid :] = jnp.broadcast_to(sums[:, at : at + 1], (2, LANES))
        for h in range(hops):
            a, b = scale_of(st_ref, slice(h * hid, (h + 1) * hid), gain_ref, shift_ref, h)
            coef_ref[h] = jnp.concatenate(
                [a, b, slope_ref[h : h + 1, :], mslope_ref[h : h + 1, :], jnp.zeros((4, hid), F32)], axis=0
            )

    def activate(h, z):
        cols = slice(h * hid, (h + 1) * hid)
        a, b = scale_of(st_ref, cols, gain_ref, shift_ref, h)
        s1 = slope_ref[h : h + 1, :]
        s2 = mslope_ref[h : h + 1, :]
        j = act2(z * a + b, s1, LOG2E * (1.0 - s1))
        u = act2(j, s2, LOG2E * (1.0 - s2))
        us = split(u)
        uh_ref[:, cols], ul_ref[:, cols] = us
        return us

    def mix(h, us):
        cols = slice(h * hid, (h + 1) * hid)
        part = dot3(us, (wh_ref[cols, :], wl_ref[cols, :]))
        v_ref[...] = part if h == 0 else v_ref[...] + part

    before = None
    for h in range(hops):
        if before is not None:
            mix(h - 1, before)
        before = activate(h, z_ref[:, h * hid : (h + 1) * hid])
    mix(hops - 1, before)
    piece = pl.ds(pl.multiple_of(step * wh_out.shape[0], wh_out.shape[0]), wh_out.shape[0])
    wh_out[...], wl_out[...] = wh_ref[piece, :], wl_ref[piece, :]
    v = v_ref[...]
    v = LN2 * v
    v_ref[...] = v
    vm = jnp.where(mask, v, 0.0)
    st2_ref[0:1, :] += jnp.sum(vm, axis=0, keepdims=True)
    st2_ref[1:2, :] += jnp.sum(vm * vm, axis=0, keepdims=True)

    @pl.when(step == pl.num_programs(0) - 1)
    def _():
        copies_ref[...] = jnp.broadcast_to(st2_ref[...][None], copies_ref.shape)


def forward(valid, z, wp, sums, gain, shift, slope, mslope, w, in_w, copies, tile):
    rows = z.shape[0]
    mix, hid = w.shape
    by = lambda n: pl.BlockSpec((tile, n), lambda i: (i, 0))
    return pl.pallas_call(
        functools.partial(forward_kernel, in_w),
        grid=(rows // tile,),
        in_specs=[whole(valid), by(mix)]
        + [whole(t, 1) for t in (wp, sums, gain, shift, slope, mslope, w)],
        out_specs=[by(mix)] * 2
        + [by(hid), pl.BlockSpec((copies, 2, hid), lambda i: (0, 0, 0))]
        + [pl.BlockSpec((mix * tile // rows, hid), lambda i: (i, 0))] * 2
        + [pl.BlockSpec((2, mix + LANES), lambda i: (0, 0))]
        + [pl.BlockSpec((mix // hid, 8, hid), lambda i: (0, 0, 0))],
        out_shape=[
            pltpu.HBM((rows, mix), BF16),
            pltpu.HBM((rows, mix), BF16),
            pltpu.HBM((rows, hid), F32),
            jax.ShapeDtypeStruct((copies, 2, hid), F32),
            pltpu.HBM((mix, hid), BF16),
            pltpu.HBM((mix, hid), BF16),
            jax.ShapeDtypeStruct((2, mix + LANES), F32),
            jax.ShapeDtypeStruct((mix // hid, 8, hid), F32),
        ],
        scratch_shapes=[
            pltpu.VMEM((2, hid), F32),
            pltpu.VMEM((mix, hid), BF16),
            pltpu.VMEM((mix, hid), BF16),
        ],
        compiler_params=params(48),
        name="forward",
        cost_estimate=cost(30),
    )(valid, far(z), far(wp), sums, gain, shift, slope, mslope, far(w))


def as_column(row):
    n = row.shape[1]
    same = lax.broadcasted_iota(jnp.int32, (n, n), 0) == lax.broadcasted_iota(jnp.int32, (n, n), 1)
    return jnp.sum(jnp.where(same, jnp.broadcast_to(row, (n, n)), 0.0), axis=1, keepdims=True)


def as_row(col):
    n = col.shape[0]
    same = lax.broadcasted_iota(jnp.int32, (n, n), 0) == lax.broadcasted_iota(jnp.int32, (n, n), 1)
    return jnp.sum(jnp.where(same, jnp.broadcast_to(col, (n, n)), 0.0), axis=0, keepdims=True)


def head_kernel(
    valid_ref, labels_ref, v_ref, st_ref, cnt_ref, gain_ref, shift_ref, slope_ref, hw_ref, hb_ref,
    dy_ref, copies_ref, misc_ref, st3_ref,
):
    step = pl.program_id(0)
    tile, hid = v_ref.shape
    classes = hw_ref.shape[0]
    padded = -(-classes // 16) * 16
    mask = row_mask(valid_ref, step, tile, 1)
    count = count_of(cnt_ref)

    @pl.when(step == 0)
    def _():
        st3_ref[...] = jnp.zeros_like(st3_ref)
        misc_ref[...] = jnp.zeros_like(misc_ref)

    sums = jnp.sum(st_ref[...], axis=0)
    mean = sums[0:1, :] / count
    rstd = lax.rsqrt(sums[1:2, :] / count - mean * mean + EPS)
    s = slope_ref[...]
    zn = (v_ref[...] - mean) * rstd
    y = gain_ref[...] * zn + shift_ref[...]
    e1 = 1.0 + jnp.exp(jnp.minimum(y, 20.0))
    sp = jnp.maximum(jnp.log(e1), y)
    w = s * y + (1.0 - s) * sp
    ws = split(w)
    hw = hw_ref[...]
    if padded > classes:
        hw = jnp.concatenate([hw, jnp.zeros((padded - classes, hid), F32)], axis=0)
    hh, hl = split(hw)
    dot = functools.partial(lax.dot_general, dimension_numbers=NT, preferred_element_type=F32)
    both = dot(jnp.concatenate([hh, hl], axis=0), ws[0])
    logits = both[:padded] + both[padded:] + dot(hh, ws[1])
    logits = logits[:classes] + as_column(hb_ref[...])
    peak = jnp.max(logits, axis=0, keepdims=True)
    ex = jnp.exp(logits - peak)
    tot = jnp.sum(ex, axis=0, keepdims=True)
    per = tile // LANES
    lab = jnp.concatenate([labels_ref[pl.ds(step * per + k, 1), :] for k in range(per)], axis=1)
    hit = lab == lax.broadcasted_iota(jnp.int32, (classes, tile), 0)
    picked = jnp.sum(jnp.where(hit, logits, 0.0), axis=0, keepdims=True)
    loss = jnp.sum(jnp.where(mask, peak + jnp.log(tot) - picked, 0.0))
    dl = jnp.where(mask, (ex / tot - hit.astype(F32)) / count, 0.0)
    bias = as_row(jnp.sum(dl, axis=1, keepdims=True))
    if padded > classes:
        dl = jnp.concatenate([dl, jnp.zeros((padded - classes, tile), F32)], axis=0)
    dh, dlo = split(dl)
    dot = functools.partial(lax.dot_general, dimension_numbers=NN, preferred_element_type=F32)
    both = dot(jnp.concatenate([dh, dlo], axis=0), ws[0])
    hwg = both[:padded] + both[padded:] + dot(dh, ws[1])
    misc_ref[0:classes, :] += hwg[:classes]
    misc_ref[classes : classes + 1, 0:classes] += bias
    misc_ref[classes : classes + 1, LANES : 2 * LANES] += jnp.broadcast_to(loss, (1, LANES))
    dw = lax.dot_general(
        jnp.concatenate([dh, dlo, dh], axis=0),
        jnp.concatenate([hh, hh, hl], axis=0),
        TN,
        preferred_element_type=F32,
    )
    dy = dw * (1.0 - (1.0 - s) / e1)
    dy_ref[...] = dy
    row = lambda t: jnp.sum(t, axis=0, keepdims=True)
    misc_ref[classes + 1 : classes + 2, :] += row(dw * (y - sp))
    st3_ref[0:1, :] += row(dy)
    st3_ref[1:2, :] += row(dy * zn)

    @pl.when(step == pl.num_programs(0) - 1)
    def _():
        copies_ref[...] = jnp.broadcast_to(st3_ref[...][None], copies_ref.shape)


def head(valid, labels, v, st2, st, gain, shift, slope, hw, hb, tile):
    rows, hid = v.shape
    by = lambda n: pl.BlockSpec((tile, n), lambda i: (i, 0))
    misc = -(-(hw.shape[0] + 2) // 8) * 8
    return pl.pallas_call(
        head_kernel,
        grid=(rows // tile,),
        in_specs=[whole(valid), whole(labels), by(hid)]
        + [whole(t) for t in (st2, st, gain, shift, slope, hw, hb)],
        out_specs=[
            by(hid),
            whole(st2),
            pl.BlockSpec((misc, hid), lambda i: (0, 0)),
        ],
        out_shape=[
            pltpu.HBM((rows, hid), F32),
            jax.ShapeDtypeStruct(st2.shape, F32),
            jax.ShapeDtypeStruct((misc, hid), F32),
        ],
        scratch_shapes=[pltpu.VMEM((2, hid), F32)],
        compiler_params=params(24),
        name="head",
        cost_estimate=cost(9),
    )(valid, labels, far(v), st2, st, gain, shift, slope, hw, hb)


def mix_product(parts, half_ref, g_ref, uh_ref, ul_ref, m_ref):
    mix = uh_ref.shape[1]
    some, n = g_ref.shape[0] // 2, g_ref.shape[1]

    @pl.when(pl.program_id(0) == 0)
    def _():
        m_ref[...] = jnp.zeros_like(m_ref)
        for h in range(some):
            g = g_ref[half_ref[0] * some + h]
            at = mix + h * n // 4
            m_ref[at : at + n // 4, :] = jnp.concatenate(
                [g[q * n // 4 : (q + 1) * n // 4] for q in range(4)], axis=1
            )

    ahead = parts[0][1]()
    for k, (rows, _) in enumerate(parts):
        dvs = ahead
        if k + 1 < len(parts):
            ahead = parts[k + 1][1]()
        hid = dvs[0].shape[1]
        for h in range(uh_ref.shape[1] // hid):
            cols = slice(h * hid, (h + 1) * hid)
            m_ref[cols, :] += dot3((uh_ref[rows, cols], ul_ref[rows, cols]), dvs, TN)


def mix_first_kernel(
    half_ref, valid_ref, dy_ref, v_ref, st2_ref, cnt_ref, st3_ref, gain_ref, g_ref, uh_ref, ul_ref,
    m_ref, dvh_ref, dvl_ref, st3_out,
):
    step = pl.program_id(0)
    tile = dy_ref.shape[0]
    mask = row_mask(valid_ref, step, tile)
    count = count_of(cnt_ref)
    st2 = jnp.sum(st2_ref[...], axis=0)
    st3 = jnp.sum(st3_ref[...], axis=0)
    mean = st2[0:1, :] / count
    rstd = lax.rsqrt(st2[1:2, :] / count - mean * mean + EPS)
    a = LN2 * gain_ref[...] * rstd
    c1 = a * st3[0:1, :] / count
    c2 = a * st3[1:2, :] / count

    @pl.when(step == 0)
    def _():
        st3_out[...] = st3

    def dv(rows):
        zn = (v_ref[rows, :] - mean) * rstd
        dvs = split(jnp.where(mask[rows], a * dy_ref[rows, :] - (c1 + zn * c2), 0.0))
        dvh_ref[rows, :], dvl_ref[rows, :] = dvs
        return dvs

    parts = [slice(k, k + MIX_SUB) for k in range(0, tile, MIX_SUB)]
    mix_product([(rows, functools.partial(dv, rows)) for rows in parts], half_ref, g_ref, uh_ref, ul_ref, m_ref)


def mix_second_kernel(half_ref, dvh_ref, dvl_ref, g_ref, uh_ref, ul_ref, m_ref):
    mix_product([(slice(None), lambda: (dvh_ref[...], dvl_ref[...]))], half_ref, g_ref, uh_ref, ul_ref, m_ref)


def mix_back(half, valid, dy, v, st2, st, st3, gain, g, uh, ul, extra, tile):
    rows, hid = dy.shape
    part = uh.shape[1] // 2
    by = lambda n: pl.BlockSpec((tile, n), lambda i, half: (i, 0))
    return pl.pallas_call(
        mix_first_kernel,
        grid_spec=pltpu.PrefetchScalarGridSpec(
            num_scalar_prefetch=1,
            grid=(rows // tile,),
            in_specs=[whole(valid), by(hid), by(hid)]
            + [whole(t) for t in (st2, st, st3, gain, g)]
            + [pl.BlockSpec((tile, part), lambda i, half: (i, half[0]))] * 2,
            out_specs=[pl.BlockSpec((part + extra, hid), lambda i, half: (0, 0)), by(hid), by(hid)]
            + [pl.BlockSpec((2, hid), lambda i, half: (0, 0))],
        ),
        out_shape=[
            jax.ShapeDtypeStruct((part + extra, hid), F32),
            pltpu.HBM((rows, hid), BF16),
            pltpu.HBM((rows, hid), BF16),
            jax.ShapeDtypeStruct((2, hid), F32),
        ],
        compiler_params=params(28),
        name="mix_back",
        cost_estimate=cost(14),
    )(half, valid, far(dy), far(v), st2, st, st3, gain, g, far(uh), far(ul))


def mix_back_rest(half, dvh, dvl, g, uh, ul, extra, tile):
    rows, hid = dvh.shape
    part = uh.shape[1] // 2
    by = lambda n: pl.BlockSpec((tile, n), lambda i, half: (i, 0))
    return pl.pallas_call(
        mix_second_kernel,
        grid_spec=pltpu.PrefetchScalarGridSpec(
            num_scalar_prefetch=1,
            grid=(rows // tile,),
            in_specs=[by(hid), by(hid), whole(g)]
            + [pl.BlockSpec((tile, part), lambda i, half: (i, half[0]))] * 2,
            out_specs=pl.BlockSpec((part + extra, hid), lambda i, half: (0, 0)),
        ),
        out_shape=jax.ShapeDtypeStruct((part + extra, hid), F32),
        compiler_params=params(28),
        name="mix_back_rest",
        cost_estimate=cost(12),
    )(half, far(dvh), far(dvl), g, far(uh), far(ul))


def hop_kernel(
    h, in_w, x_ref, wp_ref, coef_ref, dvh_ref, dvl_ref, mwh_ref, mwl_ref,
    dx_ref, bw_ref, sums_ref,
):
    step = pl.program_id(0)
    n = wp_ref.shape[1] // 3
    tile = x_ref.shape[1]

    @pl.when(step == 0)
    def _():
        bw_ref[...] = jnp.zeros_like(bw_ref)
        sums_ref[...] = jnp.zeros_like(sums_ref)

    a, b, s1, s2 = (coef_ref[0, k : k + 1, :] for k in range(4))
    xall = stack3(hop_rows(x_ref, h % (x_ref.shape[0] // in_w), in_w, 1.0))
    wp = wp_ref[0]
    wh, wl = split((wp[:n].astype(F32) + wp[2 * n :].astype(F32)) * a)
    whl = jnp.concatenate([wh, wl], axis=0)
    dot = functools.partial(lax.dot_general, preferred_element_type=F32)
    row = lambda t: jnp.sum(t, axis=0, keepdims=True)
    sums = [0.0] * 2
    parts = [slice(k, k + SUB) for k in range(0, tile, SUB)]

    def products(rs):
        y = dot(xall[:, rs], wp, TN)
        return y, dot3((dvh_ref[rs, :], dvl_ref[rs, :]), (mwh_ref[...], mwl_ref[...]), NT)

    def middle(rs, z, du):
        y = z * a + b
        e = 1.0 + jnp.exp2(jnp.minimum(y, 30.0))
        j = jnp.maximum(s1 * y + (LOG2E * (1.0 - s1)) * jnp.log(e), y)
        dj = du * (1.0 - (1.0 - s2) / (1.0 + jnp.exp2(j)))
        dy = dj * (1.0 - (1.0 - s1) / e)
        for q, t in enumerate((dj * (y - j), du * j)):
            sums[q] = sums[q] + row(t)
        return split(dy)

    def results(rs, dys):
        dh, dl = dys
        xs = xall[: 2 * n, rs]
        both = dot(xs, dh, NN)
        bw_ref[...] += both[:n] + both[n:] + dot(xs[:n], dl, NN)
        both = dot(whl, dh, NT)
        dx_ref[:, rs] = both[:n] + both[n:] + dot(wh, dl, NT)

    now = products(parts[0])
    before = None
    for k, rs in enumerate(parts):
        ahead = products(parts[k + 1]) if k + 1 < len(parts) else None
        if before is not None:
            results(parts[k - 1], before)
        before = middle(rs, *now)
        now = ahead
    results(parts[-1], before)
    for q in range(2):
        sums_ref[q : q + 1, :] += sums[q]


def hop_back(h, in_w, x, wp, coef, dvh, dvl, mwh, mwl, tile):
    width, rows = x.shape
    some = 2 * in_w if width % (2 * in_w) == 0 and in_w % 4 == 0 else width
    at = h * in_w // some
    hid = dvh.shape[1]
    n = wp.shape[1] // 3
    by = lambda w, k=0: pl.BlockSpec((tile, w), lambda i: (i, k))
    block = lambda r: pl.BlockSpec((r, hid), lambda i: (h, 0))
    return pl.pallas_call(
        functools.partial(hop_kernel, h, in_w),
        grid=(rows // tile,),
        in_specs=[
            pl.BlockSpec((some, tile), lambda i: (at, i)),
            pl.BlockSpec((1, 3 * n, hid), lambda i: (h, 0, 0)),
            pl.BlockSpec((1, 8, hid), lambda i: (h, 0, 0)),
        ]
        + [by(hid), by(hid), block(hid), block(hid)],
        out_specs=[
            pl.BlockSpec((n, tile), lambda i: (0, i)),
            pl.BlockSpec((n, hid), lambda i: (0, 0)),
            pl.BlockSpec((2, hid), lambda i: (0, 0)),
        ],
        out_shape=[
            pltpu.HBM((n, rows), F32),
            jax.ShapeDtypeStruct((n, hid), F32),
            jax.ShapeDtypeStruct((2, hid), F32),
        ],
        compiler_params=params(20),
        name=f"hop_back_{h}",
        cost_estimate=cost(11),
    )(far(x), far(wp), coef, far(dvh), far(dvl), far(mwh), far(mwl))


def assemble_kernel(first_ref, own_ref, got_ref, own_g_ref, got_g_ref, w_ref, m_ref, uu_ref, g_ref):
    mine = (pl.program_id(0) // 2) == first_ref[0]
    m = jnp.where(mine, own_ref[...], got_ref[...])
    m_ref[...] = m
    ones = jnp.ones((8, m.shape[1]), BF16)
    dot = functools.partial(lax.dot_general, dimension_numbers=NT, preferred_element_type=F32)
    hi, lo = split(m * w_ref[...])
    uu_ref[0] = dot(ones, hi) + dot(ones, lo)

    @pl.when(pl.program_id(0) % 2 == 0)
    def _():
        g_ref[...] = jnp.where(mine, own_g_ref[...], got_g_ref[...])


def assemble(first, own, got, w):
    rows, hid = w.shape
    block = rows // 4
    extra = own.shape[0] - rows // 2
    half = pl.BlockSpec((block, hid), lambda i, first: (i % 2, 0))
    tail = pl.BlockSpec((extra, hid), lambda i, first: (rows // 2 // extra, 0))
    by = pl.BlockSpec((block, hid), lambda i, first: (i, 0))
    return pl.pallas_call(
        assemble_kernel,
        grid_spec=pltpu.PrefetchScalarGridSpec(
            num_scalar_prefetch=1,
            grid=(4,),
            in_specs=[half, half, tail, tail, by],
            out_specs=[
                by,
                pl.BlockSpec((1, 8, block), lambda i, first: (i, 0, 0)),
                pl.BlockSpec((extra, hid), lambda i, first: (i // 2, 0)),
            ],
        ),
        out_shape=[
            jax.ShapeDtypeStruct((rows, hid), F32),
            jax.ShapeDtypeStruct((4, 8, block), F32),
            jax.ShapeDtypeStruct((2 * extra, hid), F32),
        ],
        compiler_params=params(20),
        name="assemble",
        cost_estimate=cost(5),
    )(first, own, got, own, got, far(w))


def pack_kernel(misc_ref, *refs):
    hops = (len(refs) - 1) // 2
    n = refs[0].shape[0]
    out_ref = refs[-1]
    base = hops * n
    at = base + misc_ref.shape[0]
    for h in range(hops):
        out_ref[h * n : (h + 1) * n, :] = refs[h][...]
        out_ref[at + 2 * h : at + 2 * h + 2, :] = refs[hops + h][...]
    out_ref[base:at, :] = misc_ref[...]
    used = at + 2 * hops
    if used < out_ref.shape[0]:
        out_ref[used:, :] = jnp.zeros((out_ref.shape[0] - used, out_ref.shape[1]), F32)


def pack(misc, bws, sums, unit):
    used = len(bws) * (bws[0].shape[0] + 2) + misc.shape[0]
    return pl.pallas_call(
        pack_kernel,
        out_shape=jax.ShapeDtypeStruct((-(-used // unit) * unit, misc.shape[1]), F32),
        compiler_params=params(24),
        name="pack",
        cost_estimate=cost(3),
    )(misc, *bws, *sums)


def fix_kernel(in_w, classes, misc, valid_ref, x_ref, p_ref, uu_ref, g_ref, st_ref, gain_ref, slope_ref, mslope_ref, wp_ref, *refs):
    step = pl.program_id(0)
    hops, hid = gain_ref.shape
    tile = x_ref.shape[1]
    n = wp_ref.shape[1] // 3
    dxs, rest = refs[:hops], refs[hops:]
    dx_ref, bw_ref, gain_out, shift_out, slope_out, mslope_out, oslope_out, hw_out, hb_out, loss_out, q_ref = rest
    base = hops * n
    mask = row_mask(valid_ref, step, tile, 1)

    @pl.when(step == 0)
    def _():
        count = count_of(st_ref)
        hw_out[...] = p_ref[base : base + classes, :]
        hb_out[...] = p_ref[base + classes : base + classes + 1, :classes]
        loss_out[...] = p_ref[base + classes : base + classes + 1, LANES : LANES + 1] / count
        oslope_out[...] = p_ref[base + classes + 1 : base + classes + 2, :]
        for h in range(hops):
            cols = slice(h * hid, (h + 1) * hid)
            mean, rstd = norm_of(st_ref, cols)
            gain = gain_ref[h : h + 1, :]
            wh, wl = wp_ref[h, :n, :], wp_ref[h, 2 * n :, :]
            w = wh.astype(F32) + wl.astype(F32)
            raw = p_ref[h * n : (h + 1) * n, :]
            total = LOG2E * raw[in_w : in_w + 1, :]
            gsum = rstd * (LOG2E * jnp.sum(w * raw, axis=0, keepdims=True) - mean * total)
            gain_out[h : h + 1, :] = gsum
            shift_out[h : h + 1, :] = total
            at = base + misc + 2 * h
            slope_out[h : h + 1, :] = p_ref[at : at + 1, :] / (1.0 - slope_ref[h : h + 1, :])
            uu = uu_ref[h, 0:1, :]
            mslope_out[h : h + 1, :] = (p_ref[at + 1 : at + 2, :] - uu) / (1.0 - mslope_ref[h : h + 1, :])
            a = gain * rstd / count
            c2 = a * gsum * rstd
            k0 = a * total - mean * c2
            wc = w * c2
            mask_row = lax.broadcasted_iota(jnp.int32, (n, hid), 0) == in_w
            wc = split(jnp.where(mask_row, k0, wc))
            q_ref[h, :, :n] = dot3((wh, wl), wc, NT)
            k = h // (hops // 2) * (g_ref.shape[0] // 2) + h % (hops // 2) * n // 4
            g = jnp.concatenate(
                [g_ref[k : k + n // 4, q * LANES : q * LANES + n] for q in range(4)], axis=0
            )
            bw = raw * (LOG2E * gain * rstd) - dot3(split(g), wc)
            bw_ref[:, h, :] = bw[:in_w]

    for h in range(hops):
        x = jnp.where(mask, hop_rows(x_ref, h, in_w, 1.0), 0.0)
        fix = dot3(split(q_ref[h, :, :n]), split(x))
        dx_ref[h * in_w : (h + 1) * in_w, :] = (dxs[h][...] - fix)[:in_w]


def fix(valid, x, packed, uu, g, st, gain, slope, mslope, wp, dxs, in_w, classes, misc, tile):
    width, rows = x.shape
    hops, hid = gain.shape
    n = wp.shape[1] // 3
    cols = lambda r: pl.BlockSpec((r, tile), lambda i: (0, i))
    shapes = ((in_w, hops, hid),) + ((hops, hid),) * 4 + ((1, hid), (classes, hid), (1, classes), (1, 1))
    return pl.pallas_call(
        functools.partial(fix_kernel, in_w, classes, misc),
        grid=(rows // tile,),
        in_specs=[whole(valid), cols(width)]
        + [whole(t) for t in (packed, uu, g, st, gain, slope, mslope, wp)]
        + [cols(n)] * hops,
        out_specs=[cols(width)] + [pl.BlockSpec(s, lambda i, s=s: (0,) * len(s)) for s in shapes],
        out_shape=[jax.ShapeDtypeStruct(s, F32) for s in ((width, rows),) + shapes],
        scratch_shapes=[pltpu.VMEM((hops, n, LANES), F32)],
        compiler_params=params(24),
        name="fix",
        cost_estimate=cost(8),
    )(valid, far(x), packed, uu, g, st, gain, slope, mslope, far(wp), *[far(d) for d in dxs])


def flip(v, axis, size, k):
    return lax.ppermute(v, axis, [(i, i ^ k) for i in range(size)])


def exchange(copies):
    return lax.all_to_all(copies, ("dp", "bucket"), 0, 0, tiled=True)


def pieces(v, n):
    size = v.shape[0] // n
    return [v[i * size : (i + 1) * size] for i in range(n)]


def take(v, index, n):
    size = v.shape[0] // n
    return lax.dynamic_slice_in_dim(v, index * size, size, 0)


def merge(v, got, axis, size, k):
    bit = lax.axis_index(axis) // k % 2
    return jnp.where(bit == 0, jnp.concatenate([v, got], 0), jnp.concatenate([got, v], 0))


def halve(v, axis, size, k):
    bit = lax.axis_index(axis) // k % 2
    return v, flip(take(v, 1 - bit, 2), axis, size, k)


def kept(v, got, axis, size, k):
    return take(v, lax.axis_index(axis) // k % 2, 2) + got


def spread(v, axis, size, k):
    me = lax.axis_index(axis) // k
    return tuple(flip(take(v, me ^ i, 4), axis, size, k * i) if i else take(v, me, 4) for i in range(4))


def collect(v, axis, size, k):
    return (v,) + tuple(flip(v, axis, size, k * i) for i in range(1, 4))


def in_order(parts, axis, k):
    low, high = lax.axis_index(axis) // k % 2, lax.axis_index(axis) // (2 * k) % 2
    pair = lambda a, b: jnp.where(low == 0, jnp.concatenate([a, b], 0), jnp.concatenate([b, a], 0))
    near, far = pair(parts[0], parts[1]), pair(parts[2], parts[3])
    return jnp.where(high == 0, jnp.concatenate([near, far], 0), jnp.concatenate([far, near], 0))


def total(parts):
    if len(parts) == 4:
        return (parts[0] + parts[1]) + (parts[2] + parts[3])
    return functools.reduce(jnp.add, parts)


def sum_steps(parts, sizes, large, within):
    dp, bucket = sizes["dp"], sizes["bucket"]
    across = [("dp", dp, 1 << i) for i in range(1, dp.bit_length() - 1)]
    square = len(across) == 2 and not large
    line = [("bucket", bucket, 1 << i) for i in range(bucket.bit_length() - 1)]
    core = ("dp", dp, 1)
    within = within and dp > 1
    if within:
        parts = [kept(*(yield halve(total(parts), *core)), *core)]
    if square:
        parts = yield spread(total(parts), "dp", dp, 2)
    elif across:
        a, b = across[0], across[-1]
        bits = [lax.axis_index("dp") // s[2] % 2 for s in (a, b)]
        quarter = lambda i: functools.reduce(jnp.add, [take(p, i, 4) for p in parts])
        gone = flip(quarter(1 - bits[0]), *a), flip(quarter(3 - bits[1]), *b)
        parts, got = yield tuple(parts), gone
        top, bottom = quarter(bits[0]) + got[0], quarter(2 + bits[1]) + got[1]
        for a, b in list(zip(across, across[::-1]))[1:]:
            got = yield halve(top, *a), halve(bottom, *b)
            top, bottom = kept(*got[0], *a), kept(*got[1], *b)
        parts = [jnp.concatenate([top, bottom], 0)]
    if bucket == 4:
        parts = yield spread(total(parts), "bucket", bucket, 1)
        parts = yield collect(total(parts), "bucket", bucket, 1)
        v = in_order(parts, "bucket", 1)
    else:
        v = total(parts)
        for s in line:
            v = kept(*(yield halve(v, *s)), *s)
        for s in line[::-1]:
            parts = yield v, flip(v, *s)
            v = merge(*parts, *s)
    if square:
        v = in_order((yield collect(v, "dp", dp, 2)), "dp", 2)
    elif across:
        top, bottom = pieces(v, 2)
        for a, b in zip(across[::-1], across):
            got = yield top, flip(top, *a), bottom, flip(bottom, *b)
            top, bottom = merge(*got[:2], *a), merge(*got[2:], *b)
        v = jnp.concatenate([top, bottom], 0)
    if within:
        v = merge(*(yield v, flip(v, *core)), *core)
    return v


class Steps:
    def __init__(self, steps):
        self.steps, self.state, self.done, self.value = steps, None, False, None

    def step(self):
        if not self.done:
            try:
                self.state = self.steps.send(self.state)
            except StopIteration as end:
                self.done, self.value, self.state = True, end.value, None


def per_device(sizes, feats, labels, valid, branch_w, branch_gain, branch_shift, branch_slope, mix_slope,
               mix_w, mix_gain, mix_shift, out_slope, head_w, head_bias):
    rows, width = feats.shape
    hops, in_w, hid = branch_w.shape
    classes = head_w.shape[1]
    mix = hops * hid
    valid = valid.reshape(rows // LANES, LANES)
    labels = labels.reshape(rows // LANES, LANES)
    mslope = mix_slope.reshape(hops, hid)
    row = lambda t: t.reshape(1, -1)
    x = feats.T

    devices = sizes["dp"] * sizes["bucket"]
    g, sums, wp = gram(valid, x, branch_w.transpose(1, 0, 2), devices, TILES["gram"])
    sums = exchange(sums)
    z = project(x, wp, in_w, TILES["project"])
    uh, ul, v, st2, mwh, mwl, st, coef = forward(
        valid, z, wp, sums, branch_gain, branch_shift, branch_slope, mslope, mix_w, in_w, devices,
        TILES["forward"],
    )
    st2 = exchange(st2)
    dy2, st3, misc = head(
        valid, labels, v, st2, st, row(mix_gain), row(mix_shift), row(out_slope), head_w.T, row(head_bias),
        TILES["head"],
    )
    st3 = exchange(st3)
    core = lax.axis_index("dp") % 2
    unit = max(devices, 64)
    extra = -(-(hops // 2 * g.shape[1] // 4) // unit) * unit
    half = lambda i: jnp.reshape(i, (1,)).astype(jnp.int32)
    away, dvh, dvl, st3 = mix_back(
        half(1 - core), valid, dy2, v, st2, st, st3, row(mix_gain), g, uh, ul, extra, TILES["mix"]
    )
    within = sizes["dp"] > 1
    got = flip(away, "dp", sizes["dp"], 1) if within else None
    m = mix_back_rest(half(core), dvh, dvl, g, uh, ul, extra, TILES["mix"])
    if within:
        m, got, x = lax.optimization_barrier((m, got, x))
        first = Steps(sum_steps((m, got), sizes, True, False))
    else:
        first = Steps(sum_steps((jnp.concatenate([m, away], 0),), sizes, True, False))
    dxs, bws, sums = [], [], []
    for h in range(hops):
        first.step()
        dx, bw, s = hop_back(
            h, in_w, x, wp, coef, dvh, dvl, mwh, mwl, TILES["hop"],
        )
        dxs, bws, sums = dxs + [dx], bws + [bw], sums + [s]
        first.state, x, bws, sums = lax.optimization_barrier((first.state, x, bws, sums))
    packed = pack(misc, bws, sums, max(128, 2 * devices))
    last = Steps(sum_steps((packed,), sizes, False, True))
    first.step()
    last.step()
    last.step()
    first.state, last.state = lax.optimization_barrier((first.state, last.state))
    first.step()
    last.step()
    last.step()
    first.state, last.state = lax.optimization_barrier((first.state, last.state))
    while not first.done:
        first.step()
    m = first.value
    m, other = (m, flip(m, "dp", sizes["dp"], 1)) if within else pieces(m, 2)
    last.step()
    m, uu, g = assemble(half(core), m, other, mix_w)
    m, uu, last.state = lax.optimization_barrier((m, uu, last.state))
    while not last.done:
        last.step()
    packed = last.value
    d_x, bw, gain_grad, shift_grad, slope_grad, mslope_grad, oslope_grad, hw_grad, hb_grad, loss = fix(
        valid, x, packed, uu, g, st, branch_gain, branch_slope, mslope, wp, dxs, in_w, classes, misc.shape[0],
        TILES["fix"],
    )
    return (
        loss.reshape(()),
        d_x.T,
        bw.transpose(1, 0, 2),
        gain_grad,
        shift_grad,
        slope_grad,
        mslope_grad.reshape(mix),
        m,
        st3[1],
        st3[0],
        oslope_grad.reshape(hid),
        hw_grad.T,
        hb_grad.reshape(classes),
    )


def solution(mesh):
    sizes = {axis: mesh.shape[axis] for axis in ("dp", "bucket")}
    split_rows = P(("dp", "bucket"), None)
    in_specs = (split_rows, P(("dp", "bucket")), P(("dp", "bucket"))) + (P(),) * 11
    out_specs = (P(), split_rows) + (P(),) * 11
    return jax.shard_map(
        functools.partial(per_device, sizes),
        mesh=mesh,
        in_specs=in_specs,
        out_specs=out_specs,
        check_vma=False,
    )
```
